32 devices in a mesh: ctx: 4 (over z), exp: 8 (over y, x, core).
Axes of the slice: x: 2, y: 2, z: 4, core: 2. Of those that a mesh axis runs over, the one named last changes fastest.
Arguments:
- queries: bfloat16 [256, 3072], P('ctx', 'exp'), may hold values from -8 to 8
- keys_values: bfloat16 [2, 256, 512], P(None, 'ctx', 'exp'), may hold values from -8 to 8
- residual: bfloat16 [256, 6144], P(('ctx', 'exp')), may hold values from -12 to 12
- out_weight: bfloat16 [3072, 6144], P('exp', 'ctx'), may hold values from -0.109375 to 0.109375
- norm_gain: float32 [6144], replicated, may hold values from 0.5 to 2
- routes: int32 [256, 4], P(('ctx', 'exp')), may hold values from 0 to 7, as said below
- route_weight: float32 [256, 4], P(('ctx', 'exp')), may hold values from 0.1 to 1
- gate_weight: bfloat16 [8, 6144, 5376], P('exp', None, 'ctx'), may hold values from -0.078125 to 0.078125
- up_weight: bfloat16 [8, 6144, 5376], P('exp', None, 'ctx'), may hold values from -0.078125 to 0.078125
- down_weight: bfloat16 [8, 5376, 6144], P('exp', 'ctx'), may hold values from -0.078125 to 0.078125
Outputs:
- layer_out: bfloat16 [256, 6144], P(('ctx', 'exp'))
The draws below stay inside these ranges and needn't reach their ends.
Inputs may be any that keep to these rules, and one draw needn't show every extreme that they name: `routes`: each row names 4 different experts. Within each aligned block of 8 rows (the rows of one device) no expert is named by more than 8 rows, and one expert is named by exactly 8 rows in every block.
All inputs are finite; a program needn't handle non-finite values.
Results may differ from the reference program's by a relative error of at most 0.025.
Values may be sent and summed in bfloat16 or wider, within the bound.
No kernel may reach another device: no remote copies, remote signals or barrier semaphores. Data moves between devices by JAX's collectives and lax.ppermute only.
A program may use at most 128 MiB of HBM per device.

```python
import math
import jax
import jax.numpy as jnp
from jax import lax

D = 6144
HD = 128
GROUP = 6
FF = 5376
TOP = 4
TOK_DEV = 8
SEQ = 256
KV_HEADS = 4
HEADS = 24
EXPERTS = 8
CAP = 8
N_CTX = 4
N_EXP = 8


def draw_queries(key, part):
    key = jax.random.fold_in(key, 7)
    base_draw = 1.5 * jax.random.truncated_normal(key, -4.0, 4.0, (SEQ, HEADS, HD), jnp.float32)
    return base_draw.reshape(SEQ, HEADS * HD).astype(jnp.bfloat16)


def draw_keys_values(key, part):
    key = jax.random.fold_in(key, 8)
    key_part, value_part = jax.random.split(key)
    keys = jax.random.truncated_normal(key_part, -4.0, 4.0, (SEQ, KV_HEADS, HD), jnp.float32)
    values = 2.0 * jax.random.truncated_normal(value_part, -4.0, 4.0, (SEQ, KV_HEADS, HD), jnp.float32)
    stacked = jnp.stack([keys.reshape(SEQ, KV_HEADS * HD), values.reshape(SEQ, KV_HEADS * HD)])
    return stacked.astype(jnp.bfloat16)


def draw_residual(key, part):
    key = jax.random.fold_in(key, 9)
    keys_list = jax.random.split(key, 3)
    column_scale = jnp.exp(jax.random.uniform(keys_list[0], (D,), jnp.float32, math.log(0.1), 0.0))
    row_scale = jnp.exp(jax.random.uniform(keys_list[1], (SEQ,), jnp.float32, math.log(0.3), math.log(3.0)))
    base_draw = jax.random.truncated_normal(keys_list[2], -4.0, 4.0, (SEQ, D), jnp.float32)
    return (base_draw * column_scale[None, :] * row_scale[:, None]).astype(jnp.bfloat16)


def draw_routes(key, part):
    key = jax.random.fold_in(key, 10)
    hot_key, block_key = jax.random.split(key)
    hot_expert = jax.random.randint(hot_key, (), 0, EXPERTS).astype(jnp.int32)
    block_keys = jax.random.split(block_key, SEQ // TOK_DEV)

    def one_block(single_key):
        key_rank, key_place, key_order, key_begin = jax.random.split(single_key, 4)
        rank = jax.random.permutation(key_rank, TOK_DEV).astype(jnp.int32)
        has_hot = (rank < CAP).astype(jnp.int32)
        hot_place = jax.random.randint(key_place, (TOK_DEV,), 0, TOP).astype(jnp.int32)
        others = jax.random.permutation(key_order, EXPERTS - 1).astype(jnp.int32)
        begin = jax.random.randint(key_begin, (), 0, EXPERTS - 1).astype(jnp.int32)
        per_row = TOP - has_hot
        before = jnp.cumsum(per_row) - per_row
        choice_index = jnp.arange(TOP, dtype=jnp.int32)[None, :]
        shifted = choice_index - has_hot[:, None] * (choice_index > hot_place[:, None]).astype(jnp.int32)
        counter = before[:, None] + shifted
        other_ids = (hot_expert + 1 + others[(begin + counter) % (EXPERTS - 1)]) % EXPERTS
        is_hot = (has_hot[:, None] == 1) & (choice_index == hot_place[:, None])
        return jnp.where(is_hot, hot_expert, other_ids).astype(jnp.int32)
    return jax.vmap(one_block)(block_keys).reshape(SEQ, TOP).astype(jnp.int32)


def shard_levels(stream_key, shape, cuts, smallest, high):
    loudness, own = 1.0, jax.random.fold_in(stream_key, 6)
    for position, shards_of in cuts:
        draws = jnp.exp(jax.random.uniform(jax.random.fold_in(own, position), (shards_of,), jnp.float32, smallest / len(cuts), high / len(cuts)))
        loudness = loudness * jnp.repeat(draws, shape[position] // shards_of).reshape([-1 if axis == position else 1 for axis in range(len(shape))])
    return loudness


def bell_draw(stream_key, dims, deviation, most, cuts=(), kind=jnp.bfloat16):
    result = jax.random.normal(stream_key, dims, jnp.float32) * deviation
    if len(cuts) > 0:
        result = shard_levels(stream_key, dims, cuts, -0.22, 0.18) * result
    return jnp.clip(result, min=-most, max=most).astype(kind)


def setup_inputs(seed: int = 0) -> dict:
    splits = jax.random.split(jax.random.key(seed), 11)
    return {
        "queries": draw_queries(jax.random.fold_in(splits[10], 71), 0),
        "keys_values": draw_keys_values(jax.random.fold_in(splits[10], 71), 0),
        "residual": draw_residual(jax.random.fold_in(splits[10], 71), 0),
        "out_weight": bell_draw(splits[3], (HEADS * HD, D), (HEADS * HD) ** -0.5, 0.109375, ((0, 8), (1, 4))),
        "norm_gain": jnp.clip(jnp.exp(jax.random.uniform(splits[4], (D,), jnp.float32, math.log(0.5), math.log(2.0))), 0.5, 2.0),
        "routes": draw_routes(jax.random.fold_in(splits[10], 71), 0),
        "route_weight": jnp.clip(0.1 + 0.9 * jax.random.uniform(splits[6], (SEQ, TOP), jnp.float32) ** shard_levels(splits[6], (SEQ, TOP), ((0, 32),), -0.2, 0.2), 0.1, 1.0),
        "gate_weight": bell_draw(splits[7], (EXPERTS, D, FF), D ** -0.5, 0.078125, ((0, 8), (2, 4))),
        "up_weight": bell_draw(splits[8], (EXPERTS, D, FF), D ** -0.5, 0.078125, ((0, 8), (2, 4))),
        "down_weight": bell_draw(splits[9], (EXPERTS, FF, D), FF ** -0.5, 0.078125, ((0, 8), (1, 4))),
    }


def attend_head(query_block, key_block, value_block, causal):
    scores = jnp.dot(query_block, key_block.T, preferred_element_type=jnp.float32) / math.sqrt(HD)
    masked = jnp.where(causal, scores, -jnp.inf)
    weights = jnp.exp(masked - lax.optimization_barrier(jnp.max(masked, axis=1, keepdims=True)))
    weights = weights / lax.optimization_barrier(jnp.sum(weights, axis=1, keepdims=True))
    return jnp.dot(weights, value_block.astype(jnp.float32), precision=lax.Precision.HIGHEST)

def reference(queries, keys_values, residual, out_weight, norm_gain, routes, route_weight, gate_weight, up_weight, down_weight):
    query_heads = queries.reshape(SEQ, HEADS, HD)
    key_heads = keys_values[0].reshape(SEQ, KV_HEADS, HD)
    value_heads = keys_values[1].reshape(SEQ, KV_HEADS, HD)
    positions = jnp.arange(SEQ, dtype=jnp.int32)
    causal = positions[:, None] >= positions[None, :]

    def one_head(head_index):
        group_index = head_index // GROUP
        return attend_head(query_heads[:, head_index], key_heads[:, group_index], value_heads[:, group_index], causal)
    heads_out = lax.map(one_head, jnp.arange(HEADS, dtype=jnp.int32))
    attended = jnp.transpose(heads_out, (1, 0, 2)).reshape(SEQ, HEADS * HD).astype(jnp.bfloat16)
    projected = jnp.dot(attended, out_weight, preferred_element_type=jnp.float32)
    hidden_state = residual.astype(jnp.float32) + projected
    row_mean = lax.optimization_barrier(jnp.mean(hidden_state, axis=1, keepdims=True))
    centered = hidden_state - row_mean
    variance = lax.optimization_barrier(jnp.mean(centered * centered, axis=1, keepdims=True))
    normed = (centered * lax.rsqrt(variance + 1e-05) * norm_gain).astype(jnp.bfloat16)
    limit = CAP * N_CTX * N_EXP
    pair_count = SEQ * TOP
    flat_routes = routes.reshape(-1)
    flat_weight = route_weight.reshape(-1)
    slice_width = FF // N_CTX

    def add_expert(combined, expert_index):
        pairs = jnp.nonzero(flat_routes == expert_index, size=limit, fill_value=pair_count)[0].astype(jnp.int32)
        token_index = pairs // TOP
        token_block = normed[jnp.minimum(token_index, SEQ - 1)]
        gate_part = jnp.dot(token_block, gate_weight[expert_index], preferred_element_type=jnp.float32)
        up_part = jnp.dot(token_block, up_weight[expert_index], preferred_element_type=jnp.float32)
        activated = (jax.nn.silu(gate_part) * up_part).astype(jnp.bfloat16)
        pieces = jnp.einsum('rcf,cfd->crd', activated.reshape(limit, N_CTX, slice_width).astype(jnp.float32), down_weight[expert_index].reshape(N_CTX, slice_width, D).astype(jnp.float32), precision=lax.Precision.HIGHEST)
        pieces = lax.optimization_barrier(pieces.astype(jnp.bfloat16)).astype(jnp.float32)
        expert_out = lax.optimization_barrier(jnp.sum(pieces, axis=0))
        gate_values = flat_weight[jnp.minimum(pairs, pair_count - 1)]
        combined = combined.at[token_index].add(gate_values[:, None] * expert_out, mode='drop')
        return (combined, None)
    combined, unused = lax.scan(add_expert, jnp.zeros((SEQ, D), jnp.float32), jnp.arange(EXPERTS, dtype=jnp.int32))
    return (hidden_state + combined).astype(jnp.bfloat16)
```

```python
import math

import jax
import jax.numpy as jnp
from jax import lax
from jax.sharding import PartitionSpec as P

HD = 128


def from_partner(value, axis, bit):
    return lax.ppermute(value, axis, [(i, i ^ 1 << bit) for i in range(lax.axis_size(axis))])


def on_device(
    queries,
    keys_values,
    residual,
    out_weight,
    norm_gain,
    routes,
    route_weight,
    gate_weight,
    up_weight,
    down_weight,
):
    C = lax.axis_size("ctx")
    E = lax.axis_size("exp")
    block_rows = queries.shape[0]
    heads = queries.shape[1] // HD
    seq = block_rows * C
    token_rows, features = residual.shape
    partner = from_partner(keys_values, "exp", 0)
    is_lower = lax.axis_index("exp") % 2 == 0
    joined = jnp.where(
        is_lower,
        jnp.concatenate([keys_values, partner], axis=2),
        jnp.concatenate([partner, keys_values], axis=2),
    )
    kv = lax.all_gather(joined, "ctx", axis=1, tiled=True)
    q = lax.all_gather(queries, "ctx", axis=0, tiled=True).reshape(seq, heads, HD)
    experts = jnp.arange(E, dtype=jnp.int32)
    own_weights = jnp.sum(
        jnp.where(routes[:, :, None] == experts, route_weight[:, :, None], 0.0), axis=1
    )
    all_weights = lax.all_gather(own_weights, ("ctx", "exp"), axis=0, tiled=True)
    scores = jnp.einsum("qhd,kd->hqk", q, kv[0], preferred_element_type=jnp.float32) / math.sqrt(HD)
    position = jnp.arange(seq, dtype=jnp.int32)
    scores = jnp.where(position[None, None, :] <= position[None, :, None], scores, -jnp.inf)
    top = jnp.max(scores, axis=2, keepdims=True)
    weights = jnp.exp(scores - top)
    total = jnp.sum(weights, axis=2, keepdims=True)
    summed = jnp.einsum(
        "hqk,kd->hqd",
        weights,
        kv[1].astype(jnp.float32),
        precision=lax.Precision.HIGHEST,
        preferred_element_type=jnp.float32,
    )
    attended = (summed / total).transpose(1, 0, 2).reshape(seq, heads * HD).astype(jnp.bfloat16)
    partial_value = jnp.dot(attended, out_weight, preferred_element_type=jnp.float32)
    blocks = partial_value.astype(jnp.bfloat16).reshape(C, E, token_rows, -1).transpose(1, 0, 2, 3)
    blocks = blocks.reshape(seq, -1)
    mine = lax.psum_scatter(blocks, "exp", scatter_dimension=0, tiled=True)
    mine = mine.reshape(C, token_rows, -1)
    projected = lax.all_to_all(mine, "ctx", split_axis=0, concat_axis=2, tiled=True)
    hidden_state = residual.astype(jnp.float32) + projected.reshape(token_rows, features).astype(
        jnp.float32
    )
    row_mean = jnp.mean(hidden_state, axis=1, keepdims=True)
    centered = hidden_state - row_mean
    variance = jnp.mean(centered * centered, axis=1, keepdims=True)
    normed = (centered * lax.rsqrt(variance + 1e-05) * norm_gain).astype(jnp.bfloat16)
    rows = lax.all_gather(normed, ("ctx", "exp"), axis=0, tiled=True)
    gate_part = jnp.dot(rows, gate_weight[0], preferred_element_type=jnp.float32)
    up_part = jnp.dot(rows, up_weight[0], preferred_element_type=jnp.float32)
    activated = (jax.nn.silu(gate_part) * up_part).astype(jnp.bfloat16)
    piece = jnp.dot(activated, down_weight[0], preferred_element_type=jnp.float32)
    mine_only = (lax.axis_index("exp") == experts).astype(jnp.float32)
    scale = jnp.sum(all_weights * mine_only, axis=1, keepdims=True)
    weighted = (piece * scale).astype(jnp.bfloat16)
    combined = lax.psum_scatter(weighted, ("ctx", "exp"), scatter_dimension=0, tiled=True)
    return (hidden_state + combined.astype(jnp.float32)).astype(jnp.bfloat16)


def solution(mesh):
    in_specs = (
        P("ctx", "exp"),
        P(None, "ctx", "exp"),
        P(("ctx", "exp"), None),
        P("exp", "ctx"),
        P(),
        P(("ctx", "exp"), None),
        P(("ctx", "exp"), None),
        P("exp", None, "ctx"),
        P("exp", None, "ctx"),
        P("exp", "ctx", None),
    )
    out_specs = P(("ctx", "exp"), None)
    return jax.shard_map(
        on_device, mesh=mesh, in_specs=in_specs, out_specs=out_specs, check_vma=False
    )
```

```python
import functools
import math

import jax
import jax.numpy as jnp
from jax import lax
from jax.experimental import pallas as pl
from jax.experimental.pallas import tpu as pltpu
from jax.sharding import PartitionSpec as P

HD = 128
EXTRA = 128
SPLIT = 3
VMEM_LIMIT = 56 * 1024 * 1024
F32 = jnp.float32
BF16 = jnp.bfloat16
WHOLE = pl.BlockSpec(memory_space=pltpu.VMEM)
SCALARS = pl.BlockSpec(memory_space=pltpu.SMEM)


def swap(value, axis, mask):
    return lax.ppermute(value, axis, [(i, i ^ mask) for i in range(lax.axis_size(axis))])


def call(kernel, out_shape, operands, in_specs, scratch=()):
    return pl.pallas_call(
        kernel,
        out_shape=out_shape,
        in_specs=in_specs,
        out_specs=jax.tree.map(lambda _: WHOLE, out_shape),
        scratch_shapes=list(scratch),
        compiler_params=pltpu.CompilerParams(vmem_limit_bytes=VMEM_LIMIT),
    )(*operands)


def shape(dims, dtype):
    return jax.ShapeDtypeStruct(tuple(dims), dtype)


def attend_kernel(C, E, heads, place, *refs):
    blocks, out_weight, mate_out, own_out, projected = refs[:C], *refs[C:]
    ctx, exp = place[0], place[1]
    rows = blocks[0].shape[0]
    seq = rows * C
    width = heads * HD
    half = HD // 2
    lower = (exp & 1) == 0

    def joined(start):
        own = jnp.concatenate([b[:, start : start + half] for b in blocks], axis=0)
        first = start + 2 * half
        mate = jnp.concatenate([b[:, first : first + half] for b in blocks], axis=0)
        both = jnp.concatenate([own, mate], axis=1)
        other = jnp.concatenate([mate, own], axis=1)
        return jnp.where(lower, both, other)

    keys = joined(width)
    values = joined(width + half)
    shift = rows.bit_length() - 1
    column = lax.broadcasted_iota(jnp.int32, (rows, seq), 1)
    key_position = ((column >> shift) ^ ctx) * rows + (column & (rows - 1))
    row = lax.broadcasted_iota(jnp.int32, (rows, seq), 0)
    parts = []
    for k in range(C):
        allowed = key_position <= (ctx ^ k) * rows + row
        block_parts = []
        for h in range(heads):
            q = blocks[k][:, h * HD : (h + 1) * HD]
            scores = lax.dot_general(
                q, keys, (((1,), (1,)), ((), ())), preferred_element_type=F32
            ) * (1.0 / math.sqrt(HD))
            scores = jnp.where(allowed, scores, -jnp.inf)
            top = jnp.max(scores, axis=1, keepdims=True)
            weights = jnp.exp(scores - top)
            total = jnp.sum(weights, axis=1, keepdims=True)
            high = weights.astype(BF16)
            low = (weights - high.astype(F32)).astype(BF16)
            summed = jnp.dot(high, values, preferred_element_type=F32) + jnp.dot(
                low, values, preferred_element_type=F32
            )
            block_parts.append((summed / total).astype(BF16))
        parts.append(jnp.concatenate(block_parts, axis=1))
    attended = jnp.concatenate(parts, axis=0)
    projected[...] = jnp.dot(attended, out_weight[...], preferred_element_type=F32)
    token_rows = mate_out.shape[2]
    for p in range(E):
        for k in range(C):
            start = pl.multiple_of((k * E + (exp ^ p)) * token_rows, token_rows)
            piece = projected[pl.ds(start, token_rows), :]
            if p & 1:
                mate_out[p >> 1, k] = piece.astype(BF16)
            else:
                own_out[p >> 1, k] = piece


def mate_sum_kernel(own, received, kept, *sent):
    kept[...] = own[0] + received[0].astype(F32)
    for p, out in enumerate(sent):
        out[...] = (own[p + 1] + received[p + 1].astype(F32)).astype(BF16)


def plane_sum_kernel(count, *refs):
    own, received, kept, sent = refs[0], refs[1 : 1 + count], refs[1 + count], refs[2 + count :]
    total = own[...]
    for piece in received:
        total = total + piece[...].astype(F32)
    kept[...] = total[0]
    for k, out in enumerate(sent):
        out[...] = total[k + 1].astype(BF16)


def norm_kernel(C, place, *refs):
    pieces, residual, gain, extra, hidden, rows_out = refs[:C], *refs[C:]
    ctx = place[0]
    cols = pieces[0].shape[1]
    features = residual.shape[1]
    for k in range(C):
        at = pl.ds(pl.multiple_of((ctx ^ k) * cols, 128), cols)
        hidden[:, at] = residual[:, at].astype(F32) + pieces[k][...].astype(F32)
    value = hidden[...]
    mean = jnp.sum(value, axis=1, keepdims=True) * (1.0 / features)
    centered = value - mean
    variance = jnp.sum(centered * centered, axis=1, keepdims=True) * (1.0 / features)
    normed = centered * lax.rsqrt(variance + 1e-05) * gain[...]
    rows_out[:, :features] = normed.astype(BF16)
    rows_out[:, features:] = extra[...]


def expert_kernel(E, groups, up_steps, place, *refs):
    packed = refs[: 2 * groups]
    gate, up, down = refs[2 * groups : 2 * groups + 3]
    outs = refs[2 * groups + 3 : 4 * groups + 3]
    rows, gate_sum, up_sum, activated, scale = refs[4 * groups + 3 :]
    step = pl.program_id(0)
    token_rows = packed[0].shape[1]
    features = rows.shape[1]
    depth = gate.shape[1]
    group_rows = packed[0].shape[0] * token_rows

    @pl.when(step == 0)
    def _():
        lane = lax.broadcasted_iota(jnp.int32, (group_rows, EXTRA), 1)
        wanted = ((lane & (E - 1)) == place[1]) & (lane < SPLIT * E)
        for g in range(2 * groups):
            at = slice(g * group_rows, (g + 1) * group_rows)
            value = packed[g][:, :, :features].astype(F32)
            rows[at, :] = value.reshape(group_rows, features).astype(BF16)
            tail = packed[g][:, :, features:].astype(F32).reshape(group_rows, EXTRA)
            scale[at, :] = jnp.sum(jnp.where(wanted, tail, 0.0), axis=1, keepdims=True)

    @pl.when(step < up_steps)
    def _():
        at = pl.ds(pl.multiple_of(step * depth, depth), depth)
        block = rows[:, at]
        gate_part = jnp.dot(block, gate[0], preferred_element_type=F32)
        up_part = jnp.dot(block, up[0], preferred_element_type=F32)

        @pl.when(step == 0)
        def _():
            gate_sum[...] = gate_part
            up_sum[...] = up_part

        @pl.when(step > 0)
        def _():
            gate_sum[...] += gate_part
            up_sum[...] += up_part

    @pl.when(step == up_steps)
    def _():
        value = gate_sum[...]
        activated[...] = (value / (1.0 + jnp.exp(-value)) * up_sum[...]).astype(BF16)

    @pl.when(step >= up_steps)
    def _():
        piece = jnp.dot(activated[...], down[0], preferred_element_type=F32) * scale[...]
        for g in range(2 * groups):
            part = piece[g * group_rows : (g + 1) * group_rows]
            outs[g][...] = part.reshape(-1, token_rows, part.shape[1]).astype(BF16)


def run_experts(place, packed, gate_weight, up_weight, down_weight, E):
    count = len(packed)
    pieces, token_rows, wide = packed[0].shape
    features = wide - EXTRA
    units = gate_weight.shape[2]
    total = count * pieces * token_rows
    depth = 512
    columns = 512
    up_steps = features // depth
    down_steps = features // columns
    last = up_steps - 1

    def column_block(i):
        return jnp.maximum(i - up_steps, 0)

    once = pl.Buffered(1)
    return pl.pallas_call(
        functools.partial(expert_kernel, E, count // 2, up_steps),
        out_shape=[shape((pieces, token_rows, features), BF16) for _ in packed],
        grid=(up_steps + down_steps,),
        in_specs=[SCALARS]
        + [
            pl.BlockSpec((pieces, token_rows, wide), lambda i: (0, 0, 0), pipeline_mode=once)
            for _ in packed
        ]
        + [
            pl.BlockSpec((1, depth, units), lambda i: (0, jnp.minimum(i, last), 0)),
            pl.BlockSpec((1, depth, units), lambda i: (0, jnp.minimum(i, last), 0)),
            pl.BlockSpec((1, units, columns), lambda i: (0, 0, column_block(i))),
        ],
        out_specs=[
            pl.BlockSpec((pieces, token_rows, columns), lambda i: (0, 0, column_block(i)))
            for _ in packed
        ],
        scratch_shapes=[
            pltpu.VMEM((total, features), BF16),
            pltpu.VMEM((total, units), F32),
            pltpu.VMEM((total, units), F32),
            pltpu.VMEM((total, units), BF16),
            pltpu.VMEM((total, 1), F32),
        ],
        compiler_params=pltpu.CompilerParams(
            vmem_limit_bytes=VMEM_LIMIT, dimension_semantics=("arbitrary",)
        ),
        cost_estimate=pl.CostEstimate(
            flops=6 * total * features * units,
            bytes_accessed=6 * features * units + 4 * total * features,
            transcendentals=total * units,
        ),
    )(place, *packed, gate_weight, up_weight, down_weight)


def group_sum_kernel(own, received, *outs):
    for i, out in enumerate(outs):
        out[...] = (own[i].astype(F32) + received[i].astype(F32)).astype(BF16)


def add(a, b):
    return (a.astype(F32) + b.astype(F32)).astype(BF16)


def on_device(
    queries,
    keys_values,
    residual,
    out_weight,
    norm_gain,
    routes,
    route_weight,
    gate_weight,
    up_weight,
    down_weight,
):
    C = lax.axis_size("ctx")
    E = lax.axis_size("exp")
    chips = E // 2
    chip_bits = list(range(1, E.bit_length() - 1))
    heads = queries.shape[1] // HD
    seq = queries.shape[0] * C
    token_rows, features = residual.shape
    cols = out_weight.shape[1]
    place = jnp.stack([lax.axis_index("ctx"), lax.axis_index("exp")]).astype(jnp.int32)

    own_kv = jnp.concatenate([keys_values[0], keys_values[1]], axis=1)
    bundle = jnp.concatenate([queries, own_kv, swap(own_kv, "exp", 1)], axis=1)
    blocks = [bundle] + [swap(bundle, "ctx", k) for k in range(1, C)]

    experts = jnp.arange(E, dtype=jnp.int32)
    left = jnp.sum(jnp.where(routes[:, :, None] == experts, route_weight[:, :, None], 0.0), axis=1)
    terms = []
    for _ in range(SPLIT):
        term = lax.reduce_precision(left, 8, 7)
        terms.append(term.astype(BF16))
        left = left - term
    extra = jnp.pad(jnp.concatenate(terms, axis=1), ((0, 0), (0, EXTRA - SPLIT * E)))

    mate_part, own_part = call(
        functools.partial(attend_kernel, C, E, heads),
        [
            shape((chips, C, token_rows, cols), BF16),
            shape((chips, C, token_rows, cols), F32),
        ],
        [place, *blocks, out_weight],
        [SCALARS] + [WHOLE] * (C + 1),
        [pltpu.VMEM((seq, cols), F32)],
    )

    kept, *sent = call(
        mate_sum_kernel,
        [shape((C, token_rows, cols), F32)] + [shape((C, token_rows, cols), BF16)] * (chips - 1),
        [own_part, swap(mate_part, "exp", 1)],
        [WHOLE, WHOLE],
    )
    received = [swap(piece, "exp", (p + 1) << 1) for p, piece in enumerate(sent)]
    kept, *sent = call(
        functools.partial(plane_sum_kernel, chips - 1),
        [shape((token_rows, cols), F32)] + [shape((token_rows, cols), BF16)] * (C - 1),
        [kept, *received],
        [WHOLE] * chips,
    )
    pieces = [kept] + [swap(piece, "ctx", k + 1) for k, piece in enumerate(sent)]
    hidden, rows = call(
        functools.partial(norm_kernel, C),
        [shape((token_rows, features), F32), shape((token_rows, features + EXTRA), BF16)],
        [place, *pieces, residual, norm_gain.reshape(1, -1), extra],
        [SCALARS] + [WHOLE] * (C + 3),
    )

    shards = [rows] + [swap(rows, "ctx", k) for k in range(1, C)]
    packed = []
    for g in range(C // 2):
        group = []
        for s in range(2):
            held = {0: shards[2 * g + s]}
            for bit in chip_bits if s else chip_bits[::-1]:
                for p in sorted(held):
                    held[p | 1 << (bit - 1)] = swap(held[p], "exp", 1 << bit)
            group += [held[p] for p in range(chips)]
        packed.append(jnp.stack(group))
    packed += [swap(group, "exp", 1) for group in packed]

    outs = run_experts(place, packed, gate_weight, up_weight, down_weight, E)

    count = C // 2
    shards = [None] * C
    for g in reversed(range(count)):
        received = swap(outs[count + g], "exp", 1)
        group = call(
            group_sum_kernel,
            [shape((token_rows, features), BF16)] * E,
            [outs[g], received],
            [WHOLE, WHOLE],
        )
        for s in range(2):
            held = dict(enumerate(group[s * chips : (s + 1) * chips]))
            for bit in chip_bits[::-1] if s else chip_bits:
                far = 1 << (bit - 1)
                for p in sorted(held):
                    if p & far:
                        held[p ^ far] = add(held[p ^ far], swap(held.pop(p), "exp", 1 << bit))
            shards[2 * g + s] = held[0]
    total = hidden
    for k, shard in enumerate(shards):
        total = total + (swap(shard, "ctx", k) if k else shard).astype(F32)
    return total.astype(BF16)


def solution(mesh):
    in_specs = (
        P("ctx", "exp"),
        P(None, "ctx", "exp"),
        P(("ctx", "exp"), None),
        P("exp", "ctx"),
        P(),
        P(("ctx", "exp"), None),
        P(("ctx", "exp"), None),
        P("exp", None, "ctx"),
        P("exp", None, "ctx"),
        P("exp", "ctx", None),
    )
    out_specs = P(("ctx", "exp"), None)
    return jax.shard_map(
        on_device, mesh=mesh, in_specs=in_specs, out_specs=out_specs, check_vma=False
    )
```

```python
import functools
import math

import jax
import jax.numpy as jnp
from jax import lax
from jax.experimental import pallas as pl
from jax.experimental.pallas import tpu as pltpu
from jax.sharding import PartitionSpec as P

HD = 128
EXTRA = 128
SPLIT = 3
MIB = 1024 * 1024
F32 = jnp.float32
BF16 = jnp.bfloat16
WHOLE = pl.BlockSpec(memory_space=pltpu.VMEM)
SCALARS = pl.BlockSpec(memory_space=pltpu.SMEM)


def swap(value, axis, mask):
    return lax.ppermute(value, axis, [(i, i ^ mask) for i in range(lax.axis_size(axis))])


def call(kernel, out_shape, operands, in_specs, scratch=(), limit=16):
    return pl.pallas_call(
        kernel,
        out_shape=out_shape,
        in_specs=in_specs,
        out_specs=jax.tree.map(lambda _: WHOLE, out_shape),
        scratch_shapes=list(scratch),
        compiler_params=pltpu.CompilerParams(vmem_limit_bytes=limit * MIB),
    )(*operands)


def shape(dims, dtype):
    return jax.ShapeDtypeStruct(tuple(dims), dtype)


def attend_kernel(C, E, heads, place, *refs):
    blocks, out_weight, mate_out, own_out, projected = refs[:C], *refs[C:]
    ctx, exp = place[0], place[1]
    rows = blocks[0].shape[0]
    seq = rows * C
    width = heads * HD
    half = HD // 2
    lower = (exp & 1) == 0

    def joined(start):
        own = jnp.concatenate([b[:, start : start + half] for b in blocks], axis=0)
        first = start + 2 * half
        mate = jnp.concatenate([b[:, first : first + half] for b in blocks], axis=0)
        both = jnp.concatenate([own, mate], axis=1)
        other = jnp.concatenate([mate, own], axis=1)
        return jnp.where(lower, both, other)

    keys = joined(width)
    values = joined(width + half)
    shift = rows.bit_length() - 1
    column = lax.broadcasted_iota(jnp.int32, (rows, seq), 1)
    key_position = ((column >> shift) ^ ctx) * rows + (column & (rows - 1))
    row = lax.broadcasted_iota(jnp.int32, (rows, seq), 0)
    parts = []
    for k in range(C):
        allowed = key_position <= (ctx ^ k) * rows + row
        block_parts = []
        for h in range(heads):
            q = blocks[k][:, h * HD : (h + 1) * HD]
            scores = lax.dot_general(
                q, keys, (((1,), (1,)), ((), ())), preferred_element_type=F32
            ) * (1.0 / math.sqrt(HD))
            scores = jnp.where(allowed, scores, -jnp.inf)
            top = jnp.max(scores, axis=1, keepdims=True)
            weights = jnp.exp(scores - top)
            total = jnp.sum(weights, axis=1, keepdims=True)
            high = weights.astype(BF16)
            low = (weights - high.astype(F32)).astype(BF16)
            summed = jnp.dot(high, values, preferred_element_type=F32) + jnp.dot(
                low, values, preferred_element_type=F32
            )
            block_parts.append((summed / total).astype(BF16))
        parts.append(jnp.concatenate(block_parts, axis=1))
    attended = jnp.concatenate(parts, axis=0)
    projected[...] = jnp.dot(attended, out_weight[...], preferred_element_type=F32)
    token_rows = mate_out.shape[2]
    for p in range(E):
        for k in range(C):
            start = pl.multiple_of((k * E + (exp ^ p)) * token_rows, token_rows)
            piece = projected[pl.ds(start, token_rows), :]
            if p & 1:
                mate_out[p >> 1, k] = piece.astype(BF16)
            else:
                own_out[p >> 1, k] = piece


def mate_sum_kernel(own, received, kept, *sent):
    kept[...] = own[0] + received[0].astype(F32)
    for p, out in enumerate(sent):
        out[...] = (own[p + 1] + received[p + 1].astype(F32)).astype(BF16)


def plane_sum_kernel(count, *refs):
    own, received, kept, sent = refs[0], refs[1 : 1 + count], refs[1 + count], refs[2 + count :]
    total = own[...]
    for piece in received:
        total = total + piece[...].astype(F32)
    kept[...] = total[0]
    for k, out in enumerate(sent):
        out[...] = total[k + 1].astype(BF16)


def norm_kernel(C, place, *refs):
    pieces, residual, gain, extra, hidden, rows_out = refs[:C], *refs[C:]
    ctx = place[0]
    cols = pieces[0].shape[1]
    features = residual.shape[1]
    for k in range(C):
        at = pl.ds(pl.multiple_of((ctx ^ k) * cols, 128), cols)
        hidden[:, at] = residual[:, at].astype(F32) + pieces[k][...].astype(F32)
    value = hidden[...]
    mean = jnp.sum(value, axis=1, keepdims=True) * (1.0 / features)
    centered = value - mean
    variance = jnp.sum(centered * centered, axis=1, keepdims=True) * (1.0 / features)
    normed = centered * lax.rsqrt(variance + 1e-05) * gain[...]
    rows_out[:, :features] = normed.astype(BF16)
    rows_out[:, features:] = extra[...]


def expert_kernel(E, groups, up_steps, place, *refs):
    packed = refs[: 2 * groups]
    gate, up, down = refs[2 * groups : 2 * groups + 3]
    outs = refs[2 * groups + 3 : 4 * groups + 3]
    rows, turned, activated, scale = refs[4 * groups + 3 :]
    step = pl.program_id(0)
    token_rows = packed[0].shape[1]
    features = rows.shape[1]
    depth = gate.shape[1]
    group_rows = packed[0].shape[0] * token_rows

    @pl.when(step == 0)
    def _():
        lane = lax.broadcasted_iota(jnp.int32, (group_rows, EXTRA), 1)
        wanted = ((lane & (E - 1)) == place[1]) & (lane < SPLIT * E)
        for g in range(2 * groups):
            at = slice(g * group_rows, (g + 1) * group_rows)
            value = packed[g][:, :, :features].astype(F32)
            rows[at, :] = value.reshape(group_rows, features).astype(BF16)
            tail = packed[g][:, :, features:].astype(F32).reshape(group_rows, EXTRA)
            scale[at, :] = jnp.sum(jnp.where(wanted, tail, 0.0), axis=1, keepdims=True)

    @pl.when(step < up_steps)
    def _():
        turned_dot = functools.partial(
            lax.dot_general,
            dimension_numbers=(((1,), (1,)), ((), ())),
            preferred_element_type=F32,
        )
        gate_part = turned_dot(gate[0], rows[...])
        up_part = turned_dot(up[0], rows[...])
        value = gate_part / (1.0 + jnp.exp(-gate_part)) * up_part
        turned[pl.ds(pl.multiple_of(step * depth, depth), depth), :] = value.astype(BF16)

    @pl.when(step == up_steps)
    def _():
        activated[...] = turned[...].T

    @pl.when(step >= up_steps)
    def _():
        piece = jnp.dot(activated[...], down[0], preferred_element_type=F32) * scale[...]
        for g in range(2 * groups):
            part = piece[g * group_rows : (g + 1) * group_rows]
            outs[g][...] = part.reshape(-1, token_rows, part.shape[1]).astype(BF16)


def largest_part(size, most, unit):
    return max(c for c in range(unit, most + 1, unit) if size % c == 0)


def run_experts(place, packed, gate_weight, up_weight, down_weight, E):
    count = len(packed)
    pieces, token_rows, wide = packed[0].shape
    features = wide - EXTRA
    units = gate_weight.shape[2]
    total = count * pieces * token_rows
    depth = largest_part(units, 192, 16)
    columns = largest_part(features, 768, 128)
    up_steps = units // depth
    down_steps = features // columns
    last = up_steps - 1

    def column_block(i):
        return jnp.maximum(i - up_steps, 0)

    once = pl.Buffered(1)
    return pl.pallas_call(
        functools.partial(expert_kernel, E, count // 2, up_steps),
        out_shape=[shape((pieces, token_rows, features), BF16) for _ in packed],
        grid=(up_steps + down_steps,),
        in_specs=[SCALARS]
        + [
            pl.BlockSpec((pieces, token_rows, wide), lambda i: (0, 0, 0), pipeline_mode=once)
            for _ in packed
        ]
        + [
            pl.BlockSpec((1, depth, features), lambda i: (0, jnp.minimum(i, last), 0)),
            pl.BlockSpec((1, depth, features), lambda i: (0, jnp.minimum(i, last), 0)),
            pl.BlockSpec((1, units, columns), lambda i: (0, 0, column_block(i))),
        ],
        out_specs=[
            pl.BlockSpec((pieces, token_rows, columns), lambda i: (0, 0, column_block(i)))
            for _ in packed
        ],
        scratch_shapes=[
            pltpu.VMEM((total, features), BF16),
            pltpu.VMEM((units, total), BF16),
            pltpu.VMEM((total, units), BF16),
            pltpu.VMEM((total, 1), F32),
        ],
        compiler_params=pltpu.CompilerParams(
            vmem_limit_bytes=(30 if total <= 256 else 56) * MIB,
            dimension_semantics=("arbitrary",),
        ),
        cost_estimate=pl.CostEstimate(
            flops=6 * total * features * units,
            bytes_accessed=6 * features * units + 4 * total * features,
            transcendentals=total * units,
        ),
    )(place, *packed, jnp.swapaxes(gate_weight, 1, 2), jnp.swapaxes(up_weight, 1, 2), down_weight)


def fold_kernel(plan, *refs):
    ins, outs = refs[: -len(plan)], refs[-len(plan) :]
    for out, (pair, places) in zip(outs, plan):
        kept, received = ins[2 * pair], ins[2 * pair + 1]
        for i, at in enumerate(places):
            out[i] = (kept[at].astype(F32) + received[at].astype(F32)).astype(BF16)


def fold(plan, operands):
    tail = operands[0].shape[1:]
    return call(
        functools.partial(fold_kernel, plan),
        [shape((len(places), *tail), BF16) for _, places in plan],
        operands,
        [WHOLE] * len(operands),
    )


def sum_over_plane(own, received, orders):
    chips = own.shape[0] // 2
    holds = [list(range(chips)) for _ in orders]
    operands, pairs, base = [own, received], [0, 0], [0, chips]
    for step in range(len(orders[0])):
        plan, keeps = [], []
        for s, order in enumerate(orders):
            far = 1 << (order[step] - 1)
            sent = [base[s] + i for i, p in enumerate(holds[s]) if p & far]
            kept = [base[s] + i for i, p in enumerate(holds[s]) if not p & far]
            holds[s] = [p for p in holds[s] if not p & far]
            plan.append((pairs[s], sent))
            keeps.append((pairs[s], kept))
        *sends, keep0, keep1 = fold(plan + keeps, operands)
        got = [swap(sent, "exp", 1 << order[step]) for sent, order in zip(sends, orders)]
        operands, pairs, base = [keep0, got[0], keep1, got[1]], [0, 1], [0, 0]
    return [value[0] for value in fold([(0, [0]), (1, [0])], operands)]


def on_device(
    queries,
    keys_values,
    residual,
    out_weight,
    norm_gain,
    routes,
    route_weight,
    gate_weight,
    up_weight,
    down_weight,
):
    C = lax.axis_size("ctx")
    E = lax.axis_size("exp")
    chips = E // 2
    chip_bits = list(range(1, E.bit_length() - 1))
    heads = queries.shape[1] // HD
    seq = queries.shape[0] * C
    token_rows, features = residual.shape
    cols = out_weight.shape[1]
    place = jnp.stack([lax.axis_index("ctx"), lax.axis_index("exp")]).astype(jnp.int32)

    own_kv = jnp.concatenate([keys_values[0], keys_values[1]], axis=1)
    bundle = jnp.concatenate([queries, own_kv, swap(own_kv, "exp", 1)], axis=1)
    blocks = [bundle] + [swap(bundle, "ctx", k) for k in range(1, C)]

    experts = jnp.arange(E, dtype=jnp.int32)
    left = jnp.sum(jnp.where(routes[:, :, None] == experts, route_weight[:, :, None], 0.0), axis=1)
    terms = []
    for _ in range(SPLIT):
        term = lax.reduce_precision(left, 8, 7)
        terms.append(term.astype(BF16))
        left = left - term
    extra = jnp.pad(jnp.concatenate(terms, axis=1), ((0, 0), (0, EXTRA - SPLIT * E)))

    mate_part, own_part = call(
        functools.partial(attend_kernel, C, E, heads),
        [
            shape((chips, C, token_rows, cols), BF16),
            shape((chips, C, token_rows, cols), F32),
        ],
        [place, *blocks, out_weight],
        [SCALARS] + [WHOLE] * (C + 1),
        [pltpu.VMEM((seq, cols), F32)],
        limit=16 if seq <= 256 else 56,
    )

    kept, *sent = call(
        mate_sum_kernel,
        [shape((C, token_rows, cols), F32)] + [shape((C, token_rows, cols), BF16)] * (chips - 1),
        [own_part, swap(mate_part, "exp", 1)],
        [WHOLE, WHOLE],
    )
    received = [swap(piece, "exp", (p + 1) << 1) for p, piece in enumerate(sent)]
    kept, *sent = call(
        functools.partial(plane_sum_kernel, chips - 1),
        [shape((token_rows, cols), F32)] + [shape((token_rows, cols), BF16)] * (C - 1),
        [kept, *received],
        [WHOLE] * chips,
    )
    pieces = [kept] + [swap(piece, "ctx", k + 1) for k, piece in enumerate(sent)]
    hidden, rows = call(
        functools.partial(norm_kernel, C),
        [shape((token_rows, features), F32), shape((token_rows, features + EXTRA), BF16)],
        [place, *pieces, residual, norm_gain.reshape(1, -1), extra],
        [SCALARS] + [WHOLE] * (C + 3),
    )

    shards = [rows] + [swap(rows, "ctx", k) for k in range(1, C)]
    packed = []
    for g in range(C // 2):
        group = []
        for s in range(2):
            held = {0: shards[2 * g + s]}
            for bit in chip_bits if s else chip_bits[::-1]:
                for p in sorted(held):
                    held[p | 1 << (bit - 1)] = swap(held[p], "exp", 1 << bit)
            group += [held[p] for p in range(chips)]
        packed.append(jnp.stack(group))
    packed += [swap(group, "exp", 1) for group in packed]

    outs = run_experts(place, packed, gate_weight, up_weight, down_weight, E)

    count = C // 2
    shards = [None] * C
    for g in reversed(range(count)):
        received = swap(outs[count + g], "exp", 1)
        pair = sum_over_plane(outs[g], received, (chip_bits, chip_bits[::-1]))
        shards[2 * g : 2 * g + 2] = pair
    total = hidden
    for k, shard in enumerate(shards):
        total = total + (swap(shard, "ctx", k) if k else shard).astype(F32)
    return total.astype(BF16)


def solution(mesh):
    in_specs = (
        P("ctx", "exp"),
        P(None, "ctx", "exp"),
        P(("ctx", "exp"), None),
        P("exp", "ctx"),
        P(),
        P(("ctx", "exp"), None),
        P(("ctx", "exp"), None),
        P("exp", None, "ctx"),
        P("exp", None, "ctx"),
        P("exp", "ctx", None),
    )
    out_specs = P(("ctx", "exp"), None)
    return jax.shard_map(
        on_device, mesh=mesh, in_specs=in_specs, out_specs=out_specs, check_vma=False
    )
```

```python
import functools
import math

import jax
import jax.numpy as jnp
from jax import lax
from jax.experimental import pallas as pl
from jax.experimental.pallas import tpu as pltpu
from jax.sharding import PartitionSpec as P

HD = 128
EXTRA = 128
SPLIT = 3
FIRST = 8
MIB = 1024 * 1024
F32 = jnp.float32
BF16 = jnp.bfloat16
WHOLE = pl.BlockSpec(memory_space=pltpu.VMEM)
SCALARS = pl.BlockSpec(memory_space=pltpu.SMEM)


def swap(value, axis, mask):
    return lax.ppermute(value, axis, [(i, i ^ mask) for i in range(lax.axis_size(axis))])


def call(kernel, out_shape, operands, in_specs, scratch=(), limit=16):
    return pl.pallas_call(
        kernel,
        out_shape=out_shape,
        in_specs=in_specs,
        out_specs=jax.tree.map(lambda _: WHOLE, out_shape),
        scratch_shapes=list(scratch),
        compiler_params=pltpu.CompilerParams(vmem_limit_bytes=limit * MIB),
    )(*operands)


def shape(dims, dtype):
    return jax.ShapeDtypeStruct(tuple(dims), dtype)


def attend_kernel(C, E, heads, place, *refs):
    blocks, out_weight, mate_out, own_out, projected = refs[:C], *refs[C:]
    ctx, exp = place[0], place[1]
    rows = blocks[0].shape[0]
    seq = rows * C
    width = heads * HD
    half = HD // 2
    lower = (exp & 1) == 0

    def joined(start):
        own = jnp.concatenate([b[:, start : start + half] for b in blocks], axis=0)
        first = start + 2 * half
        mate = jnp.concatenate([b[:, first : first + half] for b in blocks], axis=0)
        both = jnp.concatenate([own, mate], axis=1)
        other = jnp.concatenate([mate, own], axis=1)
        return jnp.where(lower, both, other)

    keys = joined(width)
    values = joined(width + half)
    shift = rows.bit_length() - 1
    column = lax.broadcasted_iota(jnp.int32, (rows, seq), 1)
    key_position = ((column >> shift) ^ ctx) * rows + (column & (rows - 1))
    row = lax.broadcasted_iota(jnp.int32, (rows, seq), 0)
    parts = []
    for k in range(C):
        allowed = key_position <= (ctx ^ k) * rows + row
        block_parts = []
        for h in range(heads):
            q = blocks[k][:, h * HD : (h + 1) * HD]
            scores = lax.dot_general(
                q, keys, (((1,), (1,)), ((), ())), preferred_element_type=F32
            ) * (1.0 / math.sqrt(HD))
            scores = jnp.where(allowed, scores, -jnp.inf)
            top = jnp.max(scores, axis=1, keepdims=True)
            weights = jnp.exp(scores - top)
            total = jnp.sum(weights, axis=1, keepdims=True)
            high = weights.astype(BF16)
            low = (weights - high.astype(F32)).astype(BF16)
            summed = jnp.dot(high, values, preferred_element_type=F32) + jnp.dot(
                low, values, preferred_element_type=F32
            )
            block_parts.append((summed / total).astype(BF16))
        parts.append(jnp.concatenate(block_parts, axis=1))
    attended = jnp.concatenate(parts, axis=0)
    projected[...] = jnp.dot(attended, out_weight[...], preferred_element_type=F32)
    token_rows = mate_out.shape[2]
    for p in range(E):
        for j in range(C):
            start = pl.multiple_of(((ctx ^ j) * E + (exp ^ p)) * token_rows, token_rows)
            piece = projected[pl.ds(start, token_rows), :]
            if p & 1:
                mate_out[p >> 1, j] = piece.astype(BF16)
            else:
                own_out[p >> 1, j] = piece


def mate_sum_kernel(own, received, kept, *sent):
    kept[...] = own[0] + received[0].astype(F32)
    for p, out in enumerate(sent):
        out[...] = (own[p + 1] + received[p + 1].astype(F32)).astype(BF16)


def residual_kernel(C, place, residual, extra, *outs):
    cols = outs[0].shape[1] - EXTRA
    for k, out in enumerate(outs):
        at = pl.ds(pl.multiple_of((place[0] ^ k) * cols, 128), cols)
        out[:, :cols] = residual[:, at]
        out[:, cols:] = extra[...]


def split_terms(value):
    terms = []
    for _ in range(SPLIT):
        term = value.astype(BF16).astype(F32)
        terms.append(term)
        value = value - term
    return terms


def plane_sum_kernel(C, count, place, *refs):
    own, received, residual = refs[0], refs[1 : 1 + count], refs[1 + count : 1 + count + C]
    out = refs[-1]
    cols = own.shape[2]
    lane = lax.broadcasted_iota(jnp.int32, (own.shape[1], EXTRA), 1)
    for k in range(C):
        j = place[0] ^ k
        total = own[j] + residual[k][:, :cols].astype(F32)
        for piece in received:
            total = total + piece[j].astype(F32)
        mean = jnp.sum(total, axis=1, keepdims=True) * (1.0 / cols)
        centered = total - mean
        squares = jnp.sum(centered * centered, axis=1, keepdims=True)
        out[j, :, :cols] = centered.astype(BF16)
        tail = residual[k][:, cols:].astype(F32)
        for i, term in enumerate(split_terms(mean) + split_terms(squares)):
            tail = jnp.where(lane == i, term, tail)
        out[j, :, cols:] = tail.astype(BF16)


def expert_kernel(C, E, per_block, place, *refs):
    groups = C // 2
    packed = refs[: 2 * groups]
    gain, gate, up, down = refs[2 * groups : 2 * groups + 4]
    outs = refs[2 * groups + 4 : 4 * groups + 4]
    hidden = refs[4 * groups + 4]
    gate_sum, up_sum, activated, piece, shift, spread, scale = refs[4 * groups + 5 :]
    step = pl.program_id(0)
    ctx, exp = place[0], place[1]
    chips = E // 2
    token_rows = packed[0].shape[2]
    cols = packed[0].shape[3] - EXTRA
    half_rows = chips * C * token_rows
    width = gate.shape[2]
    features = hidden.shape[1]
    up_steps = C * per_block

    def read(g, s, at):
        parts = [
            packed[side * groups + g][pl.ds(s * chips, chips), :, :, at] for side in range(2)
        ]
        parts = [part.astype(F32).reshape(half_rows, part.shape[-1]) for part in parts]
        return jnp.concatenate(parts, axis=0)

    @pl.when(step == 0)
    def _():
        tails = [read(k // 2, k % 2, slice(cols, cols + EXTRA)) for k in range(C)]
        lane = lax.broadcasted_iota(jnp.int32, tails[0].shape, 1)

        def pick(tail, wanted):
            return jnp.sum(jnp.where(wanted, tail, 0.0), axis=1, keepdims=True)

        means = [pick(tail, lane < SPLIT) for tail in tails]
        squares = [pick(tail, (lane >= SPLIT) & (lane < 2 * SPLIT)) for tail in tails]
        mean = sum(means) * (1.0 / C)
        deviation = sum(squares) + cols * sum((m - mean) * (m - mean) for m in means)
        spread[...] = lax.rsqrt(deviation * (1.0 / features) + 1e-05)
        for k in range(C):
            shift[k, 0] = means[k]
            shift[k, 1] = means[k] - mean
        first = lane - FIRST
        wanted = (first >= 0) & ((first & (E - 1)) == exp) & (first < SPLIT * E)
        scale[...] = pick(tails[0], wanted)

    for g in range(groups):
        k = step // per_block

        @pl.when((step < up_steps) & (k // 2 == g))
        def _():
            part = step % per_block
            s = k % 2
            at = pl.ds(pl.multiple_of(part * width, 128), width)
            place_at = pl.multiple_of((ctx ^ k) * cols + part * width, 128)
            centered = read(g, s, at)
            value = (centered + shift[k, 1]) * spread[...] * gain[:, pl.ds(place_at, width)]
            block = value.astype(BF16)
            own = packed[g][s * chips, ctx, :, at].astype(F32)
            own_mean = shift[k, 0, pl.ds(pl.multiple_of(ctx * token_rows, token_rows), token_rows)]
            hidden[:, pl.ds(place_at, width)] = own + own_mean
            turned_dot = functools.partial(
                lax.dot_general,
                dimension_numbers=(((1,), (1,)), ((), ())),
                preferred_element_type=F32,
            )

            @pl.when(step == 0)
            def _():
                gate_sum[...] = turned_dot(gate[0], block)
                up_sum[...] = turned_dot(up[0], block)

            @pl.when(step > 0)
            def _():
                gate_sum[...] += turned_dot(gate[0], block)
                up_sum[...] += turned_dot(up[0], block)

    @pl.when(step == up_steps)
    def _():
        value = gate_sum[...]
        value = value / (1.0 + jnp.exp(-value)) * up_sum[...]
        activated[...] = value.astype(BF16).T

    @pl.when(step >= up_steps)
    def _():
        piece[...] = jnp.dot(activated[...], down[0], preferred_element_type=F32) * scale[...]
        for g in range(groups):
            for side in range(2):
                for s in range(2):
                    for p in range(chips):
                        row = ((side * chips + p) * C + (ctx ^ (2 * g + s))) * token_rows
                        at = pl.ds(pl.multiple_of(row, token_rows), token_rows)
                        outs[side * groups + g][s * chips + p] = piece[at, :].astype(BF16)


def largest_part(size, most, unit):
    return max(c for c in range(unit, most + 1, unit) if size % c == 0)


def run_experts(place, packed, gain, gate_weight, up_weight, down_weight, C, E):
    count = len(packed)
    pieces, _, token_rows, wide = packed[0].shape
    cols = wide - EXTRA
    features = cols * C
    units = gate_weight.shape[2]
    total = C * E * token_rows
    small = total <= 256
    width = largest_part(cols, 768 if small else 384, 128)
    columns = largest_part(features, 768 if small else 384, 128)
    per_block = cols // width
    up_steps = C * per_block
    down_steps = features // columns

    def feature_block(i, place):
        i = jnp.minimum(i, up_steps - 1)
        return (0, 0, (place[0] ^ (i // per_block)) * per_block + i % per_block)

    def column_block(i, place):
        return (0, 0, jnp.maximum(i - up_steps, 0))

    def whole(*dims):
        return pl.BlockSpec(dims, lambda i, place: (0,) * len(dims), pipeline_mode=pl.Buffered(1))

    *outs, hidden = pl.pallas_call(
        functools.partial(expert_kernel, C, E, per_block),
        out_shape=[shape((pieces, token_rows, features), BF16) for _ in packed]
        + [shape((token_rows, features), F32)],
        grid_spec=pltpu.PrefetchScalarGridSpec(
            num_scalar_prefetch=1,
            grid=(up_steps + down_steps,),
            in_specs=[whole(*packed[0].shape) for _ in packed]
            + [
                whole(1, features),
                pl.BlockSpec((1, units, width), feature_block),
                pl.BlockSpec((1, units, width), feature_block),
                pl.BlockSpec((1, units, columns), column_block),
            ],
            out_specs=[pl.BlockSpec((pieces, token_rows, columns), column_block) for _ in packed]
            + [pl.BlockSpec((token_rows, features), lambda i, place: (0, 0))],
            scratch_shapes=[
                pltpu.VMEM((units, total), F32),
                pltpu.VMEM((units, total), F32),
                pltpu.VMEM((total, units), BF16),
                pltpu.VMEM((total, columns), F32),
                pltpu.VMEM((C, 2, total, 1), F32),
                pltpu.VMEM((total, 1), F32),
                pltpu.VMEM((total, 1), F32),
            ],
        ),
        compiler_params=pltpu.CompilerParams(
            vmem_limit_bytes=(44 if small else 58) * MIB,
            dimension_semantics=("arbitrary",),
        ),
        cost_estimate=pl.CostEstimate(
            flops=6 * total * features * units,
            bytes_accessed=6 * features * units + 4 * total * features,
            transcendentals=total * units,
        ),
    )(
        place,
        *packed,
        gain,
        jnp.swapaxes(gate_weight, 1, 2),
        jnp.swapaxes(up_weight, 1, 2),
        down_weight,
    )
    return outs, hidden


def fold_kernel(plan, *refs):
    ins, outs = refs[: -len(plan)], refs[-len(plan) :]
    for out, (pair, places) in zip(outs, plan):
        kept, received = ins[2 * pair], ins[2 * pair + 1]
        for i, at in enumerate(places):
            out[i] = (kept[at].astype(F32) + received[at].astype(F32)).astype(BF16)


def fold(plan, operands):
    tail = operands[0].shape[1:]
    return call(
        functools.partial(fold_kernel, plan),
        [shape((len(places), *tail), BF16) for _, places in plan],
        operands,
        [WHOLE] * len(operands),
    )


def sum_over_plane(own, received, orders):
    chips = own.shape[0] // 2
    holds = [list(range(chips)) for _ in orders]
    operands, pairs, base = [own, received], [0, 0], [0, chips]
    for step in range(len(orders[0])):
        plan, keeps = [], []
        for s, order in enumerate(orders):
            far = 1 << (order[step] - 1)
            sent = [base[s] + i for i, p in enumerate(holds[s]) if p & far]
            kept = [base[s] + i for i, p in enumerate(holds[s]) if not p & far]
            holds[s] = [p for p in holds[s] if not p & far]
            plan.append((pairs[s], sent))
            keeps.append((pairs[s], kept))
        *sends, keep0, keep1 = fold(plan + keeps, operands)
        got = [swap(sent, "exp", 1 << order[step]) for sent, order in zip(sends, orders)]
        operands, pairs, base = [keep0, got[0], keep1, got[1]], [0, 1], [0, 0]
    return [value[0] for value in fold([(0, [0]), (1, [0])], operands)]


def on_device(
    queries,
    keys_values,
    residual,
    out_weight,
    norm_gain,
    routes,
    route_weight,
    gate_weight,
    up_weight,
    down_weight,
):
    C = lax.axis_size("ctx")
    E = lax.axis_size("exp")
    chips = E // 2
    chip_bits = list(range(1, E.bit_length() - 1))
    heads = queries.shape[1] // HD
    seq = queries.shape[0] * C
    token_rows, features = residual.shape
    cols = out_weight.shape[1]
    place = jnp.stack([lax.axis_index("ctx"), lax.axis_index("exp")]).astype(jnp.int32)

    own_kv = jnp.concatenate([keys_values[0], keys_values[1]], axis=1)
    bundle = jnp.concatenate([queries, own_kv, swap(own_kv, "exp", 1)], axis=1)
    blocks = [bundle] + [swap(bundle, "ctx", k) for k in range(1, C)]

    experts = jnp.arange(E, dtype=jnp.int32)
    left = jnp.sum(jnp.where(routes[:, :, None] == experts, route_weight[:, :, None], 0.0), axis=1)
    terms = []
    for _ in range(SPLIT):
        term = lax.reduce_precision(left, 8, 7)
        terms.append(term.astype(BF16))
        left = left - term
    extra = jnp.pad(
        jnp.concatenate(terms, axis=1), ((0, 0), (FIRST, EXTRA - FIRST - SPLIT * E))
    )

    _, residual, extra = lax.optimization_barrier((bundle, residual, extra))
    sent = call(
        functools.partial(residual_kernel, C),
        [shape((token_rows, cols + EXTRA), BF16)] * C,
        [place, residual, extra],
        [SCALARS, WHOLE, WHOLE],
    )
    residuals = [swap(piece, "ctx", k) if k else piece for k, piece in enumerate(sent)]

    mate_part, own_part = call(
        functools.partial(attend_kernel, C, E, heads),
        [
            shape((chips, C, token_rows, cols), BF16),
            shape((chips, C, token_rows, cols), F32),
        ],
        [place, *blocks, out_weight],
        [SCALARS] + [WHOLE] * (C + 1),
        [pltpu.VMEM((seq, cols), F32)],
        limit=16 if seq <= 256 else 56,
    )

    kept, *sent = call(
        mate_sum_kernel,
        [shape((C, token_rows, cols), F32)] + [shape((C, token_rows, cols), BF16)] * (chips - 1),
        [own_part, swap(mate_part, "exp", 1)],
        [WHOLE, WHOLE],
    )
    received = [swap(piece, "exp", (p + 1) << 1) for p, piece in enumerate(sent)]
    (rows,) = call(
        functools.partial(plane_sum_kernel, C, chips - 1),
        [shape((C, token_rows, cols + EXTRA), BF16)],
        [place, kept, *received, *residuals],
        [SCALARS] + [WHOLE] * (chips + C),
    )

    shards = [rows] + [swap(rows, "ctx", k) for k in range(1, C)]
    packed = []
    for g in range(C // 2):
        group = []
        for s in range(2):
            held = {0: shards[2 * g + s]}
            for bit in chip_bits if s else chip_bits[::-1]:
                for p in sorted(held):
                    held[p | 1 << (bit - 1)] = swap(held[p], "exp", 1 << bit)
            group += [held[p] for p in range(chips)]
        packed.append(jnp.stack(group))
    packed += [swap(group, "exp", 1) for group in packed]

    outs, hidden = run_experts(
        place, packed, norm_gain.reshape(1, -1), gate_weight, up_weight, down_weight, C, E
    )

    count = C // 2
    shards = [None] * C
    for g in reversed(range(count)):
        received = swap(outs[count + g], "exp", 1)
        pair = sum_over_plane(outs[g], received, (chip_bits, chip_bits[::-1]))
        shards[2 * g : 2 * g + 2] = pair
    total = hidden
    for k, shard in enumerate(shards):
        total = total + (swap(shard, "ctx", k) if k else shard).astype(F32)
    return total.astype(BF16)


def solution(mesh):
    in_specs = (
        P("ctx", "exp"),
        P(None, "ctx", "exp"),
        P(("ctx", "exp"), None),
        P("exp", "ctx"),
        P(),
        P(("ctx", "exp"), None),
        P(("ctx", "exp"), None),
        P("exp", None, "ctx"),
        P("exp", None, "ctx"),
        P("exp", "ctx", None),
    )
    out_specs = P(("ctx", "exp"), None)
    return jax.shard_map(
        on_device, mesh=mesh, in_specs=in_specs, out_specs=out_specs, check_vma=False
    )
```

```python
import functools
import math

import jax
import jax.numpy as jnp
from jax import lax
from jax.experimental import pallas as pl
from jax.experimental.pallas import tpu as pltpu
from jax.sharding import PartitionSpec as P

HD = 128
EXTRA = 128
SPLIT = 3
FIRST = 8
MIB = 1024 * 1024
F32 = jnp.float32
BF16 = jnp.bfloat16
WHOLE = pl.BlockSpec(memory_space=pltpu.VMEM)
SCALARS = pl.BlockSpec(memory_space=pltpu.SMEM)
IN_HBM = pl.BlockSpec(memory_space=pltpu.HBM)


def swap(value, axis, mask):
    return lax.ppermute(value, axis, [(i, i ^ mask) for i in range(lax.axis_size(axis))])


def call(kernel, out_shape, operands, in_specs, scratch=(), limit=16):
    return pl.pallas_call(
        kernel,
        out_shape=out_shape,
        in_specs=in_specs,
        out_specs=jax.tree.map(lambda _: WHOLE, out_shape),
        scratch_shapes=list(scratch),
        compiler_params=pltpu.CompilerParams(vmem_limit_bytes=limit * MIB),
    )(*operands)


def shape(dims, dtype):
    return jax.ShapeDtypeStruct(tuple(dims), dtype)


def attend_kernel(C, E, heads, place, *refs):
    messages, out_weight, mate_out, own_out = refs[:C], *refs[C : C + 3]
    projected, weight, weight_sem = refs[C + 3 :]
    load = pltpu.make_async_copy(out_weight, weight, weight_sem)
    load.start()
    ctx, exp = place[0], place[1]
    token_rows = mate_out.shape[2]
    rows = E * token_rows
    seq = rows * C
    blocks = [
        m[:E].astype(F32).reshape(rows, m.shape[2]).astype(BF16) for m in messages
    ]
    width = heads * HD
    half = HD // 2
    lower = (exp & 1) == 0

    def joined(start):
        own = jnp.concatenate([b[:, start : start + half] for b in blocks], axis=0)
        first = start + 2 * half
        mate = jnp.concatenate([b[:, first : first + half] for b in blocks], axis=0)
        both = jnp.concatenate([own, mate], axis=1)
        other = jnp.concatenate([mate, own], axis=1)
        return jnp.where(lower, both, other)

    keys = joined(width)
    values = joined(width + half)
    shift = rows.bit_length() - 1
    column = lax.broadcasted_iota(jnp.int32, (rows, seq), 1)
    key_position = ((column >> shift) ^ ctx) * rows + (column & (rows - 1))
    row = lax.broadcasted_iota(jnp.int32, (rows, seq), 0)
    parts = []
    for k in range(C):
        allowed = key_position <= (ctx ^ k) * rows + row
        block_parts = []
        for h in range(heads):
            q = blocks[k][:, h * HD : (h + 1) * HD]
            scores = lax.dot_general(
                q, keys, (((1,), (1,)), ((), ())), preferred_element_type=F32
            ) * (1.0 / math.sqrt(HD))
            scores = jnp.where(allowed, scores, -jnp.inf)
            top = jnp.max(scores, axis=1, keepdims=True)
            weights = jnp.exp(scores - top)
            total = jnp.sum(weights, axis=1, keepdims=True)
            high = weights.astype(BF16)
            low = (weights - high.astype(F32)).astype(BF16)
            summed = jnp.dot(high, values, preferred_element_type=F32) + jnp.dot(
                low, values, preferred_element_type=F32
            )
            block_parts.append((summed / total).astype(BF16))
        parts.append(jnp.concatenate(block_parts, axis=1))
    attended = jnp.concatenate(parts, axis=0)
    load.wait()
    projected[...] = jnp.dot(attended, weight[...], preferred_element_type=F32)
    for p in range(E):
        for j in range(C):
            start = pl.multiple_of(((ctx ^ j) * E + (exp ^ p)) * token_rows, token_rows)
            piece = projected[pl.ds(start, token_rows), :]
            if p & 1:
                mate_out[p >> 1, j] = piece.astype(BF16)
            else:
                own_out[p >> 1, j] = piece


def mate_sum_kernel(own, received, kept, *sent):
    kept[...] = own[0] + received[0].astype(F32)
    for p, out in enumerate(sent):
        out[...] = (own[p + 1] + received[p + 1].astype(F32)).astype(BF16)


def message_kernel(C, E, place, queries_in, own_in, mate, residual_in, gain_in, *outs):
    messages, gain_out = outs[:C], outs[C]
    queries, own, residual, sems = outs[C + 1 :]
    loads = [
        pltpu.make_async_copy(source, target, sems.at[i])
        for i, (source, target) in enumerate(
            [
                (queries_in, queries),
                (own_in, own),
                (residual_in, residual),
                (gain_in, gain_out),
            ]
        )
    ]
    for load in loads:
        load.start()
    for load in loads:
        load.wait()
    token_rows, wide = messages[0].shape[1:]
    cols = residual.shape[1] // C
    parts = [queries[...], own[0], own[1], mate[0], mate[1]]
    bundle = jnp.concatenate([part.astype(F32) for part in parts], axis=1)
    bundle = bundle.reshape(E, token_rows, wide).astype(BF16)
    for k, out in enumerate(messages):
        out[:E] = bundle
        first = (place[0] ^ k) * cols
        for i in range(out.shape[0] - E):
            width = min(wide, cols - i * wide)
            at = pl.ds(pl.multiple_of(first + i * wide, 128), width)
            out[E + i, :, :width] = residual[:, at]


def split_terms(value):
    terms = []
    for _ in range(SPLIT):
        term = value.astype(BF16).astype(F32)
        terms.append(term)
        value = value - term
    return terms


def plane_sum_kernel(C, E, count, place, *refs):
    own, received, messages = refs[0], refs[1 : 1 + count], refs[1 + count : 1 + count + C]
    extra, out = refs[1 + count + C :]
    cols = own.shape[2]
    wide = messages[0].shape[2]
    lane = lax.broadcasted_iota(jnp.int32, (own.shape[1], EXTRA), 1)
    for k in range(C):
        j = place[0] ^ k
        pieces = [
            messages[k][E + i, :, : min(wide, cols - i * wide)].astype(F32)
            for i in range(messages[k].shape[0] - E)
        ]
        total = own[j] + jnp.concatenate(pieces, axis=1)
        for piece in received:
            total = total + piece[j].astype(F32)
        mean = jnp.sum(total, axis=1, keepdims=True) * (1.0 / cols)
        centered = total - mean
        squares = jnp.sum(centered * centered, axis=1, keepdims=True)
        out[j, :, :cols] = centered.astype(BF16)
        tail = jnp.zeros(lane.shape, F32) if k else extra[...].astype(F32)
        for i, term in enumerate(split_terms(mean) + split_terms(squares)):
            tail = jnp.where(lane == i, term, tail)
        out[j, :, cols:] = tail.astype(BF16)


def pack_kernel(plan, *refs):
    ins, outs = refs[: -len(plan)], refs[-len(plan) :]
    for out, sources in zip(outs, plan):
        for i, (at, place) in enumerate(sources):
            value = ins[at][...] if place is None else ins[at][place]
            if len(sources) == 1:
                out[...] = value
            else:
                out[i] = value


def pack(plan, arrays, tail):
    return call(
        functools.partial(pack_kernel, plan),
        [shape(tail if len(p) == 1 else (len(p), *tail), BF16) for p in plan],
        arrays,
        [WHOLE] * len(arrays),
    )


def spread_over_plane(arrays, sources, orders, chips):
    tail = arrays[0].shape[-3:]
    holds = [{0: source} for source in sources]
    arrays = list(arrays)
    for step in range(len(orders[0])):
        plan = [[hold[p] for p in sorted(hold)] for hold in holds]
        if step == 0 and len(arrays) == 2:
            sends = arrays[:]
        else:
            sends = pack(plan, arrays, tail)
        for hold, order, send in zip(holds, orders, sends):
            at = len(arrays)
            arrays.append(swap(send, "exp", 1 << order[step]))
            far = 1 << (order[step] - 1)
            for i, p in enumerate(sorted(hold)):
                hold[p | far] = (at, None if step == 0 else i)
    (packed,) = pack([[hold[p] for hold in holds for p in range(chips)]], arrays, tail)
    return packed


def expert_kernel(C, E, per_block, place, *refs):
    groups = C // 2
    packed = refs[: 2 * groups]
    gain, gate, up, down = refs[2 * groups : 2 * groups + 4]
    outs = refs[2 * groups + 4 : 4 * groups + 4]
    hidden = refs[4 * groups + 4]
    gate_sum, up_sum, activated, piece, shift, spread, scale = refs[4 * groups + 5 :]
    step = pl.program_id(0)
    ctx, exp = place[0], place[1]
    chips = E // 2
    token_rows = packed[0].shape[2]
    cols = packed[0].shape[3] - EXTRA
    half_rows = chips * C * token_rows
    width = gate.shape[2]
    features = hidden.shape[1]
    up_steps = C * per_block

    def read(g, s, at):
        parts = [
            packed[side * groups + g][pl.ds(s * chips, chips), :, :, at] for side in range(2)
        ]
        parts = [part.astype(F32).reshape(half_rows, part.shape[-1]) for part in parts]
        return jnp.concatenate(parts, axis=0)

    @pl.when(step == 0)
    def _():
        tails = [read(k // 2, k % 2, slice(cols, cols + EXTRA)) for k in range(C)]
        lane = lax.broadcasted_iota(jnp.int32, tails[0].shape, 1)

        def pick(tail, wanted):
            return jnp.sum(jnp.where(wanted, tail, 0.0), axis=1, keepdims=True)

        means = [pick(tail, lane < SPLIT) for tail in tails]
        squares = [pick(tail, (lane >= SPLIT) & (lane < 2 * SPLIT)) for tail in tails]
        mean = sum(means) * (1.0 / C)
        deviation = sum(squares) + cols * sum((m - mean) * (m - mean) for m in means)
        spread[...] = lax.rsqrt(deviation * (1.0 / features) + 1e-05)
        for k in range(C):
            shift[k, 0] = means[k]
            shift[k, 1] = means[k] - mean
        first = lane - FIRST
        wanted = (first >= 0) & ((first & (E - 1)) == exp) & (first < SPLIT * E)
        scale[...] = sum(pick(tail, wanted) for tail in tails)

    for g in range(groups):
        k = step // per_block

        @pl.when((step < up_steps) & (k // 2 == g))
        def _():
            part = step % per_block
            s = k % 2
            at = pl.ds(pl.multiple_of(part * width, 128), width)
            place_at = pl.multiple_of((ctx ^ k) * cols + part * width, 128)
            centered = read(g, s, at)
            value = (centered + shift[k, 1]) * spread[...] * gain[:, pl.ds(place_at, width)]
            block = value.astype(BF16)
            own = packed[g][s * chips, ctx, :, at].astype(F32)
            own_mean = shift[k, 0, pl.ds(pl.multiple_of(ctx * token_rows, token_rows), token_rows)]
            hidden[:, pl.ds(place_at, width)] = own + own_mean
            turned_dot = functools.partial(
                lax.dot_general,
                dimension_numbers=(((1,), (1,)), ((), ())),
                preferred_element_type=F32,
            )

            @pl.when(step == 0)
            def _():
                gate_sum[...] = turned_dot(block, gate[0])
                up_sum[...] = turned_dot(block, up[0])

            @pl.when(step > 0)
            def _():
                gate_sum[...] += turned_dot(block, gate[0])
                up_sum[...] += turned_dot(block, up[0])

    @pl.when(step == up_steps)
    def _():
        value = gate_sum[...]
        value = value / (1.0 + jnp.exp(-value)) * up_sum[...]
        activated[...] = value.astype(BF16)

    @pl.when(step >= up_steps)
    def _():
        piece[...] = jnp.dot(activated[...], down[0], preferred_element_type=F32) * scale[...]
        for g in range(groups):
            for side in range(2):
                for s in range(2):
                    for p in range(chips):
                        row = ((side * chips + p) * C + (ctx ^ (2 * g + s))) * token_rows
                        at = pl.ds(pl.multiple_of(row, token_rows), token_rows)
                        outs[side * groups + g][s * chips + p] = piece[at, :].astype(BF16)


def largest_part(size, most, unit):
    return max(c for c in range(unit, most + 1, unit) if size % c == 0)


def run_experts(place, packed, gain, gate_weight, up_weight, down_weight, C, E):
    count = len(packed)
    pieces, _, token_rows, wide = packed[0].shape
    cols = wide - EXTRA
    features = cols * C
    units = gate_weight.shape[2]
    total = C * E * token_rows
    small = total <= 256
    width = largest_part(cols, 768 if small else 384, 128)
    columns = largest_part(features, 1024 if small else 384, 128)
    per_block = cols // width
    up_steps = C * per_block
    down_steps = features // columns

    def feature_block(i, place):
        i = jnp.minimum(i, up_steps - 1)
        return (0, 0, (place[0] ^ (i // per_block)) * per_block + i % per_block)

    def column_block(i, place):
        return (0, 0, jnp.maximum(i - up_steps, 0))

    def whole(*dims):
        return pl.BlockSpec(dims, lambda i, place: (0,) * len(dims), pipeline_mode=pl.Buffered(1))

    *outs, hidden = pl.pallas_call(
        functools.partial(expert_kernel, C, E, per_block),
        out_shape=[shape((pieces, token_rows, features), BF16) for _ in packed]
        + [shape((token_rows, features), F32)],
        grid_spec=pltpu.PrefetchScalarGridSpec(
            num_scalar_prefetch=1,
            grid=(up_steps + down_steps,),
            in_specs=[whole(*packed[0].shape) for _ in packed]
            + [
                whole(1, features),
                pl.BlockSpec((1, units, width), feature_block),
                pl.BlockSpec((1, units, width), feature_block),
                pl.BlockSpec((1, units, columns), column_block),
            ],
            out_specs=[pl.BlockSpec((pieces, token_rows, columns), column_block) for _ in packed]
            + [pl.BlockSpec((token_rows, features), lambda i, place: (0, 0))],
            scratch_shapes=[
                pltpu.VMEM((total, units), F32),
                pltpu.VMEM((total, units), F32),
                pltpu.VMEM((total, units), BF16),
                pltpu.VMEM((total, columns), F32),
                pltpu.VMEM((C, 2, total, 1), F32),
                pltpu.VMEM((total, 1), F32),
                pltpu.VMEM((total, 1), F32),
            ],
        ),
        compiler_params=pltpu.CompilerParams(
            vmem_limit_bytes=(44 if small else 58) * MIB,
            dimension_semantics=("arbitrary",),
        ),
        cost_estimate=pl.CostEstimate(
            flops=6 * total * features * units,
            bytes_accessed=6 * features * units + 4 * total * features,
            transcendentals=total * units,
        ),
    )(
        place,
        *packed,
        gain,
        jnp.swapaxes(gate_weight, 1, 2),
        jnp.swapaxes(up_weight, 1, 2),
        down_weight,
    )
    return outs, hidden


def fold_kernel(plan, *refs):
    ins, outs = refs[: -len(plan)], refs[-len(plan) :]
    for out, places in zip(outs, plan):
        for i, parts in enumerate(places):
            out[i] = sum(ins[at][place].astype(F32) for at, place in parts).astype(BF16)


def fold(plan, operands):
    tail = operands[0].shape[1:]
    return call(
        functools.partial(fold_kernel, plan),
        [shape((len(places), *tail), BF16) for places in plan],
        operands,
        [WHOLE] * len(operands),
    )


def sum_over_plane(own, received, orders, added, apart):
    chips = own.shape[0] // 2
    operands = [own, received]
    holds = [
        {p: [(0, s * chips + p), (1, s * chips + p)] for p in range(chips)}
        for s in range(len(orders))
    ]
    for step in range(len(orders[0])):
        far = [1 << (order[step] - 1) for order in orders]
        sent = [[p for p in sorted(hold) if p & f] for hold, f in zip(holds, far)]
        kept = [[p for p in sorted(hold) if not p & f] for hold, f in zip(holds, far)]
        plan = [[hold[p] for p in ps] for hold, ps in zip(holds * 2, sent + kept)]
        *sends, keep0, keep1 = fold(plan, operands)
        got = [swap(value, "exp", 1 << order[step]) for value, order in zip(sends, orders)]
        operands = [keep0, got[0], keep1, got[1]]
        holds = [
            {p: [(2 * s, i), (2 * s + 1, i)] for i, p in enumerate(kept[s])}
            for s in range(len(orders))
        ]
    parts = [hold[0] + [(4 + i, s) for i in range(len(added))] for s, hold in enumerate(holds)]
    return fold([[part] for part in parts] if apart else [parts], operands + added)


def on_device(
    queries,
    keys_values,
    residual,
    out_weight,
    norm_gain,
    routes,
    route_weight,
    gate_weight,
    up_weight,
    down_weight,
):
    C = lax.axis_size("ctx")
    E = lax.axis_size("exp")
    chips = E // 2
    chip_bits = list(range(1, E.bit_length() - 1))
    heads = queries.shape[1] // HD
    seq = queries.shape[0] * C
    token_rows, features = residual.shape
    cols = out_weight.shape[1]
    place = jnp.stack([lax.axis_index("ctx"), lax.axis_index("exp")]).astype(jnp.int32)

    wide = queries.shape[1] + 2 * HD
    slots = E + -(-cols // wide)
    *sent, gain = call(
        functools.partial(message_kernel, C, E),
        [shape((slots, token_rows, wide), BF16)] * C + [shape((1, features), F32)],
        [
            place,
            queries,
            keys_values,
            swap(keys_values, "exp", 1),
            residual,
            norm_gain.reshape(1, -1),
        ],
        [SCALARS, IN_HBM, IN_HBM, WHOLE, IN_HBM, IN_HBM],
        [
            pltpu.VMEM(queries.shape, BF16),
            pltpu.VMEM(keys_values.shape, BF16),
            pltpu.VMEM(residual.shape, BF16),
            pltpu.SemaphoreType.DMA((4,)),
        ],
        limit=60,
    )
    messages = [swap(piece, "ctx", k) if k else piece for k, piece in enumerate(sent)]

    experts = jnp.arange(E, dtype=jnp.int32)
    left = jnp.sum(jnp.where(routes[:, :, None] == experts, route_weight[:, :, None], 0.0), axis=1)
    terms = []
    for _ in range(SPLIT):
        term = lax.reduce_precision(left, 8, 7)
        terms.append(term.astype(BF16))
        left = left - term
    extra = jnp.pad(
        jnp.concatenate(terms, axis=1), ((0, 0), (FIRST, EXTRA - FIRST - SPLIT * E))
    )

    mate_part, own_part = call(
        functools.partial(attend_kernel, C, E, heads),
        [
            shape((chips, C, token_rows, cols), BF16),
            shape((chips, C, token_rows, cols), F32),
        ],
        [place, *messages, out_weight],
        [SCALARS] + [WHOLE] * C + [IN_HBM],
        [
            pltpu.VMEM((seq, cols), F32),
            pltpu.VMEM(out_weight.shape, BF16),
            pltpu.SemaphoreType.DMA,
        ],
        limit=16 if seq <= 256 else 56,
    )

    kept, *sent = call(
        mate_sum_kernel,
        [shape((C, token_rows, cols), F32)] + [shape((C, token_rows, cols), BF16)] * (chips - 1),
        [own_part, swap(mate_part, "exp", 1)],
        [WHOLE, WHOLE],
    )
    received = [swap(piece, "exp", (p + 1) << 1) for p, piece in enumerate(sent)]
    (rows,) = call(
        functools.partial(plane_sum_kernel, C, E, chips - 1),
        [shape((C, token_rows, cols + EXTRA), BF16)],
        [place, kept, *received, *messages, extra],
        [SCALARS] + [WHOLE] * (chips + C + 1),
    )

    orders = (chip_bits[::-1], chip_bits)
    near = [rows, swap(rows, "ctx", 1)]
    (pair,) = pack([[(0, None), (1, None)]], near, rows.shape)
    pairs = [pair]
    for bit in range(1, C.bit_length() - 1):
        pairs += [swap(value, "ctx", 1 << bit) for value in pairs]
    packed = [spread_over_plane(near, [(0, None), (1, None)], orders, chips)]
    packed += [spread_over_plane([p], [(0, 0), (0, 1)], orders, chips) for p in pairs[1:]]
    packed += [swap(group, "exp", 1) for group in packed]

    outs, hidden = run_experts(
        place, packed, gain, gate_weight, up_weight, down_weight, C, E
    )

    count = C // 2
    added = [[] for _ in range(count)]
    for g in reversed(range(count)):
        received = swap(outs[count + g], "exp", 1)
        values = sum_over_plane(outs[g], received, orders[::-1], added[g], g == 0)
        if g:
            top = 1 << (g.bit_length() - 1)
            added[g ^ top].append(swap(values[0], "ctx", 2 * top))
    kept, sent = values
    total = hidden + kept[0].astype(F32) + swap(sent, "ctx", 1)[0].astype(F32)
    return total.astype(BF16)


def solution(mesh):
    in_specs = (
        P("ctx", "exp"),
        P(None, "ctx", "exp"),
        P(("ctx", "exp"), None),
        P("exp", "ctx"),
        P(),
        P(("ctx", "exp"), None),
        P(("ctx", "exp"), None),
        P("exp", None, "ctx"),
        P("exp", None, "ctx"),
        P("exp", "ctx", None),
    )
    out_specs = P(("ctx", "exp"), None)
    return jax.shard_map(
        on_device, mesh=mesh, in_specs=in_specs, out_specs=out_specs, check_vma=False
    )
```

```python
import functools
import math

import jax
import jax.numpy as jnp
from jax import lax
from jax.experimental import pallas as pl
from jax.experimental.pallas import tpu as pltpu
from jax.sharding import PartitionSpec as P

HD = 128
EXTRA = 128
SPLIT = 3
FIRST = 8
MIB = 1024 * 1024
F32 = jnp.float32
BF16 = jnp.bfloat16
WHOLE = pl.BlockSpec(memory_space=pltpu.VMEM)
IN_HBM = pl.BlockSpec(memory_space=pltpu.HBM)


def swap(value, axis, mask):
    return lax.ppermute(value, axis, [(i, i ^ mask) for i in range(lax.axis_size(axis))])


def call(kernel, out_shape, operands, in_specs, scratch=(), limit=16):
    return pl.pallas_call(
        kernel,
        out_shape=out_shape,
        in_specs=in_specs,
        out_specs=jax.tree.map(lambda _: WHOLE, out_shape),
        scratch_shapes=list(scratch),
        compiler_params=pltpu.CompilerParams(vmem_limit_bytes=limit * MIB),
    )(*operands)


def shape(dims, dtype):
    return jax.ShapeDtypeStruct(tuple(dims), dtype)


def attend_kernel(C, E, heads, *refs):
    messages, mates, out_weight, mate_out, own_out, projected = refs[:C], *refs[C:]
    ctx, exp = lax.axis_index("ctx"), lax.axis_index("exp")
    token_rows = mate_out.shape[2]
    rows = E * token_rows
    seq = rows * C
    blocks = [
        m[:E].astype(F32).reshape(rows, m.shape[2]).astype(BF16) for m in messages
    ]
    width = heads * HD
    half = HD // 2
    lower = (exp & 1) == 0

    other_half = mates[...].astype(F32).reshape(seq, HD).astype(BF16)

    def joined(start):
        first = width + start
        own = jnp.concatenate([b[:, first : first + half] for b in blocks], axis=0)
        mate = other_half[:, start : start + half]
        both = jnp.concatenate([own, mate], axis=1)
        other = jnp.concatenate([mate, own], axis=1)
        return jnp.where(lower, both, other)

    keys = joined(0)
    values = joined(half)
    shift = rows.bit_length() - 1
    column = lax.broadcasted_iota(jnp.int32, (rows, seq), 1)
    key_position = ((column >> shift) ^ ctx) * rows + (column & (rows - 1))
    row = lax.broadcasted_iota(jnp.int32, (rows, seq), 0)
    parts = []
    for k in range(C):
        allowed = key_position <= (ctx ^ k) * rows + row
        block_parts = []
        for h in range(heads):
            q = blocks[k][:, h * HD : (h + 1) * HD]
            scores = lax.dot_general(
                q, keys, (((1,), (1,)), ((), ())), preferred_element_type=F32
            ) * (1.0 / math.sqrt(HD))
            scores = jnp.where(allowed, scores, -jnp.inf)
            top = jnp.max(scores, axis=1, keepdims=True)
            weights = jnp.exp(scores - top)
            total = jnp.sum(weights, axis=1, keepdims=True)
            high = weights.astype(BF16)
            low = (weights - high.astype(F32)).astype(BF16)
            summed = jnp.dot(high, values, preferred_element_type=F32) + jnp.dot(
                low, values, preferred_element_type=F32
            )
            block_parts.append((summed / total).astype(BF16))
        parts.append(jnp.concatenate(block_parts, axis=1))
    attended = jnp.concatenate(parts, axis=0)
    projected[...] = jnp.dot(attended, out_weight[...], preferred_element_type=F32)
    for p in range(E):
        for j in range(C):
            start = pl.multiple_of(((ctx ^ j) * E + (exp ^ p)) * token_rows, token_rows)
            piece = projected[pl.ds(start, token_rows), :]
            if p & 1:
                mate_out[p >> 1, j] = piece.astype(BF16)
            else:
                own_out[p >> 1, j] = piece


def mate_sum_kernel(own, received, kept, *sent):
    kept[...] = own[0] + received[0].astype(F32)
    for p, out in enumerate(sent):
        out[...] = (own[p + 1] + received[p + 1].astype(F32)).astype(BF16)


def message_kernel(C, E, queries_in, own_in, residual_in, *refs):
    messages = refs[:C]
    queries, own, residual, sems = refs[C:]
    pairs = [(queries_in, queries), (own_in, own), (residual_in, residual)]
    loads = [pltpu.make_async_copy(a, b, sems.at[i]) for i, (a, b) in enumerate(pairs)]
    for load in loads:
        load.start()
    for load in loads:
        load.wait()
    token_rows, wide = messages[0].shape[1:]
    cols = residual.shape[1] // C
    parts = [queries[...], own[0], own[1]]
    bundle = jnp.concatenate([part.astype(F32) for part in parts], axis=1)
    bundle = bundle.reshape(E, token_rows, wide).astype(BF16)
    ctx = lax.axis_index("ctx")
    for k, out in enumerate(messages):
        out[:E] = bundle
        first = (ctx ^ k) * cols
        for i in range(out.shape[0] - E):
            width = min(wide, cols - i * wide)
            at = pl.ds(pl.multiple_of(first + i * wide, 128), width)
            out[E + i, :, :width] = residual[:, at]


def keep_kernel(after, out_weight, gain, weight_out, gain_out):
    weight_out[...] = out_weight[...]
    gain_out[...] = gain[...]


def halves_kernel(C, E, *refs):
    for k in range(C):
        refs[-1][k] = refs[k][:E, :, refs[k].shape[2] - HD :]


def split_terms(value):
    terms = []
    for _ in range(SPLIT):
        term = value.astype(BF16).astype(F32)
        terms.append(term)
        value = value - term
    return terms


def plane_sum_kernel(C, E, count, *refs):
    own, received, messages = refs[0], refs[1 : 1 + count], refs[1 + count : 1 + count + C]
    extra, out = refs[1 + count + C :]
    cols = own.shape[2]
    wide = messages[0].shape[2]
    lane = lax.broadcasted_iota(jnp.int32, (own.shape[1], EXTRA), 1)
    for k in range(C):
        j = lax.axis_index("ctx") ^ k
        pieces = [
            messages[k][E + i, :, : min(wide, cols - i * wide)].astype(F32)
            for i in range(messages[k].shape[0] - E)
        ]
        total = own[j] + jnp.concatenate(pieces, axis=1)
        for piece in received:
            total = total + piece[j].astype(F32)
        mean = jnp.sum(total, axis=1, keepdims=True) * (1.0 / cols)
        centered = total - mean
        squares = jnp.sum(centered * centered, axis=1, keepdims=True)
        out[j, :, :cols] = centered.astype(BF16)
        tail = jnp.zeros(lane.shape, F32) if k else extra[...].astype(F32)
        for i, term in enumerate(split_terms(mean) + split_terms(squares)):
            tail = jnp.where(lane == i, term, tail)
        out[j, :, cols:] = tail.astype(BF16)


def pack_kernel(plan, *refs):
    ins, outs = refs[: -len(plan)], refs[-len(plan) :]
    for out, sources in zip(outs, plan):
        for i, (at, place) in enumerate(sources):
            value = ins[at][...] if place is None else ins[at][place]
            if len(sources) == 1:
                out[...] = value
            else:
                out[i] = value


def pack(plan, arrays, tail, after=()):
    return call(
        functools.partial(pack_kernel, plan),
        [shape(tail if len(p) == 1 else (len(p), *tail), BF16) for p in plan],
        [*arrays, *after],
        [WHOLE] * (len(arrays) + len(after)),
    )


def spread_over_plane(arrays, sources, orders, chips, after):
    tail = arrays[0].shape[-3:]
    holds = [{0: source} for source in sources]
    arrays = list(arrays)
    for step in range(len(orders[0])):
        plan = [[hold[p] for p in sorted(hold)] for hold in holds]
        if step == 0 and len(arrays) == 2:
            sends = arrays[:]
        else:
            sends = pack(plan, arrays, tail, after)
            after = []
        for hold, order, send in zip(holds, orders, sends):
            at = len(arrays)
            arrays.append(swap(send, "exp", 1 << order[step]))
            far = 1 << (order[step] - 1)
            for i, p in enumerate(sorted(hold)):
                hold[p | far] = (at, None if step == 0 else i)
    (packed,) = pack([[hold[p] for hold in holds for p in range(chips)]], arrays, tail)
    return packed, sends


def expert_kernel(C, E, per_block, width, columns, *refs):
    groups = C // 2
    packed = refs[: 2 * groups]
    gain, gate, up, down = refs[2 * groups : 2 * groups + 4]
    outs = refs[2 * groups + 4 : 4 * groups + 4]
    hidden = refs[4 * groups + 4]
    gate_sum, up_sum, activated, piece, shift, spread, scale = refs[4 * groups + 5 : -5]
    gate_slots, up_slots, down_slots, up_sems, down_sems = refs[-5:]
    step = pl.program_id(0)
    ctx, exp = lax.axis_index("ctx"), lax.axis_index("exp")
    chips = E // 2
    token_rows = packed[0].shape[2]
    cols = packed[0].shape[3] - EXTRA
    half_rows = chips * C * token_rows
    features = hidden.shape[1]
    up_steps = C * per_block
    down_steps = features // columns
    ahead, down_ahead = gate_slots.shape[0], down_slots.shape[0]

    def up_copies(i, slot):
        at = pl.ds(pl.multiple_of(i * width, 128), width)
        return [
            pltpu.make_async_copy(gate.at[0, :, at], gate_slots.at[slot], up_sems.at[0, slot]),
            pltpu.make_async_copy(up.at[0, :, at], up_slots.at[slot], up_sems.at[1, slot]),
        ]

    def down_copy(i, slot):
        at = pl.ds(pl.multiple_of(i * columns, 128), columns)
        return pltpu.make_async_copy(down.at[0, :, at], down_slots.at[slot], down_sems.at[slot])

    @pl.when(step == 0)
    def _():
        for i in range(ahead):
            for copy in up_copies(i, i):
                copy.start()

    @pl.when(step < up_steps)
    def _():
        for copy in up_copies(step, step % ahead):
            copy.wait()

    @pl.when(step >= up_steps)
    def _():
        done = step - up_steps
        down_copy(done, done % down_ahead).wait()

    def read(g, s, at):
        parts = [
            packed[side * groups + g][pl.ds(s * chips, chips), :, :, at] for side in range(2)
        ]
        parts = [part.astype(F32).reshape(half_rows, part.shape[-1]) for part in parts]
        return jnp.concatenate(parts, axis=0)

    @pl.when(step == 0)
    def _():
        tails = [read(k // 2, k % 2, slice(cols, cols + EXTRA)) for k in range(C)]
        lane = lax.broadcasted_iota(jnp.int32, tails[0].shape, 1)

        def pick(tail, wanted):
            return jnp.sum(jnp.where(wanted, tail, 0.0), axis=1, keepdims=True)

        means = [pick(tail, lane < SPLIT) for tail in tails]
        squares = [pick(tail, (lane >= SPLIT) & (lane < 2 * SPLIT)) for tail in tails]
        mean = sum(means) * (1.0 / C)
        deviation = sum(squares) + cols * sum((m - mean) * (m - mean) for m in means)
        spread[...] = lax.rsqrt(deviation * (1.0 / features) + 1e-05)
        for k in range(C):
            shift[k, 0] = means[k]
            shift[k, 1] = means[k] - mean
        first = lane - FIRST
        wanted = (first >= 0) & ((first & (E - 1)) == exp) & (first < SPLIT * E)
        scale[...] = sum(pick(tail, wanted) for tail in tails)

    for g in range(groups):
        block_at = step // per_block
        k = block_at ^ ctx

        @pl.when((step < up_steps) & (k // 2 == g))
        def _():
            part = step % per_block
            s = k % 2
            at = pl.ds(pl.multiple_of(part * width, 128), width)
            place_at = pl.multiple_of(block_at * cols + part * width, 128)
            centered = read(g, s, at)
            value = (centered + shift[k, 1]) * spread[...] * gain[:, pl.ds(place_at, width)]
            block = value.astype(BF16)
            own = packed[g][s * chips, ctx, :, at].astype(F32)
            own_mean = shift[k, 0, pl.ds(pl.multiple_of(ctx * token_rows, token_rows), token_rows)]
            hidden[:, pl.ds(place_at, width)] = own + own_mean
            turned_dot = functools.partial(
                lax.dot_general,
                dimension_numbers=(((1,), (1,)), ((), ())),
                preferred_element_type=F32,
            )

            @pl.when(step == 0)
            def _():
                gate_sum[...] = turned_dot(block, gate_slots[step % ahead])
                up_sum[...] = turned_dot(block, up_slots[step % ahead])

            @pl.when(step > 0)
            def _():
                gate_sum[...] += turned_dot(block, gate_slots[step % ahead])
                up_sum[...] += turned_dot(block, up_slots[step % ahead])

    @pl.when(step + ahead < up_steps)
    def _():
        for copy in up_copies(step + ahead, step % ahead):
            copy.start()

    first = step + ahead - up_steps

    @pl.when((first >= 0) & (first < down_ahead))
    def _():
        down_copy(first, first).start()

    @pl.when(step == up_steps)
    def _():
        value = gate_sum[...]
        value = value / (1.0 + jnp.exp(-value)) * up_sum[...]
        activated[...] = value.astype(BF16)

    @pl.when(step >= up_steps)
    def _():
        done = step - up_steps
        block = down_slots[done % down_ahead]
        piece[...] = jnp.dot(activated[...], block, preferred_element_type=F32) * scale[...]

        @pl.when(done + down_ahead < down_steps)
        def _():
            down_copy(done + down_ahead, done % down_ahead).start()

        for g in range(groups):
            for side in range(2):
                for s in range(2):
                    for p in range(chips):
                        row = ((side * chips + p) * C + (ctx ^ (2 * g + s))) * token_rows
                        at = pl.ds(pl.multiple_of(row, token_rows), token_rows)
                        outs[side * groups + g][s * chips + p] = piece[at, :].astype(BF16)


def largest_part(size, most, unit):
    return max(c for c in range(unit, most + 1, unit) if size % c == 0)


def run_experts(packed, gain, gate_weight, up_weight, down_weight, C, E):
    count = len(packed)
    pieces, _, token_rows, wide = packed[0].shape
    cols = wide - EXTRA
    features = cols * C
    units = gate_weight.shape[2]
    total = C * E * token_rows
    small = total <= 256
    width = largest_part(cols, 768 if small else 384, 128)
    columns = largest_part(features, 1024 if small else 384, 128)
    per_block = cols // width
    up_steps = C * per_block
    down_steps = features // columns

    def column_block(i):
        return (0, 0, jnp.maximum(i - up_steps, 0))

    def whole(*dims):
        return pl.BlockSpec(dims, lambda i: (0,) * len(dims), pipeline_mode=pl.Buffered(1))

    ahead = 4 if small else 2
    down_ahead = 3 if small else 2
    *outs, hidden = pl.pallas_call(
        functools.partial(expert_kernel, C, E, per_block, width, columns),
        out_shape=[shape((pieces, token_rows, features), BF16) for _ in packed]
        + [shape((token_rows, features), F32)],
        grid=(up_steps + down_steps,),
        in_specs=[whole(*packed[0].shape) for _ in packed]
        + [whole(1, features), IN_HBM, IN_HBM, IN_HBM],
        out_specs=[pl.BlockSpec((pieces, token_rows, columns), column_block) for _ in packed]
        + [pl.BlockSpec((token_rows, features), lambda i: (0, 0))],
        scratch_shapes=[
            pltpu.VMEM((total, units), F32),
            pltpu.VMEM((total, units), F32),
            pltpu.VMEM((total, units), BF16),
            pltpu.VMEM((total, columns), F32),
            pltpu.VMEM((C, 2, total, 1), F32),
            pltpu.VMEM((total, 1), F32),
            pltpu.VMEM((total, 1), F32),
            pltpu.VMEM((ahead, units, width), BF16),
            pltpu.VMEM((ahead, units, width), BF16),
            pltpu.VMEM((down_ahead, units, columns), BF16),
            pltpu.SemaphoreType.DMA((2, ahead)),
            pltpu.SemaphoreType.DMA((down_ahead,)),
        ],
        compiler_params=pltpu.CompilerParams(
            vmem_limit_bytes=(42 if small else 58) * MIB,
            dimension_semantics=("arbitrary",),
        ),
        cost_estimate=pl.CostEstimate(
            flops=6 * total * features * units,
            bytes_accessed=6 * features * units + 4 * total * features,
            transcendentals=total * units,
        ),
    )(
        *packed,
        gain,
        jnp.swapaxes(gate_weight, 1, 2),
        jnp.swapaxes(up_weight, 1, 2),
        down_weight,
    )
    return outs, hidden


def fold_kernel(plan, *refs):
    ins, outs = refs[: -len(plan)], refs[-len(plan) :]
    for out, places in zip(outs, plan):
        for i, parts in enumerate(places):
            out[i] = sum(ins[at][place].astype(F32) for at, place in parts).astype(BF16)


def fold(plan, operands):
    tail = operands[0].shape[1:]
    return call(
        functools.partial(fold_kernel, plan),
        [shape((len(places), *tail), BF16) for places in plan],
        operands,
        [WHOLE] * len(operands),
    )


def sum_over_plane(own, received, orders):
    chips = own.shape[0] // 2
    operands = [own, received]
    holds = [
        {p: [(0, s * chips + p), (1, s * chips + p)] for p in range(chips)}
        for s in range(len(orders))
    ]
    for step in range(len(orders[0])):
        far = [1 << (order[step] - 1) for order in orders]
        sent = [[p for p in sorted(hold) if p & f] for hold, f in zip(holds, far)]
        kept = [[p for p in sorted(hold) if not p & f] for hold, f in zip(holds, far)]
        plan = [[hold[p] for p in ps] for hold, ps in zip(holds * 2, sent + kept)]
        *sends, keep0, keep1 = fold(plan, operands)
        got = [swap(value, "exp", 1 << order[step]) for value, order in zip(sends, orders)]
        operands = [keep0, got[0], keep1, got[1]]
        holds = [
            {p: [(2 * s, i), (2 * s + 1, i)] for i, p in enumerate(kept[s])}
            for s in range(len(orders))
        ]
    return fold([[hold[0]] for hold in holds], operands)


def on_device(
    queries,
    keys_values,
    residual,
    out_weight,
    norm_gain,
    routes,
    route_weight,
    gate_weight,
    up_weight,
    down_weight,
):
    C = lax.axis_size("ctx")
    E = lax.axis_size("exp")
    chips = E // 2
    chip_bits = list(range(1, E.bit_length() - 1))
    heads = queries.shape[1] // HD
    seq = queries.shape[0] * C
    token_rows, features = residual.shape
    cols = out_weight.shape[1]
    wide = queries.shape[1] + HD
    slots = E + -(-cols // wide)
    sent = call(
        functools.partial(message_kernel, C, E),
        [shape((slots, token_rows, wide), BF16)] * C,
        [queries, keys_values, residual],
        [IN_HBM] * 3,
        [
            pltpu.VMEM(queries.shape, BF16),
            pltpu.VMEM(keys_values.shape, BF16),
            pltpu.VMEM(residual.shape, BF16),
            pltpu.SemaphoreType.DMA((3,)),
        ],
        limit=60,
    )
    messages = [swap(piece, "ctx", k) if k else piece for k, piece in enumerate(sent)]
    weight, gain = call(
        keep_kernel,
        [shape(out_weight.shape, BF16), shape((1, features), F32)],
        [sent[0], out_weight, norm_gain.reshape(1, -1)],
        [WHOLE] * 3,
    )
    (halves,) = call(
        functools.partial(halves_kernel, C, E),
        [shape((C, E, token_rows, HD), BF16)],
        [*messages, weight, gain],
        [WHOLE] * (C + 2),
    )

    experts = jnp.arange(E, dtype=jnp.int32)
    left = jnp.sum(jnp.where(routes[:, :, None] == experts, route_weight[:, :, None], 0.0), axis=1)
    terms = []
    for _ in range(SPLIT):
        term = lax.reduce_precision(left, 8, 7)
        terms.append(term.astype(BF16))
        left = left - term
    extra = jnp.pad(
        jnp.concatenate(terms, axis=1), ((0, 0), (FIRST, EXTRA - FIRST - SPLIT * E))
    )

    mate_part, own_part = call(
        functools.partial(attend_kernel, C, E, heads),
        [
            shape((chips, C, token_rows, cols), BF16),
            shape((chips, C, token_rows, cols), F32),
        ],
        [*messages, swap(halves, "exp", 1), weight],
        [WHOLE] * (C + 2),
        [pltpu.VMEM((seq, cols), F32)],
        limit=16 if seq <= 256 else 56,
    )

    kept, *sent = call(
        mate_sum_kernel,
        [shape((C, token_rows, cols), F32)] + [shape((C, token_rows, cols), BF16)] * (chips - 1),
        [own_part, swap(mate_part, "exp", 1)],
        [WHOLE, WHOLE],
    )
    received = [swap(piece, "exp", (p + 1) << 1) for p, piece in enumerate(sent)]
    (rows,) = call(
        functools.partial(plane_sum_kernel, C, E, chips - 1),
        [shape((C, token_rows, cols + EXTRA), BF16)],
        [kept, *received, *messages, extra],
        [WHOLE] * (chips + C + 1),
    )

    orders = (chip_bits[::-1], chip_bits)
    near = [rows, swap(rows, "ctx", 1)]
    (pair,) = pack([[(0, None), (1, None)]], near, rows.shape)
    pairs = [pair]
    for bit in range(1, C.bit_length() - 1):
        pairs += [swap(value, "ctx", 1 << bit) for value in pairs]
    group, sends = spread_over_plane(near, [(0, None), (1, None)], orders, chips, [])
    packed = [group]
    for value in pairs[1:]:
        group, sends = spread_over_plane([value], [(0, 0), (0, 1)], orders, chips, sends)
        packed.append(group)
    packed += [swap(group, "exp", 1) for group in packed]

    outs, hidden = run_experts(packed, gain, gate_weight, up_weight, down_weight, C, E)

    count = C // 2
    shards = [None] * C
    for g in reversed(range(count)):
        received = swap(outs[count + g], "exp", 1)
        shards[2 * g : 2 * g + 2] = sum_over_plane(outs[g], received, orders[::-1])
    total = hidden
    for k, shard in enumerate(shards):
        total = total + (swap(shard, "ctx", k) if k else shard)[0].astype(F32)
    return total.astype(BF16)


def solution(mesh):
    in_specs = (
        P("ctx", "exp"),
        P(None, "ctx", "exp"),
        P(("ctx", "exp"), None),
        P("exp", "ctx"),
        P(),
        P(("ctx", "exp"), None),
        P(("ctx", "exp"), None),
        P("exp", None, "ctx"),
        P("exp", None, "ctx"),
        P("exp", "ctx", None),
    )
    out_specs = P(("ctx", "exp"), None)
    return jax.shard_map(
        on_device, mesh=mesh, in_specs=in_specs, out_specs=out_specs, check_vma=False
    )
```

```python
import functools
import math

import jax
import jax.numpy as jnp
from jax import lax
from jax.experimental import pallas as pl
from jax.experimental.pallas import tpu as pltpu
from jax.sharding import PartitionSpec as P

HD = 128
EXTRA = 128
SPLIT = 3
FIRST = 8
MIB = 1024 * 1024
F32 = jnp.float32
BF16 = jnp.bfloat16
WHOLE = pl.BlockSpec(memory_space=pltpu.VMEM)
IN_HBM = pl.BlockSpec(memory_space=pltpu.HBM)


def swap(value, axis, mask):
    return lax.ppermute(value, axis, [(i, i ^ mask) for i in range(lax.axis_size(axis))])


def call(kernel, out_shape, operands, in_specs, scratch=(), limit=16):
    return pl.pallas_call(
        kernel,
        out_shape=out_shape,
        in_specs=in_specs,
        out_specs=jax.tree.map(lambda _: WHOLE, out_shape),
        scratch_shapes=list(scratch),
        compiler_params=pltpu.CompilerParams(vmem_limit_bytes=limit * MIB),
    )(*operands)


def shape(dims, dtype):
    return jax.ShapeDtypeStruct(tuple(dims), dtype)


def attend_kernel(C, E, heads, *refs):
    messages, mates, out_weight, mate_out, own_out, projected = refs[:C], *refs[C:]
    ctx, exp = lax.axis_index("ctx"), lax.axis_index("exp")
    token_rows = mate_out.shape[2]
    rows = E * token_rows
    seq = rows * C
    blocks = [
        m[:E].astype(F32).reshape(rows, m.shape[2]).astype(BF16) for m in messages
    ]
    width = heads * HD
    half = HD // 2
    lower = (exp & 1) == 0

    other_half = mates[...].astype(F32).reshape(seq, HD).astype(BF16)

    def joined(start):
        first = width + start
        own = jnp.concatenate([b[:, first : first + half] for b in blocks], axis=0)
        mate = other_half[:, start : start + half]
        both = jnp.concatenate([own, mate], axis=1)
        other = jnp.concatenate([mate, own], axis=1)
        return jnp.where(lower, both, other)

    keys = joined(0)
    values = joined(half)
    shift = rows.bit_length() - 1
    column = lax.broadcasted_iota(jnp.int32, (rows, seq), 1)
    key_position = ((column >> shift) ^ ctx) * rows + (column & (rows - 1))
    row = lax.broadcasted_iota(jnp.int32, (rows, seq), 0)
    parts = []
    for k in range(C):
        allowed = key_position <= (ctx ^ k) * rows + row
        block_parts = []
        for h in range(heads):
            q = blocks[k][:, h * HD : (h + 1) * HD]
            scores = lax.dot_general(
                q, keys, (((1,), (1,)), ((), ())), preferred_element_type=F32
            ) * (1.0 / math.sqrt(HD))
            scores = jnp.where(allowed, scores, -jnp.inf)
            top = jnp.max(scores, axis=1, keepdims=True)
            weights = jnp.exp(scores - top)
            total = jnp.sum(weights, axis=1, keepdims=True)
            high = weights.astype(BF16)
            low = (weights - high.astype(F32)).astype(BF16)
            summed = jnp.dot(high, values, preferred_element_type=F32) + jnp.dot(
                low, values, preferred_element_type=F32
            )
            block_parts.append((summed / total).astype(BF16))
        parts.append(jnp.concatenate(block_parts, axis=1))
    attended = jnp.concatenate(parts, axis=0)
    projected[...] = jnp.dot(attended, out_weight[...], preferred_element_type=F32)
    for p in range(E):
        for j in range(C):
            start = pl.multiple_of(((ctx ^ j) * E + (exp ^ p)) * token_rows, token_rows)
            piece = projected[pl.ds(start, token_rows), :]
            if p & 1:
                mate_out[p >> 1, j] = piece.astype(BF16)
            else:
                own_out[p >> 1, j] = piece


def mate_sum_kernel(own, received, kept, *sent):
    kept[...] = own[0] + received[0].astype(F32)
    for p, out in enumerate(sent):
        out[...] = (own[p + 1] + received[p + 1].astype(F32)).astype(BF16)


def message_kernel(C, E, queries_in, own_in, residual_in, *refs):
    messages = refs[:C]
    queries, own, residual, sems = refs[C:]
    pairs = [(queries_in, queries), (own_in, own), (residual_in, residual)]
    loads = [pltpu.make_async_copy(a, b, sems.at[i]) for i, (a, b) in enumerate(pairs)]
    for load in loads:
        load.start()
    for load in loads:
        load.wait()
    token_rows, wide = messages[0].shape[1:]
    cols = residual.shape[1] // C
    parts = [queries[...], own[0], own[1]]
    bundle = jnp.concatenate([part.astype(F32) for part in parts], axis=1)
    bundle = bundle.reshape(E, token_rows, wide).astype(BF16)
    ctx = lax.axis_index("ctx")
    for k, out in enumerate(messages):
        out[:E] = bundle
        first = (ctx ^ k) * cols
        for i in range(out.shape[0] - E):
            width = min(wide, cols - i * wide)
            at = pl.ds(pl.multiple_of(first + i * wide, 128), width)
            out[E + i, :, :width] = residual[:, at]


def keep_kernel(after, out_weight, gain, weight_out, gain_out):
    weight_out[...] = out_weight[...]
    gain_out[...] = gain[...]


def halves_kernel(C, E, *refs):
    halves, residual = refs[-2:]
    for k in range(C):
        halves[k] = refs[k][:E, :, refs[k].shape[2] - HD :]
    residual[...] = refs[0][E:]


def split_terms(value):
    terms = []
    for _ in range(SPLIT):
        term = value.astype(BF16).astype(F32)
        terms.append(term)
        value = value - term
    return terms


def plane_sum_kernel(C, E, count, *refs):
    own, received, messages = refs[0], refs[1 : 1 + count], refs[1 + count : 1 + count + C]
    extra, out = refs[1 + count + C :]
    cols = own.shape[2]
    wide = messages[0].shape[2]
    lane = lax.broadcasted_iota(jnp.int32, (own.shape[1], EXTRA), 1)
    for k in range(C):
        j = lax.axis_index("ctx") ^ k
        start = E if k else 0
        pieces = [
            messages[k][start + i, :, : min(wide, cols - i * wide)].astype(F32)
            for i in range(messages[k].shape[0] - start)
        ]
        total = own[j] + jnp.concatenate(pieces, axis=1)
        for piece in received:
            total = total + piece[j].astype(F32)
        mean = jnp.sum(total, axis=1, keepdims=True) * (1.0 / cols)
        centered = total - mean
        squares = jnp.sum(centered * centered, axis=1, keepdims=True)
        out[j, :, :cols] = centered.astype(BF16)
        tail = jnp.zeros(lane.shape, F32) if k else extra[...].astype(F32)
        for i, term in enumerate(split_terms(mean) + split_terms(squares)):
            tail = jnp.where(lane == i, term, tail)
        out[j, :, cols:] = tail.astype(BF16)


def pack_kernel(plan, *refs):
    ins, outs = refs[: -len(plan)], refs[-len(plan) :]
    for out, sources in zip(outs, plan):
        for i, (at, place) in enumerate(sources):
            value = ins[at][...] if place is None else ins[at][place]
            if len(sources) == 1:
                out[...] = value
            else:
                out[i] = value


def pack(plan, arrays, tail, after=()):
    return call(
        functools.partial(pack_kernel, plan),
        [shape(tail if len(p) == 1 else (len(p), *tail), BF16) for p in plan],
        [*arrays, *after],
        [WHOLE] * (len(arrays) + len(after)),
    )


def spread_over_plane(arrays, sources, orders, chips, afters, last=lambda sends: []):
    tail = arrays[0].shape[-3:]
    holds = [{0: source} for source in sources]
    arrays = list(arrays)
    for step in range(len(orders[0])):
        plan = [[hold[p] for p in sorted(hold)] for hold in holds]
        if step == 0 and len(arrays) == 2:
            sends = arrays[:]
        else:
            sends = pack(plan, arrays, tail, afters[step])
        for hold, order, send in zip(holds, orders, sends):
            at = len(arrays)
            arrays.append(swap(send, "exp", 1 << order[step]))
            far = 1 << (order[step] - 1)
            for i, p in enumerate(sorted(hold)):
                hold[p | far] = (at, None if step == 0 else i)
    plan = [[hold[p] for hold in holds for p in range(chips)]]
    (packed,) = pack(plan, arrays, tail, last(sends))
    return packed, sends


def load_kernel(blocks, *refs):
    token, sems = refs[-2:]
    outs = refs[-2 - len(blocks) : -2]
    copies = []
    for i, (out, (which, j)) in enumerate(zip(outs, blocks)):
        cols = out.shape[1]
        source = refs[which].at[0, :, j * cols : (j + 1) * cols]
        copies.append(pltpu.make_async_copy(source, out, sems.at[i]))
    for copy in copies:
        copy.start()
    for copy in copies:
        copy.wait()
    token[...] = jnp.zeros_like(token)


def load_blocks(weights, blocks, cols, after, limit):
    units = weights[0].shape[1]
    *loaded, token = pl.pallas_call(
        functools.partial(load_kernel, blocks),
        out_shape=[shape((units, cols), BF16) for _ in blocks] + [shape((8, 128), F32)],
        in_specs=[IN_HBM, IN_HBM, WHOLE],
        out_specs=[WHOLE] * (len(blocks) + 1),
        scratch_shapes=[pltpu.SemaphoreType.DMA((len(blocks),))],
        compiler_params=pltpu.CompilerParams(vmem_limit_bytes=limit * MIB),
        cost_estimate=pl.CostEstimate(
            flops=0, bytes_accessed=4 * units * cols * len(blocks), transcendentals=0
        ),
    )(*weights, after)
    return loaded, token


def expert_kernel(C, E, per_block, width, columns, held, *refs):
    groups = C // 2
    packed, refs = refs[: 2 * groups], refs[2 * groups :]
    gate_held, up_held, refs = refs[:held], refs[held : 2 * held], refs[2 * held :]
    gain, gate, up, down = refs[:4]
    outs, hidden, refs = refs[4 : 2 * groups + 4], refs[2 * groups + 4], refs[2 * groups + 5 :]
    gate_sum, up_sum, activated, piece, block, shift, spread, scale = refs[:8]
    gate_slots, up_slots, down_slots, up_sems, down_sems = refs[8:]
    ctx, exp = lax.axis_index("ctx"), lax.axis_index("exp")
    chips = E // 2
    token_rows = packed[0].shape[2]
    cols = packed[0].shape[3] - EXTRA
    half_rows = chips * C * token_rows
    features = hidden.shape[1]
    up_steps = C * per_block
    first = held * per_block
    down_steps = features // columns
    ahead, down_ahead = gate_slots.shape[0], down_slots.shape[0]

    def up_copies(i, slot):
        at = pl.ds(pl.multiple_of(i * width, 128), width)
        return [
            pltpu.make_async_copy(gate.at[0, :, at], gate_slots.at[slot], up_sems.at[0, slot]),
            pltpu.make_async_copy(up.at[0, :, at], up_slots.at[slot], up_sems.at[1, slot]),
        ]

    def down_copy(i, slot):
        at = pl.ds(pl.multiple_of(i * columns, 128), columns)
        return pltpu.make_async_copy(down.at[0, :, at], down_slots.at[slot], down_sems.at[slot])

    for i in range(ahead):
        for copy in up_copies(first + i, i):
            copy.start()

    def read(g, s, at):
        parts = [
            packed[side * groups + g][pl.ds(s * chips, chips), :, :, at] for side in range(2)
        ]
        parts = [part.astype(F32).reshape(half_rows, part.shape[-1]) for part in parts]
        return jnp.concatenate(parts, axis=0)

    tails = [read(k % groups, k // groups, slice(cols, cols + EXTRA)) for k in range(C)]
    lane = lax.broadcasted_iota(jnp.int32, tails[0].shape, 1)

    def pick(tail, wanted):
        return jnp.sum(jnp.where(wanted, tail, 0.0), axis=1, keepdims=True)

    means = [pick(tail, lane < SPLIT) for tail in tails]
    squares = [pick(tail, (lane >= SPLIT) & (lane < 2 * SPLIT)) for tail in tails]
    mean = sum(means) * (1.0 / C)
    deviation = sum(squares) + cols * sum((m - mean) * (m - mean) for m in means)
    spread[...] = lax.rsqrt(deviation * (1.0 / features) + 1e-05)
    for k in range(C):
        shift[k, 0] = means[k]
        shift[k, 1] = means[k] - mean
    term = lane - FIRST
    wanted = (term >= 0) & ((term & (E - 1)) == exp) & (term < SPLIT * E)
    scale[...] = sum(pick(tail, wanted) for tail in tails)

    def normalise(j, part):
        k = j ^ ctx
        at = pl.ds(pl.multiple_of(part * width, 128), width)
        place = pl.multiple_of(j * cols + part * width, 128)
        for g in range(groups):

            @pl.when(k % groups == g)
            def _():
                s = k // groups
                value = (read(g, s, at) + shift[k, 1]) * spread[...]
                block[...] = (value * gain[:, pl.ds(place, width)]).astype(BF16)
                own = packed[g][s * chips, ctx, :, at].astype(F32)
                rows = pl.ds(pl.multiple_of(ctx * token_rows, token_rows), token_rows)
                hidden[:, pl.ds(place, width)] = own + shift[k, 0, rows]

    turned_dot = functools.partial(
        lax.dot_general,
        dimension_numbers=(((1,), (1,)), ((), ())),
        preferred_element_type=F32,
    )
    if held == 0:
        gate_sum[...] = jnp.zeros_like(gate_sum)
        up_sum[...] = jnp.zeros_like(up_sum)
        for i in range(down_ahead):
            down_copy(i, i).start()
    for i in range(first):
        j, part = i // per_block, i % per_block
        normalise(j, part)
        at = slice(part * width, (part + 1) * width)
        gate_part = turned_dot(block[...], gate_held[j][:, at])
        gate_sum[...] = gate_part if i == 0 else gate_sum[...] + gate_part
        up_part = turned_dot(block[...], up_held[j][:, at])
        up_sum[...] = up_part if i == 0 else up_sum[...] + up_part
        if i == first // 2:
            for d in range(down_ahead):
                down_copy(d, d).start()

    @pl.loop(first, up_steps)
    def _(i):
        slot = (i - first) % ahead
        normalise(i // per_block, i % per_block)
        for copy in up_copies(i, slot):
            copy.wait()
        gate_sum[...] += turned_dot(block[...], gate_slots[slot])
        up_sum[...] += turned_dot(block[...], up_slots[slot])

        @pl.when(i + ahead < up_steps)
        def _():
            for copy in up_copies(i + ahead, slot):
                copy.start()

    value = gate_sum[...]
    value = value / (1.0 + jnp.exp(-value)) * up_sum[...]
    activated[...] = value.astype(BF16)

    @pl.loop(0, down_steps)
    def _(i):
        slot = i % down_ahead
        down_copy(i, slot).wait()
        value = jnp.dot(activated[...], down_slots[slot], preferred_element_type=F32)
        piece[...] = value * scale[...]

        @pl.when(i + down_ahead < down_steps)
        def _():
            down_copy(i + down_ahead, slot).start()

        place = pl.ds(pl.multiple_of(i * columns, 128), columns)
        for g in range(groups):
            for side in range(2):
                for s in range(2):
                    for p in range(chips):
                        k = s * groups + g
                        row = ((side * chips + p) * C + (ctx ^ k)) * token_rows
                        at = pl.ds(pl.multiple_of(row, token_rows), token_rows)
                        out = outs[side * groups + g]
                        out[s * chips + p, :, place] = piece[at, :].astype(BF16)


def largest_part(size, most, unit):
    return max(c for c in range(unit, most + 1, unit) if size % c == 0)


def run_experts(packed, gate_held, up_held, gain, weights, down_weight, C, E):
    count = len(packed)
    pieces, _, token_rows, wide = packed[0].shape
    cols = wide - EXTRA
    features = cols * C
    units = weights[0].shape[1]
    total = C * E * token_rows
    held = len(gate_held)
    width = largest_part(cols, 768 if held else 384, 128)
    columns = largest_part(features, 768 if held else 384, 128)
    per_block = cols // width
    ahead = 3 if held else 2
    down_ahead = 3 if held else 2
    operands = [*packed, *gate_held, *up_held, gain]
    *outs, hidden = pl.pallas_call(
        functools.partial(expert_kernel, C, E, per_block, width, columns, held),
        out_shape=[shape((pieces, token_rows, features), BF16) for _ in packed]
        + [shape((token_rows, features), F32)],
        in_specs=[WHOLE] * len(operands) + [IN_HBM] * 3,
        out_specs=[WHOLE] * (count + 1),
        scratch_shapes=[
            pltpu.VMEM((total, units), F32),
            pltpu.VMEM((total, units), F32),
            pltpu.VMEM((total, units), BF16),
            pltpu.VMEM((total, columns), F32),
            pltpu.VMEM((total, width), BF16),
            pltpu.VMEM((C, 2, total, 1), F32),
            pltpu.VMEM((total, 1), F32),
            pltpu.VMEM((total, 1), F32),
            pltpu.VMEM((ahead, units, width), BF16),
            pltpu.VMEM((ahead, units, width), BF16),
            pltpu.VMEM((down_ahead, units, columns), BF16),
            pltpu.SemaphoreType.DMA((2, ahead)),
            pltpu.SemaphoreType.DMA((down_ahead,)),
        ],
        compiler_params=pltpu.CompilerParams(vmem_limit_bytes=(35 if held else 58) * MIB),
        cost_estimate=pl.CostEstimate(
            flops=6 * total * features * units,
            bytes_accessed=6 * features * units + 4 * total * features,
            transcendentals=total * units,
        ),
    )(*operands, *weights, down_weight)
    return outs, hidden


def fold_kernel(plan, *refs):
    ins, outs = refs[: -len(plan)], refs[-len(plan) :]
    for out, places in zip(outs, plan):
        for i, parts in enumerate(places):
            out[i] = sum(ins[at][place].astype(F32) for at, place in parts).astype(BF16)


def fold(plan, operands):
    tail = operands[0].shape[1:]
    return call(
        functools.partial(fold_kernel, plan),
        [shape((len(places), *tail), BF16) for places in plan],
        operands,
        [WHOLE] * len(operands),
    )


def sum_over_plane(own, received, orders, added, apart):
    chips = own.shape[0] // 2
    operands = [own, received]
    holds = [
        {p: [(0, s * chips + p), (1, s * chips + p)] for p in range(chips)}
        for s in range(len(orders))
    ]
    for step in range(len(orders[0])):
        far = [1 << (order[step] - 1) for order in orders]
        sent = [[p for p in sorted(hold) if p & f] for hold, f in zip(holds, far)]
        kept = [[p for p in sorted(hold) if not p & f] for hold, f in zip(holds, far)]
        plan = [[hold[p] for p in ps] for hold, ps in zip(holds * 2, sent + kept)]
        *sends, keep0, keep1 = fold(plan, operands)
        got = [swap(value, "exp", 1 << order[step]) for value, order in zip(sends, orders)]
        operands = [keep0, got[0], keep1, got[1]]
        holds = [
            {p: [(2 * s, i), (2 * s + 1, i)] for i, p in enumerate(kept[s])}
            for s in range(len(orders))
        ]
    parts = [hold[0] + [(4 + i, s) for i in range(len(added))] for s, hold in enumerate(holds)]
    return fold([[part] for part in parts] if apart else [parts], operands + added)


def on_device(
    queries,
    keys_values,
    residual,
    out_weight,
    norm_gain,
    routes,
    route_weight,
    gate_weight,
    up_weight,
    down_weight,
):
    C = lax.axis_size("ctx")
    E = lax.axis_size("exp")
    chips = E // 2
    chip_bits = list(range(1, E.bit_length() - 1))
    heads = queries.shape[1] // HD
    seq = queries.shape[0] * C
    token_rows, features = residual.shape
    cols = out_weight.shape[1]
    wide = queries.shape[1] + HD
    slots = E + -(-cols // wide)
    sent = call(
        functools.partial(message_kernel, C, E),
        [shape((slots, token_rows, wide), BF16)] * C,
        [queries, keys_values, residual],
        [IN_HBM] * 3,
        [
            pltpu.VMEM(queries.shape, BF16),
            pltpu.VMEM(keys_values.shape, BF16),
            pltpu.VMEM(residual.shape, BF16),
            pltpu.SemaphoreType.DMA((3,)),
        ],
        limit=60,
    )
    messages = [swap(piece, "ctx", k) if k else piece for k, piece in enumerate(sent)]
    weight, gain = call(
        keep_kernel,
        [shape(out_weight.shape, BF16), shape((1, features), F32)],
        [sent[0], out_weight, norm_gain.reshape(1, -1)],
        [WHOLE] * 3,
    )
    halves, own_residual = call(
        functools.partial(halves_kernel, C, E),
        [
            shape((C, E, token_rows, HD), BF16),
            shape((slots - E, token_rows, wide), BF16),
        ],
        [*messages, weight, gain],
        [WHOLE] * (C + 2),
    )

    experts = jnp.arange(E, dtype=jnp.int32)
    left = jnp.sum(jnp.where(routes[:, :, None] == experts, route_weight[:, :, None], 0.0), axis=1)
    terms = []
    for _ in range(SPLIT):
        term = lax.reduce_precision(left, 8, 7)
        terms.append(term.astype(BF16))
        left = left - term
    extra = jnp.pad(
        jnp.concatenate(terms, axis=1), ((0, 0), (FIRST, EXTRA - FIRST - SPLIT * E))
    )

    mate_part, own_part = call(
        functools.partial(attend_kernel, C, E, heads),
        [
            shape((chips, C, token_rows, cols), BF16),
            shape((chips, C, token_rows, cols), F32),
        ],
        [*messages, swap(halves, "exp", 1), weight],
        [WHOLE] * (C + 2),
        [pltpu.VMEM((seq, cols), F32)],
        limit=16 if seq <= 256 else 56,
    )

    kept, *sent = call(
        mate_sum_kernel,
        [shape((C, token_rows, cols), F32)] + [shape((C, token_rows, cols), BF16)] * (chips - 1),
        [own_part, swap(mate_part, "exp", 1)],
        [WHOLE, WHOLE],
    )
    received = [swap(piece, "exp", (p + 1) << 1) for p, piece in enumerate(sent)]
    (rows,) = call(
        functools.partial(plane_sum_kernel, C, E, chips - 1),
        [shape((C, token_rows, cols + EXTRA), BF16)],
        [kept, *received, own_residual, *messages[1:], extra],
        [WHOLE] * (chips + C + 1),
    )

    weights = [jnp.swapaxes(gate_weight, 1, 2), jnp.swapaxes(up_weight, 1, 2)]
    hold = C * E * token_rows <= 256 and C == 4 and len(chip_bits) == 2
    loaded = []

    def load(which, after):
        if not hold:
            return []
        blocks, token = load_blocks(weights, [(which, 0)], cols, after, 44)
        loaded.extend(blocks)
        return [token]

    orders = (chip_bits[::-1], chip_bits)
    near = [rows, swap(rows, "ctx", C // 2)]
    (pair,) = pack([[(0, None), (1, None)]], near, rows.shape)
    pairs = [pair]
    for bit in range(C.bit_length() - 2):
        pairs += [swap(value, "ctx", 1 << bit) for value in pairs]
    afters = [[]] * len(chip_bits)
    group, sends = spread_over_plane(near, [(0, None), (1, None)], orders, chips, afters)
    packed = [group]
    token = load(0, sends[0])
    for value in pairs[1:]:
        afters = [sends] + [token] * (len(chip_bits) - 1)
        last = (lambda sent: load(1, sent[0])) if hold else (lambda sent: [])
        group, sends = spread_over_plane(
            [value], [(0, 0), (0, 1)], orders, chips, afters, last
        )
        packed.append(group)
    packed += [swap(group, "exp", 1) for group in packed]

    outs, hidden = run_experts(
        packed, loaded[0::2], loaded[1::2], gain, weights, down_weight, C, E
    )

    count = C // 2
    added = [[] for _ in range(count)]
    for g in reversed(range(count)):
        received = swap(outs[count + g], "exp", 1)
        values = sum_over_plane(outs[g], received, orders[::-1], added[g], g == 0)
        if g:
            top = 1 << (g.bit_length() - 1)
            added[g ^ top].append(swap(values[0], "ctx", top))
    kept, sent = values
    total = hidden + kept[0].astype(F32) + swap(sent, "ctx", C // 2)[0].astype(F32)
    return total.astype(BF16)


def solution(mesh):
    in_specs = (
        P("ctx", "exp"),
        P(None, "ctx", "exp"),
        P(("ctx", "exp"), None),
        P("exp", "ctx"),
        P(),
        P(("ctx", "exp"), None),
        P(("ctx", "exp"), None),
        P("exp", None, "ctx"),
        P("exp", None, "ctx"),
        P("exp", "ctx", None),
    )
    out_specs = P(("ctx", "exp"), None)
    return jax.shard_map(
        on_device, mesh=mesh, in_specs=in_specs, out_specs=out_specs, check_vma=False
    )
```

```python
import functools
import math

import jax
import jax.numpy as jnp
from jax import lax
from jax.experimental import pallas as pl
from jax.experimental.pallas import tpu as pltpu
from jax.sharding import PartitionSpec as P

HD = 128
EXTRA = 128
SPLIT = 3
FIRST = 8
MIB = 1024 * 1024
F32 = jnp.float32
BF16 = jnp.bfloat16
WHOLE = pl.BlockSpec(memory_space=pltpu.VMEM)
IN_HBM = pl.BlockSpec(memory_space=pltpu.HBM)


def swap(value, axis, mask):
    return lax.ppermute(value, axis, [(i, i ^ mask) for i in range(lax.axis_size(axis))])


def call(kernel, out_shape, operands, in_specs, scratch=(), limit=16):
    return pl.pallas_call(
        kernel,
        out_shape=out_shape,
        in_specs=in_specs,
        out_specs=jax.tree.map(lambda _: WHOLE, out_shape),
        scratch_shapes=list(scratch),
        compiler_params=pltpu.CompilerParams(vmem_limit_bytes=limit * MIB),
    )(*operands)


def shape(dims, dtype):
    return jax.ShapeDtypeStruct(tuple(dims), dtype)


def attend_kernel(C, E, heads, *refs):
    messages, mates, out_weight, mate_out, own_out, projected = refs[:C], *refs[C:]
    ctx, exp = lax.axis_index("ctx"), lax.axis_index("exp")
    token_rows = mate_out.shape[2]
    rows = E * token_rows
    seq = rows * C
    blocks = [
        m[:E].astype(F32).reshape(rows, m.shape[2]).astype(BF16) for m in messages
    ]
    width = heads * HD
    half = HD // 2
    lower = (exp & 1) == 0

    other_half = mates[...].astype(F32).reshape(seq, HD).astype(BF16)

    def joined(start):
        first = width + start
        own = jnp.concatenate([b[:, first : first + half] for b in blocks], axis=0)
        mate = other_half[:, start : start + half]
        both = jnp.concatenate([own, mate], axis=1)
        other = jnp.concatenate([mate, own], axis=1)
        return jnp.where(lower, both, other)

    keys = joined(0)
    values = joined(half)
    shift = rows.bit_length() - 1
    column = lax.broadcasted_iota(jnp.int32, (rows, seq), 1)
    key_position = ((column >> shift) ^ ctx) * rows + (column & (rows - 1))
    row = lax.broadcasted_iota(jnp.int32, (rows, seq), 0)
    parts = []
    for k in range(C):
        allowed = key_position <= (ctx ^ k) * rows + row
        block_parts = []
        for h in range(heads):
            q = blocks[k][:, h * HD : (h + 1) * HD]
            scores = lax.dot_general(
                q, keys, (((1,), (1,)), ((), ())), preferred_element_type=F32
            ) * (1.0 / math.sqrt(HD))
            scores = jnp.where(allowed, scores, -jnp.inf)
            top = jnp.max(scores, axis=1, keepdims=True)
            weights = jnp.exp(scores - top)
            total = jnp.sum(weights, axis=1, keepdims=True)
            high = weights.astype(BF16)
            low = (weights - high.astype(F32)).astype(BF16)
            summed = jnp.dot(high, values, preferred_element_type=F32) + jnp.dot(
                low, values, preferred_element_type=F32
            )
            block_parts.append((summed / total).astype(BF16))
        parts.append(jnp.concatenate(block_parts, axis=1))
    attended = jnp.concatenate(parts, axis=0)
    projected[...] = jnp.dot(attended, out_weight[...], preferred_element_type=F32)
    for p in range(E):
        for j in range(C):
            start = pl.multiple_of(((ctx ^ j) * E + (exp ^ p)) * token_rows, token_rows)
            piece = projected[pl.ds(start, token_rows), :]
            if p & 1:
                mate_out[p >> 1, j] = piece.astype(BF16)
            else:
                own_out[p >> 1, j] = piece


def mate_sum_kernel(own, received, kept, *sent):
    kept[...] = own[0] + received[0].astype(F32)
    for p, out in enumerate(sent):
        out[...] = (own[p + 1] + received[p + 1].astype(F32)).astype(BF16)


def message_kernel(C, E, queries_in, own_in, residual_in, *refs):
    messages = refs[:C]
    queries, own, residual, sems = refs[C:]
    pairs = [(queries_in, queries), (own_in, own), (residual_in, residual)]
    loads = [pltpu.make_async_copy(a, b, sems.at[i]) for i, (a, b) in enumerate(pairs)]
    for load in loads:
        load.start()
    for load in loads:
        load.wait()
    token_rows, wide = messages[0].shape[1:]
    cols = residual.shape[1] // C
    parts = [queries[...], own[0], own[1]]
    bundle = jnp.concatenate([part.astype(F32) for part in parts], axis=1)
    bundle = bundle.reshape(E, token_rows, wide).astype(BF16)
    ctx = lax.axis_index("ctx")
    for k, out in enumerate(messages):
        out[:E] = bundle
        first = (ctx ^ k) * cols
        for i in range(out.shape[0] - E):
            width = min(wide, cols - i * wide)
            at = pl.ds(pl.multiple_of(first + i * wide, 128), width)
            out[E + i, :, :width] = residual[:, at]


def keep_kernel(after, out_weight, gain, weight_out, gain_out):
    weight_out[...] = out_weight[...]
    gain_out[...] = gain[...]


def halves_kernel(C, E, *refs):
    halves, residual = refs[-2:]
    for k in range(C):
        halves[k] = refs[k][:E, :, refs[k].shape[2] - HD :]
    residual[...] = refs[0][E:]


def split_terms(value):
    terms = []
    for _ in range(SPLIT):
        term = value.astype(BF16).astype(F32)
        terms.append(term)
        value = value - term
    return terms


def plane_sum_kernel(C, E, count, *refs):
    own, received, messages = refs[0], refs[1 : 1 + count], refs[1 + count : 1 + count + C]
    extra, out = refs[1 + count + C :]
    cols = own.shape[2]
    wide = messages[0].shape[2]
    lane = lax.broadcasted_iota(jnp.int32, (own.shape[1], EXTRA), 1)
    for k in range(C):
        j = lax.axis_index("ctx") ^ k
        start = E if k else 0
        pieces = [
            messages[k][start + i, :, : min(wide, cols - i * wide)].astype(F32)
            for i in range(messages[k].shape[0] - start)
        ]
        total = own[j] + jnp.concatenate(pieces, axis=1)
        for piece in received:
            total = total + piece[j].astype(F32)
        mean = jnp.sum(total, axis=1, keepdims=True) * (1.0 / cols)
        centered = total - mean
        squares = jnp.sum(centered * centered, axis=1, keepdims=True)
        out[j, :, :cols] = centered.astype(BF16)
        tail = jnp.zeros(lane.shape, F32) if k else extra[...].astype(F32)
        for i, term in enumerate(split_terms(mean) + split_terms(squares)):
            tail = jnp.where(lane == i, term, tail)
        out[j, :, cols:] = tail.astype(BF16)


def pack_kernel(plan, *refs):
    ins, outs = refs[: -len(plan)], refs[-len(plan) :]
    for out, sources in zip(outs, plan):
        for i, (at, place) in enumerate(sources):
            value = ins[at][...] if place is None else ins[at][place]
            if len(sources) == 1:
                out[...] = value
            else:
                out[i] = value


def pack(plan, arrays, tail, after=()):
    return call(
        functools.partial(pack_kernel, plan),
        [shape(tail if len(p) == 1 else (len(p), *tail), BF16) for p in plan],
        [*arrays, *after],
        [WHOLE] * (len(arrays) + len(after)),
    )


def spread_over_plane(arrays, sources, orders, chips, afters, last=lambda sends: []):
    tail = arrays[0].shape[-3:]
    holds = [{0: source} for source in sources]
    arrays = list(arrays)
    for step in range(len(orders[0])):
        plan = [[hold[p] for p in sorted(hold)] for hold in holds]
        if step == 0 and len(arrays) == 2:
            sends = arrays[:]
        else:
            sends = pack(plan, arrays, tail, afters[step])
        for hold, order, send in zip(holds, orders, sends):
            at = len(arrays)
            arrays.append(swap(send, "exp", 1 << order[step]))
            far = 1 << (order[step] - 1)
            for i, p in enumerate(sorted(hold)):
                hold[p | far] = (at, None if step == 0 else i)
    plan = [[hold[p] for hold in holds for p in range(chips)]]
    (packed,) = pack(plan, arrays, tail, last(sends))
    return packed, sends


def load_kernel(blocks, *refs):
    token, sems = refs[-2:]
    outs = refs[-2 - len(blocks) : -2]
    copies = []
    for i, (out, (which, j)) in enumerate(zip(outs, blocks)):
        cols = out.shape[1]
        source = refs[which].at[0, :, j * cols : (j + 1) * cols]
        copies.append(pltpu.make_async_copy(source, out, sems.at[i]))
    for copy in copies:
        copy.start()
    for copy in copies:
        copy.wait()
    token[...] = jnp.zeros_like(token)


def load_blocks(weights, blocks, cols, after, limit):
    units = weights[0].shape[1]
    *loaded, token = pl.pallas_call(
        functools.partial(load_kernel, blocks),
        out_shape=[shape((units, cols), BF16) for _ in blocks] + [shape((8, 128), F32)],
        in_specs=[IN_HBM, IN_HBM, WHOLE],
        out_specs=[WHOLE] * (len(blocks) + 1),
        scratch_shapes=[pltpu.SemaphoreType.DMA((len(blocks),))],
        compiler_params=pltpu.CompilerParams(vmem_limit_bytes=limit * MIB),
        cost_estimate=pl.CostEstimate(
            flops=0, bytes_accessed=4 * units * cols * len(blocks), transcendentals=0
        ),
    )(*weights, after)
    return loaded, token


def expert_kernel(C, E, per_block, width, columns, held_counts, *refs):
    groups = C // 2
    packed, refs = refs[: 2 * groups], refs[2 * groups :]
    gate_count, held = held_counts[0], sum(held_counts)
    helds, refs = (refs[:gate_count], refs[gate_count:held]), refs[held:]
    gain, *streamed, down = refs[:4]
    outs, hidden, refs = refs[4 : 2 * groups + 4], refs[2 * groups + 4], refs[2 * groups + 5 :]
    *sums, activated, block, shift, spread, scale = refs[:7]
    *slots, down_slots, gate_sems, up_sems, down_sems = refs[7:]
    sems = (gate_sems, up_sems)
    ctx, exp = lax.axis_index("ctx"), lax.axis_index("exp")
    chips = E // 2
    token_rows = packed[0].shape[2]
    cols = packed[0].shape[3] - EXTRA
    group_rows = 2 * chips * token_rows
    features = hidden.shape[1]
    up_steps = C * per_block
    firsts = [count * per_block for count in held_counts]
    first = max(firsts)
    down_steps = features // columns
    aheads, down_ahead = [ref.shape[0] for ref in slots], down_slots.shape[0]

    def up_copy(n, i, slot):
        at = pl.ds(pl.multiple_of(i * width, 128), width)
        return pltpu.make_async_copy(
            streamed[n].at[0, :, at], slots[n].at[slot], sems[n].at[slot]
        )

    def down_copy(i, slot):
        at = pl.ds(pl.multiple_of(i * columns, 128), columns)
        return pltpu.make_async_copy(down.at[0, :, at], down_slots.at[slot], down_sems.at[slot])

    for n in range(2):
        for i in range(aheads[n]):
            up_copy(n, firsts[n] + i, i).start()

    def read(g, s, at):
        parts = [
            packed[side * groups + g][s * chips + p, ctx ^ (t * groups + h), :, at]
            for side in range(2)
            for h in range(groups)
            for t in range(2)
            for p in range(chips)
        ]
        return jnp.concatenate([part.astype(F32) for part in parts], axis=0)

    tails = [read(k % groups, k // groups, slice(cols, cols + EXTRA)) for k in range(C)]
    lane = lax.broadcasted_iota(jnp.int32, tails[0].shape, 1)

    def pick(tail, wanted):
        return jnp.sum(jnp.where(wanted, tail, 0.0), axis=1, keepdims=True)

    means = [pick(tail, lane < SPLIT) for tail in tails]
    squares = [pick(tail, (lane >= SPLIT) & (lane < 2 * SPLIT)) for tail in tails]
    mean = sum(means) * (1.0 / C)
    deviation = sum(squares) + cols * sum((m - mean) * (m - mean) for m in means)
    spread[...] = lax.rsqrt(deviation * (1.0 / features) + 1e-05)
    for k in range(C):
        shift[k, 0] = means[k]
        shift[k, 1] = means[k] - mean
    term = lane - FIRST
    wanted = (term >= 0) & ((term & (E - 1)) == exp) & (term < SPLIT * E)
    scale[...] = sum(pick(tail, wanted) for tail in tails)

    def normalise(j, part):
        k = j ^ ctx
        at = pl.ds(pl.multiple_of(part * width, 128), width)
        place = pl.multiple_of(j * cols + part * width, 128)
        for g in range(groups):

            @pl.when(k % groups == g)
            def _():
                s = k // groups
                value = (read(g, s, at) + shift[k, 1]) * spread[...]
                block[...] = (value * gain[:, pl.ds(place, width)]).astype(BF16)
                own = packed[g][s * chips, ctx, :, at].astype(F32)
                hidden[:, pl.ds(place, width)] = own + shift[k, 0, :token_rows]

    turned_dot = functools.partial(
        lax.dot_general,
        dimension_numbers=(((1,), (1,)), ((), ())),
        preferred_element_type=F32,
    )
    if held == 0:
        for total in sums:
            total[...] = jnp.zeros_like(total)
        for i in range(down_ahead):
            down_copy(i, i).start()
    for i in range(first):
        j, part = i // per_block, i % per_block
        normalise(j, part)
        for n, total in enumerate(sums):
            slot = (i - firsts[n]) % aheads[n]
            if i < firsts[n]:
                weight = helds[n][j][:, part * width : (part + 1) * width]
            else:
                up_copy(n, i, slot).wait()
                weight = slots[n][slot]
            product = turned_dot(block[...], weight)
            total[...] = product if i == 0 else total[...] + product
            if i >= firsts[n] and i + aheads[n] < up_steps:
                up_copy(n, i + aheads[n], slot).start()
        if i == first // 2:
            for d in range(down_ahead):
                down_copy(d, d).start()

    @pl.loop(first, up_steps)
    def _(i):
        normalise(i // per_block, i % per_block)
        for n, total in enumerate(sums):
            slot = (i - firsts[n]) % aheads[n]
            up_copy(n, i, slot).wait()
            total[...] += turned_dot(block[...], slots[n][slot])

            @pl.when(i + aheads[n] < up_steps)
            def _():
                up_copy(n, i + aheads[n], slot).start()

    value = sums[0][...]
    value = value / (1.0 + jnp.exp(-value)) * sums[1][...]
    activated[...] = value.astype(BF16)

    @pl.loop(0, down_steps)
    def _(i):
        slot = i % down_ahead
        down_copy(i, slot).wait()
        value = jnp.dot(activated[...], down_slots[slot], preferred_element_type=F32)
        value = value * scale[...]

        @pl.when(i + down_ahead < down_steps)
        def _():
            down_copy(i + down_ahead, slot).start()

        place = pl.ds(pl.multiple_of(i * columns, 128), columns)
        for n, out in enumerate(outs):
            part = value[n * group_rows : (n + 1) * group_rows]
            out[:, :, place] = part.reshape(2 * chips, token_rows, columns).astype(BF16)


def largest_part(size, most, unit):
    return max(c for c in range(unit, most + 1, unit) if size % c == 0)


def run_experts(packed, helds, gain, weights, down_weight, C, E):
    count = len(packed)
    pieces, _, token_rows, wide = packed[0].shape
    cols = wide - EXTRA
    features = cols * C
    units = weights[0].shape[1]
    total = C * E * token_rows
    held_counts = [len(blocks) for blocks in helds]
    held = sum(held_counts)
    width = largest_part(cols, 768 if held else 384, 128)
    columns = largest_part(features, 768 if held else 384, 128)
    per_block = cols // width
    ahead, up_ahead = 2, 3 if held else 2
    down_ahead = 3 if held else 2
    operands = [*packed, *helds[0], *helds[1], gain]
    *outs, hidden = pl.pallas_call(
        functools.partial(expert_kernel, C, E, per_block, width, columns, held_counts),
        out_shape=[shape((pieces, token_rows, features), BF16) for _ in packed]
        + [shape((token_rows, features), F32)],
        in_specs=[WHOLE] * len(operands) + [IN_HBM] * 3,
        out_specs=[WHOLE] * (count + 1),
        scratch_shapes=[
            pltpu.VMEM((total, units), F32),
            pltpu.VMEM((total, units), F32),
            pltpu.VMEM((total, units), BF16),
            pltpu.VMEM((total, width), BF16),
            pltpu.VMEM((C, 2, total, 1), F32),
            pltpu.VMEM((total, 1), F32),
            pltpu.VMEM((total, 1), F32),
            pltpu.VMEM((ahead, units, width), BF16),
            pltpu.VMEM((up_ahead, units, width), BF16),
            pltpu.VMEM((down_ahead, units, columns), BF16),
            pltpu.SemaphoreType.DMA((ahead,)),
            pltpu.SemaphoreType.DMA((up_ahead,)),
            pltpu.SemaphoreType.DMA((down_ahead,)),
        ],
        compiler_params=pltpu.CompilerParams(vmem_limit_bytes=(33 if held else 58) * MIB),
        cost_estimate=pl.CostEstimate(
            flops=6 * total * features * units,
            bytes_accessed=6 * features * units + 4 * total * features,
            transcendentals=total * units,
        ),
    )(*operands, *weights, down_weight)
    return outs, hidden


def fold_kernel(plan, *refs):
    ins, outs = refs[: -len(plan)], refs[-len(plan) :]
    for out, places in zip(outs, plan):
        for i, parts in enumerate(places):
            out[i] = sum(ins[at][place].astype(F32) for at, place in parts).astype(BF16)


def fold(plan, operands):
    tail = operands[0].shape[1:]
    return call(
        functools.partial(fold_kernel, plan),
        [shape((len(places), *tail), BF16) for places in plan],
        operands,
        [WHOLE] * len(operands),
    )


def sum_over_plane(own, received, orders, added, apart):
    chips = own.shape[0] // 2
    operands = [own, received]
    holds = [
        {p: [(0, s * chips + p), (1, s * chips + p)] for p in range(chips)}
        for s in range(len(orders))
    ]
    for step in range(len(orders[0])):
        far = [1 << (order[step] - 1) for order in orders]
        sent = [[p for p in sorted(hold) if p & f] for hold, f in zip(holds, far)]
        kept = [[p for p in sorted(hold) if not p & f] for hold, f in zip(holds, far)]
        plan = [[hold[p] for p in ps] for hold, ps in zip(holds * 2, sent + kept)]
        *sends, keep0, keep1 = fold(plan, operands)
        got = [swap(value, "exp", 1 << order[step]) for value, order in zip(sends, orders)]
        operands = [keep0, got[0], keep1, got[1]]
        holds = [
            {p: [(2 * s, i), (2 * s + 1, i)] for i, p in enumerate(kept[s])}
            for s in range(len(orders))
        ]
    parts = [hold[0] + [(4 + i, s) for i in range(len(added))] for s, hold in enumerate(holds)]
    return fold([[part] for part in parts] if apart else [parts], operands + added)


def on_device(
    queries,
    keys_values,
    residual,
    out_weight,
    norm_gain,
    routes,
    route_weight,
    gate_weight,
    up_weight,
    down_weight,
):
    C = lax.axis_size("ctx")
    E = lax.axis_size("exp")
    chips = E // 2
    chip_bits = list(range(1, E.bit_length() - 1))
    heads = queries.shape[1] // HD
    seq = queries.shape[0] * C
    token_rows, features = residual.shape
    cols = out_weight.shape[1]
    wide = queries.shape[1] + HD
    slots = E + -(-cols // wide)
    sent = call(
        functools.partial(message_kernel, C, E),
        [shape((slots, token_rows, wide), BF16)] * C,
        [queries, keys_values, residual],
        [IN_HBM] * 3,
        [
            pltpu.VMEM(queries.shape, BF16),
            pltpu.VMEM(keys_values.shape, BF16),
            pltpu.VMEM(residual.shape, BF16),
            pltpu.SemaphoreType.DMA((3,)),
        ],
        limit=60,
    )
    messages = [swap(piece, "ctx", k) if k else piece for k, piece in enumerate(sent)]
    weight, gain = call(
        keep_kernel,
        [shape(out_weight.shape, BF16), shape((1, features), F32)],
        [sent[0], out_weight, norm_gain.reshape(1, -1)],
        [WHOLE] * 3,
    )
    halves, own_residual = call(
        functools.partial(halves_kernel, C, E),
        [
            shape((C, E, token_rows, HD), BF16),
            shape((slots - E, token_rows, wide), BF16),
        ],
        [*messages, weight, gain],
        [WHOLE] * (C + 2),
    )

    experts = jnp.arange(E, dtype=jnp.int32)
    left = jnp.sum(jnp.where(routes[:, :, None] == experts, route_weight[:, :, None], 0.0), axis=1)
    terms = []
    for _ in range(SPLIT):
        term = lax.reduce_precision(left, 8, 7)
        terms.append(term.astype(BF16))
        left = left - term
    extra = jnp.pad(
        jnp.concatenate(terms, axis=1), ((0, 0), (FIRST, EXTRA - FIRST - SPLIT * E))
    )

    mate_part, own_part = call(
        functools.partial(attend_kernel, C, E, heads),
        [
            shape((chips, C, token_rows, cols), BF16),
            shape((chips, C, token_rows, cols), F32),
        ],
        [*messages, swap(halves, "exp", 1), weight],
        [WHOLE] * (C + 2),
        [pltpu.VMEM((seq, cols), F32)],
        limit=16 if seq <= 256 else 56,
    )

    kept, *sent = call(
        mate_sum_kernel,
        [shape((C, token_rows, cols), F32)] + [shape((C, token_rows, cols), BF16)] * (chips - 1),
        [own_part, swap(mate_part, "exp", 1)],
        [WHOLE, WHOLE],
    )
    received = [swap(piece, "exp", (p + 1) << 1) for p, piece in enumerate(sent)]
    (rows,) = call(
        functools.partial(plane_sum_kernel, C, E, chips - 1),
        [shape((C, token_rows, cols + EXTRA), BF16)],
        [kept, *received, own_residual, *messages[1:], extra],
        [WHOLE] * (chips + C + 1),
    )

    weights = [jnp.swapaxes(gate_weight, 1, 2), jnp.swapaxes(up_weight, 1, 2)]
    hold = C * E * token_rows <= 256 and C == 4 and len(chip_bits) == 2
    loaded = []

    def load(which, j, after, limit):
        if not hold:
            return []
        blocks, token = load_blocks(weights, [(which, j)], cols, after, limit)
        loaded.extend(blocks)
        return [token]

    orders = (chip_bits[::-1], chip_bits)
    near = [rows, swap(rows, "ctx", C // 2)]
    (pair,) = pack([[(0, None), (1, None)]], near, rows.shape)
    pairs = [pair]
    for bit in range(C.bit_length() - 2):
        pairs += [swap(value, "ctx", 1 << bit) for value in pairs]
    afters = [[]] * len(chip_bits)
    group, sends = spread_over_plane(near, [(0, None), (1, None)], orders, chips, afters)
    packed = [group]
    token = load(0, 0, sends[0], 44)
    for value in pairs[1:]:
        afters = [sends] + [token] * (len(chip_bits) - 1)
        last = lambda sent: load(1, 0, sent[0], 44) + load(0, 1, packed[0], 40)
        group, sends = spread_over_plane(
            [value], [(0, 0), (0, 1)], orders, chips, afters, last
        )
        packed.append(group)
    packed += [swap(group, "exp", 1) for group in packed]

    outs, hidden = run_experts(
        packed, (loaded[0::2], loaded[1::2]), gain, weights, down_weight, C, E
    )

    count = C // 2
    added = [[] for _ in range(count)]
    for g in reversed(range(count)):
        received = swap(outs[count + g], "exp", 1)
        values = sum_over_plane(outs[g], received, orders[::-1], added[g], g == 0)
        if g:
            top = 1 << (g.bit_length() - 1)
            added[g ^ top].append(swap(values[0], "ctx", top))
    kept, sent = values
    total = hidden + kept[0].astype(F32) + swap(sent, "ctx", C // 2)[0].astype(F32)
    return total.astype(BF16)


def solution(mesh):
    in_specs = (
        P("ctx", "exp"),
        P(None, "ctx", "exp"),
        P(("ctx", "exp"), None),
        P("exp", "ctx"),
        P(),
        P(("ctx", "exp"), None),
        P(("ctx", "exp"), None),
        P("exp", None, "ctx"),
        P("exp", None, "ctx"),
        P("exp", "ctx", None),
    )
    out_specs = P(("ctx", "exp"), None)
    return jax.shard_map(
        on_device, mesh=mesh, in_specs=in_specs, out_specs=out_specs, check_vma=False
    )
```

```python
import functools
import math

import jax
import jax.numpy as jnp
from jax import lax
from jax.experimental import pallas as pl
from jax.experimental.pallas import tpu as pltpu
from jax.sharding import PartitionSpec as P

HD = 128
EXTRA = 128
SPLIT = 3
FIRST = 8
MIB = 1024 * 1024
F32 = jnp.float32
BF16 = jnp.bfloat16
WHOLE = pl.BlockSpec(memory_space=pltpu.VMEM)
IN_HBM = pl.BlockSpec(memory_space=pltpu.HBM)


def swap(value, axis, mask):
    return lax.ppermute(value, axis, [(i, i ^ mask) for i in range(lax.axis_size(axis))])


def call(kernel, out_shape, operands, in_specs, scratch=(), limit=16):
    return pl.pallas_call(
        kernel,
        out_shape=out_shape,
        in_specs=in_specs,
        out_specs=jax.tree.map(lambda _: WHOLE, out_shape),
        scratch_shapes=list(scratch),
        compiler_params=pltpu.CompilerParams(vmem_limit_bytes=limit * MIB),
    )(*operands)


def shape(dims, dtype):
    return jax.ShapeDtypeStruct(tuple(dims), dtype)


def attend_kernel(C, E, heads, *refs):
    messages, mates, out_weight, mate_out, own_out, projected = refs[:C], *refs[C:]
    ctx, exp = lax.axis_index("ctx"), lax.axis_index("exp")
    token_rows = mate_out.shape[2]
    rows = E * token_rows
    seq = rows * C
    blocks = [
        m[:E].astype(F32).reshape(rows, m.shape[2]).astype(BF16) for m in messages
    ]
    width = heads * HD
    half = HD // 2
    lower = (exp & 1) == 0

    other_half = mates[...].astype(F32).reshape(seq, HD).astype(BF16)

    def joined(start):
        first = width + start
        own = jnp.concatenate([b[:, first : first + half] for b in blocks], axis=0)
        mate = other_half[:, start : start + half]
        both = jnp.concatenate([own, mate], axis=1)
        other = jnp.concatenate([mate, own], axis=1)
        return jnp.where(lower, both, other)

    keys = joined(0)
    values = joined(half)
    shift = rows.bit_length() - 1
    column = lax.broadcasted_iota(jnp.int32, (rows, seq), 1)
    key_position = ((column >> shift) ^ ctx) * rows + (column & (rows - 1))
    row = lax.broadcasted_iota(jnp.int32, (rows, seq), 0)
    parts = []
    for k in range(C):
        allowed = key_position <= (ctx ^ k) * rows + row
        block_parts = []
        for h in range(heads):
            q = blocks[k][:, h * HD : (h + 1) * HD]
            scores = lax.dot_general(
                q, keys, (((1,), (1,)), ((), ())), preferred_element_type=F32
            ) * (1.0 / math.sqrt(HD))
            scores = jnp.where(allowed, scores, -jnp.inf)
            top = jnp.max(scores, axis=1, keepdims=True)
            weights = jnp.exp(scores - top)
            total = jnp.sum(weights, axis=1, keepdims=True)
            high = weights.astype(BF16)
            low = (weights - high.astype(F32)).astype(BF16)
            summed = jnp.dot(high, values, preferred_element_type=F32) + jnp.dot(
                low, values, preferred_element_type=F32
            )
            block_parts.append((summed / total).astype(BF16))
        parts.append(jnp.concatenate(block_parts, axis=1))
    attended = jnp.concatenate(parts, axis=0)
    projected[...] = jnp.dot(attended, out_weight[...], preferred_element_type=F32)
    for p in range(E):
        for j in range(C):
            start = pl.multiple_of(((ctx ^ j) * E + (exp ^ p)) * token_rows, token_rows)
            piece = projected[pl.ds(start, token_rows), :]
            if p & 1:
                mate_out[p >> 1, j] = piece.astype(BF16)
            else:
                own_out[p >> 1, j] = piece


def mate_sum_kernel(own, received, kept, *sent):
    kept[...] = own[0] + received[0].astype(F32)
    for p, out in enumerate(sent):
        out[...] = (own[p + 1] + received[p + 1].astype(F32)).astype(BF16)


def message_kernel(C, E, queries_in, own_in, residual_in, *refs):
    messages = refs[:C]
    queries, own, residual, sems = refs[C:]
    pairs = [(queries_in, queries), (own_in, own), (residual_in, residual)]
    loads = [pltpu.make_async_copy(a, b, sems.at[i]) for i, (a, b) in enumerate(pairs)]
    for load in loads:
        load.start()
    for load in loads:
        load.wait()
    token_rows, wide = messages[0].shape[1:]
    cols = residual.shape[1] // C
    parts = [queries[...], own[0], own[1]]
    bundle = jnp.concatenate([part.astype(F32) for part in parts], axis=1)
    bundle = bundle.reshape(E, token_rows, wide).astype(BF16)
    ctx = lax.axis_index("ctx")
    for k, out in enumerate(messages):
        out[:E] = bundle
        first = (ctx ^ k) * cols
        for i in range(out.shape[0] - E):
            width = min(wide, cols - i * wide)
            at = pl.ds(pl.multiple_of(first + i * wide, 128), width)
            out[E + i, :, :width] = residual[:, at]


def keep_kernel(after, out_weight, gain, weight_out, gain_out):
    weight_out[...] = out_weight[...]
    gain_out[...] = gain[...]


def halves_kernel(C, E, *refs):
    halves, residual = refs[-2:]
    for k in range(C):
        halves[k] = refs[k][:E, :, refs[k].shape[2] - HD :]
    residual[...] = refs[0][E:]


def split_terms(value):
    terms = []
    for _ in range(SPLIT):
        term = value.astype(BF16).astype(F32)
        terms.append(term)
        value = value - term
    return terms


def plane_sum_kernel(C, E, count, *refs):
    own, received, messages = refs[0], refs[1 : 1 + count], refs[1 + count : 1 + count + C]
    extra, out = refs[1 + count + C :]
    cols = own.shape[2]
    wide = messages[0].shape[2]
    lane = lax.broadcasted_iota(jnp.int32, (own.shape[1], EXTRA), 1)
    for k in range(C):
        j = lax.axis_index("ctx") ^ k
        start = E if k else 0
        pieces = [
            messages[k][start + i, :, : min(wide, cols - i * wide)].astype(F32)
            for i in range(messages[k].shape[0] - start)
        ]
        total = own[j] + jnp.concatenate(pieces, axis=1)
        for piece in received:
            total = total + piece[j].astype(F32)
        mean = jnp.sum(total, axis=1, keepdims=True) * (1.0 / cols)
        centered = total - mean
        squares = jnp.sum(centered * centered, axis=1, keepdims=True)
        out[j, :, :cols] = centered.astype(BF16)
        tail = jnp.zeros(lane.shape, F32) if k else extra[...].astype(F32)
        for i, term in enumerate(split_terms(mean) + split_terms(squares)):
            tail = jnp.where(lane == i, term, tail)
        out[j, :, cols:] = tail.astype(BF16)


def pack_kernel(plan, *refs):
    ins, outs = refs[: -len(plan)], refs[-len(plan) :]
    for out, sources in zip(outs, plan):
        for i, (at, place) in enumerate(sources):
            value = ins[at][...] if place is None else ins[at][place]
            if len(sources) == 1:
                out[...] = value
            else:
                out[i] = value


def pack(plan, arrays, tail, after=()):
    return call(
        functools.partial(pack_kernel, plan),
        [shape(tail if len(p) == 1 else (len(p), *tail), BF16) for p in plan],
        [*arrays, *after],
        [WHOLE] * (len(arrays) + len(after)),
    )


def spread_over_plane(arrays, sources, orders, chips, afters, last=lambda sends: []):
    tail = arrays[0].shape[-3:]
    holds = [{0: source} for source in sources]
    arrays = list(arrays)
    for step in range(len(orders[0])):
        plan = [[hold[p] for p in sorted(hold)] for hold in holds]
        if step == 0 and len(arrays) == 2:
            sends = arrays[:]
        else:
            sends = pack(plan, arrays, tail, afters[step])
        for hold, order, send in zip(holds, orders, sends):
            at = len(arrays)
            arrays.append(swap(send, "exp", 1 << order[step]))
            far = 1 << (order[step] - 1)
            for i, p in enumerate(sorted(hold)):
                hold[p | far] = (at, None if step == 0 else i)
    plan = [[hold[p] for hold in holds for p in range(chips)]]
    (packed,) = pack(plan, arrays, tail, last(sends))
    return packed, sends


def load_kernel(blocks, *refs):
    token, sems = refs[-2:]
    outs = refs[-2 - len(blocks) : -2]
    copies = []
    for i, (out, (which, j)) in enumerate(zip(outs, blocks)):
        cols = out.shape[1]
        source = refs[which].at[0, :, j * cols : (j + 1) * cols]
        copies.append(pltpu.make_async_copy(source, out, sems.at[i]))
    for copy in copies:
        copy.start()
    for copy in copies:
        copy.wait()
    token[...] = jnp.zeros_like(token)


def load_blocks(weights, blocks, cols, after, limit):
    units = weights[0].shape[1]
    *loaded, token = pl.pallas_call(
        functools.partial(load_kernel, blocks),
        out_shape=[shape((units, cols), BF16) for _ in blocks] + [shape((8, 128), F32)],
        in_specs=[IN_HBM, IN_HBM, WHOLE],
        out_specs=[WHOLE] * (len(blocks) + 1),
        scratch_shapes=[pltpu.SemaphoreType.DMA((len(blocks),))],
        compiler_params=pltpu.CompilerParams(vmem_limit_bytes=limit * MIB),
        cost_estimate=pl.CostEstimate(
            flops=0, bytes_accessed=4 * units * cols * len(blocks), transcendentals=0
        ),
    )(*weights, after)
    return loaded, token


def expert_kernel(C, E, per_block, width, columns, held_counts, *refs):
    groups = C // 2
    packed, refs = refs[: 2 * groups], refs[2 * groups :]
    gate_count, held = held_counts[0], sum(held_counts)
    helds, refs = (refs[:gate_count], refs[gate_count:held]), refs[held:]
    gain, *streamed, down = refs[:4]
    outs, hidden, refs = refs[4 : 2 * groups + 4], refs[2 * groups + 4], refs[2 * groups + 5 :]
    *sums, activated, block, next_block, shift, spread, scale = refs[:8]
    *slots, down_slots, gate_sems, up_sems, down_sems = refs[8:]
    sems = (gate_sems, up_sems)
    ctx, exp = lax.axis_index("ctx"), lax.axis_index("exp")
    chips = E // 2
    token_rows = packed[0].shape[2]
    cols = packed[0].shape[3] - EXTRA
    group_rows = 2 * chips * token_rows
    features = hidden.shape[1]
    up_steps = C * per_block
    firsts = [count * per_block for count in held_counts]
    down_steps = features // columns
    aheads, down_ahead = [ref.shape[0] for ref in slots], down_slots.shape[0]

    def up_copy(n, i, slot):
        at = pl.ds(pl.multiple_of(i * width, 128), width)
        return pltpu.make_async_copy(
            streamed[n].at[0, :, at], slots[n].at[slot], sems[n].at[slot]
        )

    def down_copy(i, slot):
        at = pl.ds(pl.multiple_of(i * columns, 128), columns)
        return pltpu.make_async_copy(down.at[0, :, at], down_slots.at[slot], down_sems.at[slot])

    for n in range(2):
        for i in range(aheads[n]):
            up_copy(n, firsts[n] + i, i).start()

    def read(g, s, at):
        parts = [
            packed[side * groups + g][s * chips + p, ctx ^ (t * groups + h), :, at]
            for side in range(2)
            for h in range(groups)
            for t in range(2)
            for p in range(chips)
        ]
        return jnp.concatenate([part.astype(F32) for part in parts], axis=0)

    tails = [read(k % groups, k // groups, slice(cols, cols + EXTRA)) for k in range(C)]
    lane = lax.broadcasted_iota(jnp.int32, tails[0].shape, 1)

    def pick(tail, wanted):
        return jnp.sum(jnp.where(wanted, tail, 0.0), axis=1, keepdims=True)

    means = [pick(tail, lane < SPLIT) for tail in tails]
    squares = [pick(tail, (lane >= SPLIT) & (lane < 2 * SPLIT)) for tail in tails]
    mean = sum(means) * (1.0 / C)
    deviation = sum(squares) + cols * sum((m - mean) * (m - mean) for m in means)
    spread[...] = lax.rsqrt(deviation * (1.0 / features) + 1e-05)
    for k in range(C):
        shift[k, 0] = means[k]
        shift[k, 1] = means[k] - mean
    term = lane - FIRST
    wanted = (term >= 0) & ((term & (E - 1)) == exp) & (term < SPLIT * E)
    scale[...] = sum(pick(tail, wanted) for tail in tails)

    def normalise(j, part):
        k = j ^ ctx
        at = pl.ds(pl.multiple_of(part * width, 128), width)
        place = pl.multiple_of(j * cols + part * width, 128)
        for g in range(groups):

            @pl.when(k % groups == g)
            def _():
                s = k // groups
                value = (read(g, s, at) + shift[k, 1]) * spread[...]
                block[...] = (value * gain[:, pl.ds(place, width)]).astype(BF16)
                own = packed[g][s * chips, ctx, :, at].astype(F32)
                hidden[:, pl.ds(place, width)] = own + shift[k, 0, :token_rows]

    def normalise_any(j, part, target):
        k = j ^ ctx
        s = k // groups
        at = slice(part * width, (part + 1) * width)
        place = slice(j * cols + part * width, j * cols + (part + 1) * width)
        centered = read(groups - 1, s, at)
        for g in range(groups - 1):
            centered = jnp.where(k % groups == g, read(g, s, at), centered)
        value = (centered + shift[k, 1]) * spread[...]
        target[...] = (value * gain[:, place]).astype(BF16)
        hidden[:, place] = centered[:token_rows] + shift[k, 0, :token_rows]

    turned_dot = functools.partial(
        lax.dot_general,
        dimension_numbers=(((1,), (1,)), ((), ())),
        preferred_element_type=F32,
    )
    if held == 0:
        for total in sums:
            total[...] = jnp.zeros_like(total)
        for i in range(down_ahead):
            down_copy(i, i).start()
    static_steps = up_steps if held else 0
    blocks = (block, next_block)
    for i in range(static_steps):
        if i == 0:
            normalise_any(0, 0, blocks[0])
        for n in range(2):
            if i >= firsts[n]:
                up_copy(n, i, (i - firsts[n]) % aheads[n]).wait()
        if i + 1 < up_steps:
            normalise_any((i + 1) // per_block, (i + 1) % per_block, blocks[(i + 1) % 2])
        for n, total in enumerate(sums):
            if i < firsts[n]:
                weight = helds[n][i // per_block]
                part = i % per_block
                weight = weight[:, part * width : (part + 1) * width]
            else:
                weight = slots[n][(i - firsts[n]) % aheads[n]]
            product = turned_dot(blocks[i % 2][...], weight)
            total[...] = product if i == 0 else total[...] + product
        for n in range(2):
            if i >= firsts[n] and i + aheads[n] < up_steps:
                up_copy(n, i + aheads[n], (i - firsts[n]) % aheads[n]).start()
        if i == 1:
            for d in range(down_ahead):
                down_copy(d, d).start()

    if static_steps < up_steps:

        @pl.loop(static_steps, up_steps)
        def _(i):
            normalise(i // per_block, i % per_block)
            for n, total in enumerate(sums):
                slot = (i - firsts[n]) % aheads[n]
                up_copy(n, i, slot).wait()
                total[...] += turned_dot(block[...], slots[n][slot])

                @pl.when(i + aheads[n] < up_steps)
                def _():
                    up_copy(n, i + aheads[n], slot).start()

    value = sums[0][...]
    value = value / (1.0 + jnp.exp(-value)) * sums[1][...]
    activated[...] = value.astype(BF16)

    @pl.loop(0, down_steps)
    def _(i):
        slot = i % down_ahead
        down_copy(i, slot).wait()
        value = jnp.dot(activated[...], down_slots[slot], preferred_element_type=F32)
        value = value * scale[...]

        @pl.when(i + down_ahead < down_steps)
        def _():
            down_copy(i + down_ahead, slot).start()

        place = pl.ds(pl.multiple_of(i * columns, 128), columns)
        for n, out in enumerate(outs):
            part = value[n * group_rows : (n + 1) * group_rows]
            out[:, :, place] = part.reshape(2 * chips, token_rows, columns).astype(BF16)


def largest_part(size, most, unit):
    return max(c for c in range(unit, most + 1, unit) if size % c == 0)


def run_experts(packed, helds, gain, weights, down_weight, C, E):
    count = len(packed)
    pieces, _, token_rows, wide = packed[0].shape
    cols = wide - EXTRA
    features = cols * C
    units = weights[0].shape[1]
    total = C * E * token_rows
    held_counts = [len(blocks) for blocks in helds]
    held = sum(held_counts)
    width = largest_part(cols, 768 if held else 384, 128)
    columns = largest_part(features, 768 if held else 384, 128)
    per_block = cols // width
    ahead = 3 if held else 2
    down_ahead = 3 if held else 2
    operands = [*packed, *helds[0], *helds[1], gain]
    *outs, hidden = pl.pallas_call(
        functools.partial(expert_kernel, C, E, per_block, width, columns, held_counts),
        out_shape=[shape((pieces, token_rows, features), BF16) for _ in packed]
        + [shape((token_rows, features), F32)],
        in_specs=[WHOLE] * len(operands) + [IN_HBM] * 3,
        out_specs=[WHOLE] * (count + 1),
        scratch_shapes=[
            pltpu.VMEM((total, units), F32),
            pltpu.VMEM((total, units), F32),
            pltpu.VMEM((total, units), BF16),
            pltpu.VMEM((total, width), BF16),
            pltpu.VMEM((total, width), BF16),
            pltpu.VMEM((C, 2, total, 1), F32),
            pltpu.VMEM((total, 1), F32),
            pltpu.VMEM((total, 1), F32),
            pltpu.VMEM((ahead, units, width), BF16),
            pltpu.VMEM((ahead, units, width), BF16),
            pltpu.VMEM((down_ahead, units, columns), BF16),
            pltpu.SemaphoreType.DMA((ahead,)),
            pltpu.SemaphoreType.DMA((ahead,)),
            pltpu.SemaphoreType.DMA((down_ahead,)),
        ],
        compiler_params=pltpu.CompilerParams(vmem_limit_bytes=(35 if held else 58) * MIB),
        cost_estimate=pl.CostEstimate(
            flops=6 * total * features * units,
            bytes_accessed=6 * features * units + 4 * total * features,
            transcendentals=total * units,
        ),
    )(*operands, *weights, down_weight)
    return outs, hidden


def fold_kernel(plan, *refs):
    ins, outs = refs[: -len(plan)], refs[-len(plan) :]
    for out, places in zip(outs, plan):
        for i, parts in enumerate(places):
            out[i] = sum(ins[at][place].astype(F32) for at, place in parts).astype(BF16)


def fold(plan, operands):
    tail = operands[0].shape[1:]
    return call(
        functools.partial(fold_kernel, plan),
        [shape((len(places), *tail), BF16) for places in plan],
        operands,
        [WHOLE] * len(operands),
    )


def sum_over_plane(own, received, orders, added, apart):
    chips = own.shape[0] // 2
    operands = [own, received]
    holds = [
        {p: [(0, s * chips + p), (1, s * chips + p)] for p in range(chips)}
        for s in range(len(orders))
    ]
    for step in range(len(orders[0])):
        far = [1 << (order[step] - 1) for order in orders]
        sent = [[p for p in sorted(hold) if p & f] for hold, f in zip(holds, far)]
        kept = [[p for p in sorted(hold) if not p & f] for hold, f in zip(holds, far)]
        plan = [[hold[p] for p in ps] for hold, ps in zip(holds * 2, sent + kept)]
        *sends, keep0, keep1 = fold(plan, operands)
        got = [swap(value, "exp", 1 << order[step]) for value, order in zip(sends, orders)]
        operands = [keep0, got[0], keep1, got[1]]
        holds = [
            {p: [(2 * s, i), (2 * s + 1, i)] for i, p in enumerate(kept[s])}
            for s in range(len(orders))
        ]
    parts = [hold[0] + [(4 + i, s) for i in range(len(added))] for s, hold in enumerate(holds)]
    return fold([[part] for part in parts] if apart else [parts], operands + added)


def on_device(
    queries,
    keys_values,
    residual,
    out_weight,
    norm_gain,
    routes,
    route_weight,
    gate_weight,
    up_weight,
    down_weight,
):
    C = lax.axis_size("ctx")
    E = lax.axis_size("exp")
    chips = E // 2
    chip_bits = list(range(1, E.bit_length() - 1))
    heads = queries.shape[1] // HD
    seq = queries.shape[0] * C
    token_rows, features = residual.shape
    cols = out_weight.shape[1]
    wide = queries.shape[1] + HD
    slots = E + -(-cols // wide)
    sent = call(
        functools.partial(message_kernel, C, E),
        [shape((slots, token_rows, wide), BF16)] * C,
        [queries, keys_values, residual],
        [IN_HBM] * 3,
        [
            pltpu.VMEM(queries.shape, BF16),
            pltpu.VMEM(keys_values.shape, BF16),
            pltpu.VMEM(residual.shape, BF16),
            pltpu.SemaphoreType.DMA((3,)),
        ],
        limit=60,
    )
    messages = [swap(piece, "ctx", k) if k else piece for k, piece in enumerate(sent)]
    weight, gain = call(
        keep_kernel,
        [shape(out_weight.shape, BF16), shape((1, features), F32)],
        [sent[0], out_weight, norm_gain.reshape(1, -1)],
        [WHOLE] * 3,
    )
    halves, own_residual = call(
        functools.partial(halves_kernel, C, E),
        [
            shape((C, E, token_rows, HD), BF16),
            shape((slots - E, token_rows, wide), BF16),
        ],
        [*messages, weight, gain],
        [WHOLE] * (C + 2),
    )

    experts = jnp.arange(E, dtype=jnp.int32)
    left = jnp.sum(jnp.where(routes[:, :, None] == experts, route_weight[:, :, None], 0.0), axis=1)
    terms = []
    for _ in range(SPLIT):
        term = lax.reduce_precision(left, 8, 7)
        terms.append(term.astype(BF16))
        left = left - term
    extra = jnp.pad(
        jnp.concatenate(terms, axis=1), ((0, 0), (FIRST, EXTRA - FIRST - SPLIT * E))
    )

    mate_part, own_part = call(
        functools.partial(attend_kernel, C, E, heads),
        [
            shape((chips, C, token_rows, cols), BF16),
            shape((chips, C, token_rows, cols), F32),
        ],
        [*messages, swap(halves, "exp", 1), weight],
        [WHOLE] * (C + 2),
        [pltpu.VMEM((seq, cols), F32)],
        limit=16 if seq <= 256 else 56,
    )

    kept, *sent = call(
        mate_sum_kernel,
        [shape((C, token_rows, cols), F32)] + [shape((C, token_rows, cols), BF16)] * (chips - 1),
        [own_part, swap(mate_part, "exp", 1)],
        [WHOLE, WHOLE],
    )
    received = [swap(piece, "exp", (p + 1) << 1) for p, piece in enumerate(sent)]
    (rows,) = call(
        functools.partial(plane_sum_kernel, C, E, chips - 1),
        [shape((C, token_rows, cols + EXTRA), BF16)],
        [kept, *received, own_residual, *messages[1:], extra],
        [WHOLE] * (chips + C + 1),
    )

    weights = [jnp.swapaxes(gate_weight, 1, 2), jnp.swapaxes(up_weight, 1, 2)]
    hold = C * E * token_rows <= 256 and C == 4 and len(chip_bits) == 2
    loaded = []

    def load(which, j, after, limit):
        if not hold:
            return []
        blocks, token = load_blocks(weights, [(which, j)], cols, after, limit)
        loaded.extend(blocks)
        return [token]

    orders = (chip_bits[::-1], chip_bits)
    near = [rows, swap(rows, "ctx", C // 2)]
    (pair,) = pack([[(0, None), (1, None)]], near, rows.shape)
    pairs = [pair]
    for bit in range(C.bit_length() - 2):
        pairs += [swap(value, "ctx", 1 << bit) for value in pairs]
    afters = [[]] * len(chip_bits)
    group, sends = spread_over_plane(near, [(0, None), (1, None)], orders, chips, afters)
    packed = [group]
    token = load(0, 0, sends[0], 44)
    for value in pairs[1:]:
        afters = [sends] + [token] * (len(chip_bits) - 1)
        last = lambda sent: load(1, 0, sent[0], 44)
        group, sends = spread_over_plane(
            [value], [(0, 0), (0, 1)], orders, chips, afters, last
        )
        packed.append(group)
    packed += [swap(group, "exp", 1) for group in packed]

    outs, hidden = run_experts(
        packed, (loaded[0::2], loaded[1::2]), gain, weights, down_weight, C, E
    )

    count = C // 2
    added = [[] for _ in range(count)]
    for g in reversed(range(count)):
        received = swap(outs[count + g], "exp", 1)
        values = sum_over_plane(outs[g], received, orders[::-1], added[g], g == 0)
        if g:
            top = 1 << (g.bit_length() - 1)
            added[g ^ top].append(swap(values[0], "ctx", top))
    kept, sent = values
    total = hidden + kept[0].astype(F32) + swap(sent, "ctx", C // 2)[0].astype(F32)
    return total.astype(BF16)


def solution(mesh):
    in_specs = (
        P("ctx", "exp"),
        P(None, "ctx", "exp"),
        P(("ctx", "exp"), None),
        P("exp", "ctx"),
        P(),
        P(("ctx", "exp"), None),
        P(("ctx", "exp"), None),
        P("exp", None, "ctx"),
        P("exp", None, "ctx"),
        P("exp", "ctx", None),
    )
    out_specs = P(("ctx", "exp"), None)
    return jax.shard_map(
        on_device, mesh=mesh, in_specs=in_specs, out_specs=out_specs, check_vma=False
    )
```

```python
import functools
import math

import jax
import jax.numpy as jnp
from jax import lax
from jax.experimental import pallas as pl
from jax.experimental.pallas import tpu as pltpu
from jax.sharding import PartitionSpec as P

HD = 128
EXTRA = 128
SPLIT = 3
FIRST = 8
MIB = 1024 * 1024
F32 = jnp.float32
BF16 = jnp.bfloat16
WHOLE = pl.BlockSpec(memory_space=pltpu.VMEM)
IN_HBM = pl.BlockSpec(memory_space=pltpu.HBM)


def swap(value, axis, mask):
    return lax.ppermute(value, axis, [(i, i ^ mask) for i in range(lax.axis_size(axis))])


def call(kernel, out_shape, operands, in_specs, scratch=(), limit=16):
    return pl.pallas_call(
        kernel,
        out_shape=out_shape,
        in_specs=in_specs,
        out_specs=jax.tree.map(lambda _: WHOLE, out_shape),
        scratch_shapes=list(scratch),
        compiler_params=pltpu.CompilerParams(vmem_limit_bytes=limit * MIB),
    )(*operands)


def shape(dims, dtype):
    return jax.ShapeDtypeStruct(tuple(dims), dtype)


def attend_kernel(C, E, heads, *refs):
    messages, mates, out_weight, mate_out, own_out, projected = refs[:C], *refs[C:]
    ctx, exp = lax.axis_index("ctx"), lax.axis_index("exp")
    token_rows = mate_out.shape[2]
    rows = E * token_rows
    seq = rows * C
    blocks = [
        m[:E].astype(F32).reshape(rows, m.shape[2]).astype(BF16) for m in messages
    ]
    width = heads * HD
    half = HD // 2
    lower = (exp & 1) == 0

    other_half = mates[...].astype(F32).reshape(seq, HD).astype(BF16)

    def joined(start):
        first = width + start
        own = jnp.concatenate([b[:, first : first + half] for b in blocks], axis=0)
        mate = other_half[:, start : start + half]
        both = jnp.concatenate([own, mate], axis=1)
        other = jnp.concatenate([mate, own], axis=1)
        return jnp.where(lower, both, other)

    keys = joined(0)
    values = joined(half)
    shift = rows.bit_length() - 1
    column = lax.broadcasted_iota(jnp.int32, (rows, seq), 1)
    key_position = ((column >> shift) ^ ctx) * rows + (column & (rows - 1))
    row = lax.broadcasted_iota(jnp.int32, (rows, seq), 0)
    parts = []
    for k in range(C):
        allowed = key_position <= (ctx ^ k) * rows + row
        block_parts = []
        for h in range(heads):
            q = blocks[k][:, h * HD : (h + 1) * HD]
            scores = lax.dot_general(
                q, keys, (((1,), (1,)), ((), ())), preferred_element_type=F32
            ) * (1.0 / math.sqrt(HD))
            scores = jnp.where(allowed, scores, -jnp.inf)
            top = jnp.max(scores, axis=1, keepdims=True)
            weights = jnp.exp(scores - top)
            total = jnp.sum(weights, axis=1, keepdims=True)
            high = weights.astype(BF16)
            low = (weights - high.astype(F32)).astype(BF16)
            summed = jnp.dot(high, values, preferred_element_type=F32) + jnp.dot(
                low, values, preferred_element_type=F32
            )
            block_parts.append((summed / total).astype(BF16))
        parts.append(jnp.concatenate(block_parts, axis=1))
    attended = jnp.concatenate(parts, axis=0)
    projected[...] = jnp.dot(attended, out_weight[...], preferred_element_type=F32)
    for p in range(E):
        for j in range(C):
            start = pl.multiple_of(((ctx ^ j) * E + (exp ^ p)) * token_rows, token_rows)
            piece = projected[pl.ds(start, token_rows), :]
            if p & 1:
                mate_out[p >> 1, j] = piece.astype(BF16)
            else:
                own_out[p >> 1, j] = piece


def mate_sum_kernel(own, received, kept, *sent):
    kept[...] = own[0] + received[0].astype(F32)
    for p, out in enumerate(sent):
        out[...] = (own[p + 1] + received[p + 1].astype(F32)).astype(BF16)


def message_kernel(C, E, queries_in, own_in, residual_in, *refs):
    messages = refs[:C]
    queries, own, residual, sems = refs[C:]
    pairs = [(queries_in, queries), (own_in, own), (residual_in, residual)]
    loads = [pltpu.make_async_copy(a, b, sems.at[i]) for i, (a, b) in enumerate(pairs)]
    for load in loads:
        load.start()
    for load in loads:
        load.wait()
    token_rows, wide = messages[0].shape[1:]
    cols = residual.shape[1] // C
    parts = [queries[...], own[0], own[1]]
    bundle = jnp.concatenate([part.astype(F32) for part in parts], axis=1)
    bundle = bundle.reshape(E, token_rows, wide).astype(BF16)
    ctx = lax.axis_index("ctx")
    for k, out in enumerate(messages):
        out[:E] = bundle
        first = (ctx ^ k) * cols
        for i in range(out.shape[0] - E):
            width = min(wide, cols - i * wide)
            at = pl.ds(pl.multiple_of(first + i * wide, 128), width)
            out[E + i, :, :width] = residual[:, at]


def keep_kernel(after, out_weight, gain, weight_out, gain_out):
    weight_out[...] = out_weight[...]
    gain_out[...] = gain[...]


def halves_kernel(C, E, *refs):
    halves, residual = refs[-2:]
    for k in range(C):
        halves[k] = refs[k][:E, :, refs[k].shape[2] - HD :]
    residual[...] = refs[0][E:]


def split_terms(value):
    terms = []
    for _ in range(SPLIT):
        term = value.astype(BF16).astype(F32)
        terms.append(term)
        value = value - term
    return terms


def plane_sum_kernel(C, E, count, *refs):
    own, received, messages = refs[0], refs[1 : 1 + count], refs[1 + count : 1 + count + C]
    extra, out = refs[1 + count + C :]
    cols = own.shape[2]
    wide = messages[0].shape[2]
    lane = lax.broadcasted_iota(jnp.int32, (own.shape[1], EXTRA), 1)
    for k in range(C):
        j = lax.axis_index("ctx") ^ k
        start = E if k else 0
        pieces = [
            messages[k][start + i, :, : min(wide, cols - i * wide)].astype(F32)
            for i in range(messages[k].shape[0] - start)
        ]
        total = own[j] + jnp.concatenate(pieces, axis=1)
        for piece in received:
            total = total + piece[j].astype(F32)
        mean = jnp.sum(total, axis=1, keepdims=True) * (1.0 / cols)
        centered = total - mean
        squares = jnp.sum(centered * centered, axis=1, keepdims=True)
        out[j, :, :cols] = centered.astype(BF16)
        tail = jnp.zeros(lane.shape, F32) if k else extra[...].astype(F32)
        for i, term in enumerate(split_terms(mean) + split_terms(squares)):
            tail = jnp.where(lane == i, term, tail)
        out[j, :, cols:] = tail.astype(BF16)


def pack_kernel(plan, *refs):
    ins, outs = refs[: -len(plan)], refs[-len(plan) :]
    for out, sources in zip(outs, plan):
        for i, (at, place) in enumerate(sources):
            value = ins[at][...] if place is None else ins[at][place]
            if len(sources) == 1:
                out[...] = value
            else:
                out[i] = value


def pack(plan, arrays, tail, after=()):
    return call(
        functools.partial(pack_kernel, plan),
        [shape(tail if len(p) == 1 else (len(p), *tail), BF16) for p in plan],
        [*arrays, *after],
        [WHOLE] * (len(arrays) + len(after)),
    )


def spread_over_plane(arrays, sources, orders, chips, afters, last=lambda sends: []):
    tail = arrays[0].shape[-3:]
    holds = [{0: source} for source in sources]
    arrays = list(arrays)
    for step in range(len(orders[0])):
        plan = [[hold[p] for p in sorted(hold)] for hold in holds]
        if step == 0 and len(arrays) == 2:
            sends = arrays[:]
        else:
            sends = pack(plan, arrays, tail, afters[step])
        for hold, order, send in zip(holds, orders, sends):
            at = len(arrays)
            arrays.append(swap(send, "exp", 1 << order[step]))
            far = 1 << (order[step] - 1)
            for i, p in enumerate(sorted(hold)):
                hold[p | far] = (at, None if step == 0 else i)
    plan = [[hold[p] for hold in holds for p in range(chips)]]
    (packed,) = pack(plan, arrays, tail, last(sends))
    return packed, sends


def load_kernel(blocks, *refs):
    token, sems = refs[-2:]
    outs = refs[-2 - len(blocks) : -2]
    copies = []
    for i, (out, (which, j)) in enumerate(zip(outs, blocks)):
        cols = out.shape[1]
        source = refs[which].at[0, :, j * cols : (j + 1) * cols]
        copies.append(pltpu.make_async_copy(source, out, sems.at[i]))
    for copy in copies:
        copy.start()
    for copy in copies:
        copy.wait()
    token[...] = jnp.zeros_like(token)


def load_blocks(weights, blocks, cols, after, limit):
    units = weights[0].shape[1]
    *loaded, token = pl.pallas_call(
        functools.partial(load_kernel, blocks),
        out_shape=[shape((units, cols), BF16) for _ in blocks] + [shape((8, 128), F32)],
        in_specs=[IN_HBM, IN_HBM, WHOLE],
        out_specs=[WHOLE] * (len(blocks) + 1),
        scratch_shapes=[pltpu.SemaphoreType.DMA((len(blocks),))],
        compiler_params=pltpu.CompilerParams(vmem_limit_bytes=limit * MIB),
        cost_estimate=pl.CostEstimate(
            flops=0, bytes_accessed=4 * units * cols * len(blocks), transcendentals=0
        ),
    )(*weights, after)
    return loaded, token


def expert_kernel(C, E, per_block, width, columns, held, *refs):
    groups = C // 2
    packed, refs = refs[: 2 * groups], refs[2 * groups :]
    gate_held, up_held, refs = refs[:held], refs[held : 2 * held], refs[2 * held :]
    gain, gate, up, down = refs[:4]
    outs, hidden, refs = refs[4 : 2 * groups + 4], refs[2 * groups + 4], refs[2 * groups + 5 :]
    gate_sum, up_sum, activated, piece, block, shift, spread, scale = refs[:8]
    gate_slots, up_slots, down_slots, up_sems, down_sems = refs[8:]
    ctx, exp = lax.axis_index("ctx"), lax.axis_index("exp")
    chips = E // 2
    token_rows = packed[0].shape[2]
    cols = packed[0].shape[3] - EXTRA
    half_rows = chips * C * token_rows
    features = hidden.shape[1]
    up_steps = C * per_block
    first = held * per_block
    down_steps = features // columns
    ahead, down_ahead = gate_slots.shape[0], down_slots.shape[0]

    def up_copies(i, slot):
        at = pl.ds(pl.multiple_of(i * width, 128), width)
        return [
            pltpu.make_async_copy(gate.at[0, :, at], gate_slots.at[slot], up_sems.at[0, slot]),
            pltpu.make_async_copy(up.at[0, :, at], up_slots.at[slot], up_sems.at[1, slot]),
        ]

    def down_copy(i, slot):
        at = pl.ds(pl.multiple_of(i * columns, 128), columns)
        return pltpu.make_async_copy(down.at[0, :, at], down_slots.at[slot], down_sems.at[slot])

    for i in range(ahead):
        for copy in up_copies(first + i, i):
            copy.start()

    def read(g, s, at):
        parts = [
            packed[side * groups + g][pl.ds(s * chips, chips), :, :, at] for side in range(2)
        ]
        parts = [part.astype(F32).reshape(half_rows, part.shape[-1]) for part in parts]
        return jnp.concatenate(parts, axis=0)

    tails = [read(k % groups, k // groups, slice(cols, cols + EXTRA)) for k in range(C)]
    lane = lax.broadcasted_iota(jnp.int32, tails[0].shape, 1)

    def pick(tail, wanted):
        return jnp.sum(jnp.where(wanted, tail, 0.0), axis=1, keepdims=True)

    means = [pick(tail, lane < SPLIT) for tail in tails]
    squares = [pick(tail, (lane >= SPLIT) & (lane < 2 * SPLIT)) for tail in tails]
    mean = sum(means) * (1.0 / C)
    deviation = sum(squares) + cols * sum((m - mean) * (m - mean) for m in means)
    spread[...] = lax.rsqrt(deviation * (1.0 / features) + 1e-05)
    for k in range(C):
        shift[k, 0] = means[k]
        shift[k, 1] = means[k] - mean
    term = lane - FIRST
    wanted = (term >= 0) & ((term & (E - 1)) == exp) & (term < SPLIT * E)
    scale[...] = sum(pick(tail, wanted) for tail in tails)

    def normalise(j, part):
        k = j ^ ctx
        at = pl.ds(pl.multiple_of(part * width, 128), width)
        place = pl.multiple_of(j * cols + part * width, 128)
        for g in range(groups):

            @pl.when(k % groups == g)
            def _():
                s = k // groups
                value = (read(g, s, at) + shift[k, 1]) * spread[...]
                block[...] = (value * gain[:, pl.ds(place, width)]).astype(BF16)
                own = packed[g][s * chips, ctx, :, at].astype(F32)
                rows = pl.ds(pl.multiple_of(ctx * token_rows, token_rows), token_rows)
                hidden[:, pl.ds(place, width)] = own + shift[k, 0, rows]

    turned_dot = functools.partial(
        lax.dot_general,
        dimension_numbers=(((1,), (1,)), ((), ())),
        preferred_element_type=F32,
    )
    if held == 0:
        gate_sum[...] = jnp.zeros_like(gate_sum)
        up_sum[...] = jnp.zeros_like(up_sum)
        for i in range(down_ahead):
            down_copy(i, i).start()
    for i in range(first):
        j, part = i // per_block, i % per_block
        normalise(j, part)
        at = slice(part * width, (part + 1) * width)
        gate_part = turned_dot(block[...], gate_held[j][:, at])
        gate_sum[...] = gate_part if i == 0 else gate_sum[...] + gate_part
        up_part = turned_dot(block[...], up_held[j][:, at])
        up_sum[...] = up_part if i == 0 else up_sum[...] + up_part
        if i == first // 2:
            for d in range(down_ahead):
                down_copy(d, d).start()

    @pl.loop(first, up_steps)
    def _(i):
        slot = (i - first) % ahead
        normalise(i // per_block, i % per_block)
        for copy in up_copies(i, slot):
            copy.wait()
        gate_sum[...] += turned_dot(block[...], gate_slots[slot])
        up_sum[...] += turned_dot(block[...], up_slots[slot])

        @pl.when(i + ahead < up_steps)
        def _():
            for copy in up_copies(i + ahead, slot):
                copy.start()

    value = gate_sum[...]
    value = value / (1.0 + jnp.exp(-value)) * up_sum[...]
    activated[...] = value.astype(BF16)

    @pl.loop(0, down_steps)
    def _(i):
        slot = i % down_ahead
        down_copy(i, slot).wait()
        value = jnp.dot(activated[...], down_slots[slot], preferred_element_type=F32)
        piece[...] = value * scale[...]

        @pl.when(i + down_ahead < down_steps)
        def _():
            down_copy(i + down_ahead, slot).start()

        place = pl.ds(pl.multiple_of(i * columns, 128), columns)
        for g in range(groups):
            for side in range(2):
                for s in range(2):
                    for p in range(chips):
                        k = s * groups + g
                        row = ((side * chips + p) * C + (ctx ^ k)) * token_rows
                        at = pl.ds(pl.multiple_of(row, token_rows), token_rows)
                        out = outs[side * groups + g]
                        out[s * chips + p, :, place] = piece[at, :].astype(BF16)


def largest_part(size, most, unit):
    return max(c for c in range(unit, most + 1, unit) if size % c == 0)


def run_experts(packed, gate_held, up_held, gain, weights, down_weight, C, E):
    count = len(packed)
    pieces, _, token_rows, wide = packed[0].shape
    cols = wide - EXTRA
    features = cols * C
    units = weights[0].shape[1]
    total = C * E * token_rows
    held = len(gate_held)
    width = largest_part(cols, 768 if held else 384, 128)
    columns = largest_part(features, 512 if held else 384, 128)
    per_block = cols // width
    ahead = 3 if held else 2
    down_ahead = 4 if held else 2
    operands = [*packed, *gate_held, *up_held, gain]
    *outs, hidden = pl.pallas_call(
        functools.partial(expert_kernel, C, E, per_block, width, columns, held),
        out_shape=[shape((pieces, token_rows, features), BF16) for _ in packed]
        + [shape((token_rows, features), F32)],
        in_specs=[WHOLE] * len(operands) + [IN_HBM] * 3,
        out_specs=[WHOLE] * (count + 1),
        scratch_shapes=[
            pltpu.VMEM((total, units), F32),
            pltpu.VMEM((total, units), F32),
            pltpu.VMEM((total, units), BF16),
            pltpu.VMEM((total, columns), F32),
            pltpu.VMEM((total, width), BF16),
            pltpu.VMEM((C, 2, total, 1), F32),
            pltpu.VMEM((total, 1), F32),
            pltpu.VMEM((total, 1), F32),
            pltpu.VMEM((ahead, units, width), BF16),
            pltpu.VMEM((ahead, units, width), BF16),
            pltpu.VMEM((down_ahead, units, columns), BF16),
            pltpu.SemaphoreType.DMA((2, ahead)),
            pltpu.SemaphoreType.DMA((down_ahead,)),
        ],
        compiler_params=pltpu.CompilerParams(vmem_limit_bytes=(35 if held else 58) * MIB),
        cost_estimate=pl.CostEstimate(
            flops=6 * total * features * units,
            bytes_accessed=6 * features * units + 4 * total * features,
            transcendentals=total * units,
        ),
    )(*operands, *weights, down_weight)
    return outs, hidden


def fold_kernel(plan, *refs):
    ins, outs = refs[: -len(plan)], refs[-len(plan) :]
    for out, places in zip(outs, plan):
        for i, parts in enumerate(places):
            out[i] = sum(ins[at][place].astype(F32) for at, place in parts).astype(BF16)


def fold(plan, operands):
    tail = operands[0].shape[1:]
    return call(
        functools.partial(fold_kernel, plan),
        [shape((len(places), *tail), BF16) for places in plan],
        operands,
        [WHOLE] * len(operands),
    )


def sum_over_plane(own, received, orders, added, apart):
    chips = own.shape[0] // 2
    operands = [own, received]
    holds = [
        {p: [(0, s * chips + p), (1, s * chips + p)] for p in range(chips)}
        for s in range(len(orders))
    ]
    for step in range(len(orders[0])):
        far = [1 << (order[step] - 1) for order in orders]
        sent = [[p for p in sorted(hold) if p & f] for hold, f in zip(holds, far)]
        kept = [[p for p in sorted(hold) if not p & f] for hold, f in zip(holds, far)]
        plan = [[hold[p] for p in ps] for hold, ps in zip(holds * 2, sent + kept)]
        *sends, keep0, keep1 = fold(plan, operands)
        got = [swap(value, "exp", 1 << order[step]) for value, order in zip(sends, orders)]
        operands = [keep0, got[0], keep1, got[1]]
        holds = [
            {p: [(2 * s, i), (2 * s + 1, i)] for i, p in enumerate(kept[s])}
            for s in range(len(orders))
        ]
    parts = [hold[0] + [(4 + i, s) for i in range(len(added))] for s, hold in enumerate(holds)]
    return fold([[part] for part in parts] if apart else [parts], operands + added)


def on_device(
    queries,
    keys_values,
    residual,
    out_weight,
    norm_gain,
    routes,
    route_weight,
    gate_weight,
    up_weight,
    down_weight,
):
    C = lax.axis_size("ctx")
    E = lax.axis_size("exp")
    chips = E // 2
    chip_bits = list(range(1, E.bit_length() - 1))
    heads = queries.shape[1] // HD
    seq = queries.shape[0] * C
    token_rows, features = residual.shape
    cols = out_weight.shape[1]
    wide = queries.shape[1] + HD
    slots = E + -(-cols // wide)
    sent = call(
        functools.partial(message_kernel, C, E),
        [shape((slots, token_rows, wide), BF16)] * C,
        [queries, keys_values, residual],
        [IN_HBM] * 3,
        [
            pltpu.VMEM(queries.shape, BF16),
            pltpu.VMEM(keys_values.shape, BF16),
            pltpu.VMEM(residual.shape, BF16),
            pltpu.SemaphoreType.DMA((3,)),
        ],
        limit=60,
    )
    messages = [swap(piece, "ctx", k) if k else piece for k, piece in enumerate(sent)]
    weight, gain = call(
        keep_kernel,
        [shape(out_weight.shape, BF16), shape((1, features), F32)],
        [sent[0], out_weight, norm_gain.reshape(1, -1)],
        [WHOLE] * 3,
    )
    halves, own_residual = call(
        functools.partial(halves_kernel, C, E),
        [
            shape((C, E, token_rows, HD), BF16),
            shape((slots - E, token_rows, wide), BF16),
        ],
        [*messages, weight, gain],
        [WHOLE] * (C + 2),
    )

    experts = jnp.arange(E, dtype=jnp.int32)
    left = jnp.sum(jnp.where(routes[:, :, None] == experts, route_weight[:, :, None], 0.0), axis=1)
    terms = []
    for _ in range(SPLIT):
        term = lax.reduce_precision(left, 8, 7)
        terms.append(term.astype(BF16))
        left = left - term
    extra = jnp.pad(
        jnp.concatenate(terms, axis=1), ((0, 0), (FIRST, EXTRA - FIRST - SPLIT * E))
    )

    mate_part, own_part = call(
        functools.partial(attend_kernel, C, E, heads),
        [
            shape((chips, C, token_rows, cols), BF16),
            shape((chips, C, token_rows, cols), F32),
        ],
        [*messages, swap(halves, "exp", 1), weight],
        [WHOLE] * (C + 2),
        [pltpu.VMEM((seq, cols), F32)],
        limit=16 if seq <= 256 else 56,
    )

    kept, *sent = call(
        mate_sum_kernel,
        [shape((C, token_rows, cols), F32)] + [shape((C, token_rows, cols), BF16)] * (chips - 1),
        [own_part, swap(mate_part, "exp", 1)],
        [WHOLE, WHOLE],
    )
    received = [swap(piece, "exp", (p + 1) << 1) for p, piece in enumerate(sent)]
    (rows,) = call(
        functools.partial(plane_sum_kernel, C, E, chips - 1),
        [shape((C, token_rows, cols + EXTRA), BF16)],
        [kept, *received, own_residual, *messages[1:], extra],
        [WHOLE] * (chips + C + 1),
    )

    weights = [jnp.swapaxes(gate_weight, 1, 2), jnp.swapaxes(up_weight, 1, 2)]
    hold = C * E * token_rows <= 256 and C == 4 and len(chip_bits) == 2
    loaded = []

    def load(which, after):
        if not hold:
            return []
        blocks, token = load_blocks(weights, [(which, 0)], cols, after, 44)
        loaded.extend(blocks)
        return [token]

    orders = (chip_bits[::-1], chip_bits)
    near = [rows, swap(rows, "ctx", C // 2)]
    (pair,) = pack([[(0, None), (1, None)]], near, rows.shape)
    pairs = [pair]
    for bit in range(C.bit_length() - 2):
        pairs += [swap(value, "ctx", 1 << bit) for value in pairs]
    afters = [[]] * len(chip_bits)
    group, sends = spread_over_plane(near, [(0, None), (1, None)], orders, chips, afters)
    packed = [group]
    token = load(0, sends[0])
    for value in pairs[1:]:
        afters = [sends] + [token] * (len(chip_bits) - 1)
        last = (lambda sent: load(1, sent[0])) if hold else (lambda sent: [])
        group, sends = spread_over_plane(
            [value], [(0, 0), (0, 1)], orders, chips, afters, last
        )
        packed.append(group)
    packed += [swap(group, "exp", 1) for group in packed]

    outs, hidden = run_experts(
        packed, loaded[0::2], loaded[1::2], gain, weights, down_weight, C, E
    )

    count = C // 2
    added = [[] for _ in range(count)]
    for g in reversed(range(count)):
        received = swap(outs[count + g], "exp", 1)
        values = sum_over_plane(outs[g], received, orders[::-1], added[g], g == 0)
        if g:
            top = 1 << (g.bit_length() - 1)
            added[g ^ top].append(swap(values[0], "ctx", top))
    kept, sent = values
    total = hidden + kept[0].astype(F32) + swap(sent, "ctx", C // 2)[0].astype(F32)
    return total.astype(BF16)


def solution(mesh):
    in_specs = (
        P("ctx", "exp"),
        P(None, "ctx", "exp"),
        P(("ctx", "exp"), None),
        P("exp", "ctx"),
        P(),
        P(("ctx", "exp"), None),
        P(("ctx", "exp"), None),
        P("exp", None, "ctx"),
        P("exp", None, "ctx"),
        P("exp", "ctx", None),
    )
    out_specs = P(("ctx", "exp"), None)
    return jax.shard_map(
        on_device, mesh=mesh, in_specs=in_specs, out_specs=out_specs, check_vma=False
    )
```
